512 devices in a mesh: view: 4 (over x), dev: 128 (over z, y, core).
Axes of the slice: x: 4, y: 4, z: 16, core: 2. Of those that a mesh axis runs over, the one named last changes fastest.
Arguments:
- attributes: float32 [59, 65536], P(None, 'dev'), may hold values from -6 to 8, as said below
- camera: float32 [4, 6], P('view'), may hold values from -0.2 to 0.2
- list_owner: int32 [4, 512, 256, 1], P('view', 'dev'), may hold values from 0 to 127; in each aligned block of 1024 rows (0 to 1023, 1024 to 2047, ..., all dimensions but the last counted through in order) at most 16 rows name the same one
- list_local: int32 [4, 512, 256], P('view', 'dev'), may hold values from 0 to 511
- term_depth: int32 [4, 512, 256], P('view', 'dev'), may hold values from 1 to 256
- image_cot: float32 [4, 3, 512, 256], P('view', None, 'dev'), may hold values from -6 to 6
Outputs:
- image: float32 [4, 3, 512, 256], P('view', None, 'dev')
- attr_grad: float32 [59, 65536], P(None, 'dev')
The draws below stay inside these ranges and needn't reach their ends.
Inputs may be any that keep to these rules, and one draw needn't show every extreme that they name: `attributes`: the quaternion's real part lies in 0.5 to 1.5, the third position coordinate in 4 to 8. `list_owner`: among the slots of one device's tiles of one view no owner is named more than 16 times.
All inputs are finite; a program needn't handle non-finite values.
Results may differ from the reference program's by a relative error of at most 0.0003.
Values sent between devices are 32-bit elements; how exact they have to be, the bound alone decides.
No kernel may reach another device: no remote copies, remote signals or barrier semaphores. Data moves between devices by JAX's collectives and lax.ppermute only.
A program may use at most 64 MiB of HBM per device.

```python
import math
import jax
import jax.numpy as jnp
import numpy as np
from jax import lax

ATTR = 59
G_DEV = 512
TILE_DEV = 4
SLOTS = 256
TILE_COLS = 16
VIEWS = 4
G_TOTAL = 65536
NTILES = 512
CAP = 16
N_DEV = 128


def draw_attributes(key, part):
    key = jax.random.fold_in(key, 11)
    keys = jax.random.split(key, 7)
    count = G_TOTAL
    plane = jax.random.uniform(keys[0], (2, count), jnp.float32, -2.5, 2.5)
    depth = jax.random.uniform(keys[1], (1, count), jnp.float32, 4.0, 8.0)
    logscale = jax.random.uniform(keys[2], (3, count), jnp.float32, math.log(0.4), math.log(2.0))
    qreal = jax.random.uniform(keys[3], (1, count), jnp.float32, 0.5, 1.5)
    qimag = jnp.clip(0.5 * jax.random.normal(keys[4], (3, count), jnp.float32), -1.5, 1.5)
    logit = jax.random.uniform(keys[5], (1, count), jnp.float32, -5.0, -2.0)
    level = jnp.concatenate([jnp.ones((3, 1), jnp.float32), 0.3 * jnp.ones((45, 1), jnp.float32)], axis=0)
    harm = jnp.clip(0.4 * jax.random.normal(keys[6], (48, count), jnp.float32), -1.6, 1.6) * level
    return jnp.concatenate([plane, depth, logscale, qreal, qimag, logit, harm], axis=0)


def with_ends(entries, own_key, smallest, largest):
    dims = entries.shape
    spot = [jax.random.randint(jax.random.fold_in(own_key, axis), (), 0, dims[axis]) for axis in range(len(dims))]
    entries = entries.at[tuple(spot)].set(smallest)
    longest = dims.index(max(dims))
    spot[longest] = (spot[longest] + 1) % dims[longest]
    return entries.at[tuple(spot)].set(largest)


def level_of(rng, dims, shards, low, top_value):
    level = 1.0
    for dim, shards_of in shards:
        draws = jax.random.uniform(jax.random.fold_in(jax.random.fold_in(rng, 6), dim), (shards_of,), jnp.float32, low / len(shards), top_value / len(shards))
        level = level * jnp.repeat(jnp.exp(draws), dims[dim] // shards_of).reshape((-1,) + (1,) * (len(dims) - 1 - dim))
    return level


def assign_block(key, own, number, rows, count, top, reach, lean):
    order = jax.random.permutation(key, count)
    packed, ordinary = load_shares(count, rows * top, reach, lean, True), load_shares(count, rows * top, reach, lean, False)
    places = jnp.arange(count)

    def named(lengths, turn):
        used = int((lengths > 0).sum())
        fixed = max(1, used // 4)
        moved = fixed + (places - fixed + turn * (used - fixed)) % max(1, count - fixed)
        return jnp.zeros((count,), jnp.int32).at[order[jnp.where(places < fixed, places, moved)]].set(jnp.asarray(lengths, jnp.int32))

    lengths = jnp.where(number % 4 == 0, named(packed, number // 4), named(ordinary, number - number // 4 - 1))
    mixed = jax.random.permutation(jax.random.fold_in(own, 3), count)
    donor, sink = mixed[0:count // 2 * 2:2], mixed[1:count // 2 * 2:2]
    slack = jnp.minimum(lengths[donor] - 1, reach - lengths[sink]) // 2
    slack = jnp.where((donor == order[0]) | (sink == order[0]) | (lengths[sink] == 0), 0, jnp.maximum(slack, 0))
    moved = jax.random.randint(jax.random.fold_in(own, 4), (count // 2,), 0, 1 << 20) % (slack + 1)
    lengths = lengths.at[donor].add(-moved).at[sink].add(moved)
    labels = jnp.searchsorted(jnp.cumsum(lengths), jnp.arange(rows * top), side="right").astype(jnp.int32)
    table = labels.reshape(top, rows).T
    table = table[jax.random.permutation(jax.random.fold_in(own, 1), rows)]
    turn = jax.random.randint(jax.random.fold_in(own, 2), (rows, 1), 0, top)
    return jnp.take_along_axis(table, (jnp.arange(top)[None, :] + turn) % top, axis=1)


def load_shares(amount, total, most, slope, full):
    loads = [(1 << 20) // math.isqrt(standing ** slope) + 1 for standing in range(1, amount + 1)]
    largest = most if full else min(most, max(-(-total // amount), total * loads[0] // sum(loads)))
    least = 1 if total - largest >= amount - 1 else 0
    holding, rest = [largest] + [least] * (amount - 1), total - largest - least * (amount - 1)
    while rest > 0:
        candidates = [i for i in range(1, amount) if holding[i] < largest] or [i for i in range(1, amount) if holding[i] < most]
        pool, budget = sum([loads[i] for i in candidates]), rest
        for i in candidates:
            more = min(most - holding[i], max(1, budget * loads[i] // pool), rest)
            holding[i] = holding[i] + more
            rest = rest - more
    return np.array(holding)


def noise(own_key, shape, spread, reach, cuts=(), held_as=jnp.bfloat16):
    values = jax.random.normal(own_key, shape, jnp.float32) * spread
    if len(cuts) > 0:
        values = level_of(own_key, shape, cuts, -0.22, 0.18) * values
    return jnp.clip(values, min=-reach, max=reach).astype(held_as)


def setup_inputs(seed: int = 0) -> dict:
    key_of = jax.random.split(jax.random.key(seed), 7)
    attributes = draw_attributes(jax.random.fold_in(key_of[6], 71), 0)
    camera = jnp.clip(jax.random.uniform(key_of[1], (VIEWS, 6), jnp.float32, -0.2, 0.2) * level_of(key_of[1], (VIEWS, 6), ((0, 4),), -0.4, 0.0), -0.2, 0.2)
    list_owner_keys = jax.random.split(jax.random.fold_in(key_of[2], 1), VIEWS * NTILES * SLOTS // (TILE_DEV * SLOTS))
    list_owner_turns = jax.random.permutation(jax.random.fold_in(key_of[2], 3), VIEWS * NTILES * SLOTS // (TILE_DEV * SLOTS))
    list_owner = jax.vmap(lambda own, number: assign_block(jax.random.fold_in(key_of[2], 2), own, number, TILE_DEV * SLOTS, N_DEV, 1, CAP, 2))(list_owner_keys, list_owner_turns).reshape((VIEWS, NTILES, SLOTS, 1))
    list_local = with_ends(jax.random.randint(key_of[3], (VIEWS, NTILES, SLOTS), 0, G_DEV), jax.random.fold_in(key_of[3], 1), 0, G_DEV - 1).astype(jnp.int32)
    term_depth = with_ends(jax.random.randint(key_of[4], (VIEWS, NTILES, 256), 1, SLOTS + 1), jax.random.fold_in(key_of[4], 1), 1, SLOTS).astype(jnp.int32)
    image_cot = noise(key_of[5], (VIEWS, 3, NTILES, 256), 1.0, 6.0, ((0, 4), (2, 128)), jnp.float32)
    return dict(attributes=attributes, camera=camera, list_owner=list_owner, list_local=list_local, term_depth=term_depth, image_cot=image_cot)


SH_C0 = 0.28209479177387814
SH_C1 = 0.4886025119029199
SH_C2 = (1.0925484305920792, -1.0925484305920792, 0.31539156525252005, -1.0925484305920792, 0.5462742152960396)
SH_C3 = (-0.5900435899266435, 2.890611442640554, -0.4570457994644658, 0.3731763325901154, -0.4570457994644658, 1.445305721320277, -0.5900435899266435)
BLUR = 1e-05

def rotation(angles):
    one = jnp.ones((), jnp.float32)
    zero = jnp.zeros((), jnp.float32)
    cosx, sinx = (jnp.cos(angles[0]), jnp.sin(angles[0]))
    cosy, siny = (jnp.cos(angles[1]), jnp.sin(angles[1]))
    cosz, sinz = (jnp.cos(angles[2]), jnp.sin(angles[2]))
    rot_x = jnp.stack([jnp.stack([one, zero, zero]), jnp.stack([zero, cosx, -sinx]), jnp.stack([zero, sinx, cosx])])
    rot_y = jnp.stack([jnp.stack([cosy, zero, siny]), jnp.stack([zero, one, zero]), jnp.stack([-siny, zero, cosy])])
    rot_z = jnp.stack([jnp.stack([cosz, -sinz, zero]), jnp.stack([sinz, cosz, zero]), jnp.stack([zero, zero, one])])
    high = lax.Precision.HIGHEST
    return jnp.dot(rot_z, jnp.dot(rot_y, rot_x, precision=high), precision=high)

def harmonics(dirx, diry, dirz):
    xx, yy, zz = (dirx * dirx, diry * diry, dirz * dirz)
    return [SH_C0 + 0.0 * dirx, -SH_C1 * diry, SH_C1 * dirz, -SH_C1 * dirx, SH_C2[0] * dirx * diry, SH_C2[1] * diry * dirz, SH_C2[2] * (2.0 * zz - xx - yy), SH_C2[3] * dirx * dirz, SH_C2[4] * (xx - yy), SH_C3[0] * diry * (3.0 * xx - yy), SH_C3[1] * dirx * diry * dirz, SH_C3[2] * diry * (4.0 * zz - xx - yy), SH_C3[3] * dirz * (2.0 * zz - 3.0 * xx - 3.0 * yy), SH_C3[4] * dirx * (4.0 * zz - xx - yy), SH_C3[5] * dirz * (xx - yy), SH_C3[6] * dirx * (xx - 3.0 * yy)]

def project(attrs, cam):
    rot = rotation(cam[0:3])
    shift = cam[3:6]
    pos = attrs[0:3]
    campos = jnp.dot(rot, pos, precision=lax.Precision.HIGHEST) + shift[:, None]
    posx, posy, posz = (campos[0], campos[1], campos[2])
    inverse = 1.0 / posz
    jac = [[inverse, 0.0 * inverse, -posx * inverse * inverse], [0.0 * inverse, inverse, -posy * inverse * inverse]]
    tmat = [[sum((jac[r][i] * rot[i, j] for i in range(3))) for j in range(3)] for r in range(2)]
    scale = jnp.exp(attrs[3:6])
    quat = attrs[6:10]
    quat = quat * lax.rsqrt(lax.optimization_barrier(jnp.sum(quat * quat, axis=0)))
    qw, qa, qb, qc = (quat[0], quat[1], quat[2], quat[3])
    rgau = [[1 - 2 * (qb * qb + qc * qc), 2 * (qa * qb - qw * qc), 2 * (qa * qc + qw * qb)], [2 * (qa * qb + qw * qc), 1 - 2 * (qa * qa + qc * qc), 2 * (qb * qc - qw * qa)], [2 * (qa * qc - qw * qb), 2 * (qb * qc + qw * qa), 1 - 2 * (qa * qa + qb * qb)]]
    mscaled = [[rgau[i][k] * scale[k] for k in range(3)] for i in range(3)]
    cov = [[sum((mscaled[i][k] * mscaled[j][k] for k in range(3))) for j in range(3)] for i in range(3)]
    sig = [[sum((tmat[r][i] * cov[i][j] * tmat[s][j] for i in range(3) for j in range(3))) for s in range(2)] for r in range(2)]
    sig_a = sig[0][0] + BLUR
    sig_b = sig[0][1]
    sig_c = sig[1][1] + BLUR
    det = sig_a * sig_c - sig_b * sig_b
    centre = [-(rot[0, j] * shift[0] + rot[1, j] * shift[1] + rot[2, j] * shift[2]) for j in range(3)]
    dirs = [pos[j] - centre[j] for j in range(3)]
    norm_inv = lax.rsqrt(dirs[0] * dirs[0] + dirs[1] * dirs[1] + dirs[2] * dirs[2])
    basis = harmonics(dirs[0] * norm_inv, dirs[1] * norm_inv, dirs[2] * norm_inv)
    colors = [0.5 + sum((basis[k] * attrs[11 + 3 * k + ch] for k in range(16))) for ch in range(3)]
    opacity = jax.nn.sigmoid(attrs[10])
    return jnp.stack([posx * inverse, posy * inverse, sig_c / det, -sig_b / det, sig_a / det, opacity] + colors)

def pixel_coords(tile, ntiles):
    pixel = jnp.arange(256, dtype=jnp.int32)
    col = tile % TILE_COLS
    row = tile // TILE_COLS
    xs = ((col * 16 + pixel % 16).astype(jnp.float32) + 0.5) / (16.0 * TILE_COLS) - 0.5
    ys = ((row * 16 + pixel // 16).astype(jnp.float32) + 0.5) / (16.0 * (ntiles // TILE_COLS)) - 0.5
    return (xs, ys)

def tile_color(rows, xs, ys, depth):
    slot_entries = rows.shape[1]
    delta_x = xs[:, None] - rows[0][None, :]
    delta_y = ys[:, None] - rows[1][None, :]
    power = 0.5 * (rows[2][None, :] * delta_x * delta_x + rows[4][None, :] * delta_y * delta_y) + rows[3][None, :] * delta_x * delta_y
    live = (jnp.arange(slot_entries, dtype=jnp.int32)[None, :] < depth[:, None]).astype(jnp.float32)
    alpha = rows[5][None, :] * jnp.exp(-power) * live
    keep = jnp.cumprod(1.0 - alpha, axis=1)
    trans = jnp.concatenate([jnp.ones((xs.shape[0], 1), jnp.float32), keep[:, :-1]], axis=1)
    weight = trans * alpha
    return jnp.einsum('ps,cs->cp', weight, rows[6:9], precision=lax.Precision.HIGHEST)

def tile_step(rows, tile, depth, cotangent, ntiles):
    xs, ys = pixel_coords(tile, ntiles)
    color, pull = jax.vjp(lambda r: tile_color(r, xs, ys, depth), rows)
    return (color, pull(cotangent)[0])

def reference(attributes, camera, list_owner, list_local, term_depth, image_cot):
    ntiles = TILE_DEV * N_DEV
    total = jnp.zeros((ATTR, G_TOTAL), jnp.float32)
    images = []
    for view in range(VIEWS):
        cam = camera[view]
        rows_all, pull = jax.vjp(lambda a: project(a, cam), attributes)
        ids = (list_owner[view, :, :, 0] * G_DEV + list_local[view]).astype(jnp.int32)
        cot_view = image_cot[view]
        depth_view = term_depth[view]

        def tile_work(tile):
            rows = rows_all[:, ids[tile]]
            return tile_step(rows, tile, depth_view[tile], cot_view[:, tile], ntiles)
        color, grads = lax.map(tile_work, jnp.arange(ntiles, dtype=jnp.int32))
        images.append(jnp.transpose(color, (1, 0, 2)))
        grads = jnp.transpose(grads, (1, 0, 2)).reshape(9, -1)
        row_grad = jnp.zeros((9, G_TOTAL), jnp.float32).at[:, ids.reshape(-1)].add(grads)
        total = total + pull(row_grad)[0]
    return (jnp.stack(images), total)
```

```python
import jax
import jax.numpy as jnp
from jax import lax
from jax.experimental import pallas as pl
from jax.experimental.pallas import tpu as pltpu
from jax.sharding import PartitionSpec as P

TILE_COLS = 16
TILES = 4
SLOTS = 256
CAP = 16
OWNERS = 128
G_DEV = 512
ATTR = 59
VIEWS = 4
LOG2E = 1.4426950408889634

SH_C0 = 0.28209479177387814
SH_C1 = 0.4886025119029199
SH_C2 = (
    1.0925484305920792,
    -1.0925484305920792,
    0.31539156525252005,
    -1.0925484305920792,
    0.5462742152960396,
)
SH_C3 = (
    -0.5900435899266435,
    2.890611442640554,
    -0.4570457994644658,
    0.3731763325901154,
    -0.4570457994644658,
    1.445305721320277,
    -0.5900435899266435,
)
BLUR = 1e-05

F32 = jnp.float32
BF16 = jnp.bfloat16
I32 = jnp.int32


def camera_terms(angles, shift):
    cosx, sinx = jnp.cos(angles[0]), jnp.sin(angles[0])
    cosy, siny = jnp.cos(angles[1]), jnp.sin(angles[1])
    cosz, sinz = jnp.cos(angles[2]), jnp.sin(angles[2])
    yx = [
        [cosy, siny * sinx, siny * cosx],
        [None, cosx, -sinx],
        [-siny, cosy * sinx, cosy * cosx],
    ]
    rot = [
        [cosz * yx[0][0]] + [cosz * yx[0][j] - sinz * yx[1][j] for j in (1, 2)],
        [sinz * yx[0][0]] + [sinz * yx[0][j] + cosz * yx[1][j] for j in (1, 2)],
        yx[2],
    ]
    centre = [-(rot[0][j] * shift[0] + rot[1][j] * shift[1] + rot[2][j] * shift[2]) for j in range(3)]
    return rot, shift, centre


def harmonics(dirx, diry, dirz):
    xx, yy, zz = (dirx * dirx, diry * diry, dirz * dirz)
    return [
        -SH_C1 * diry,
        SH_C1 * dirz,
        -SH_C1 * dirx,
        SH_C2[0] * dirx * diry,
        SH_C2[1] * diry * dirz,
        SH_C2[2] * (2.0 * zz - xx - yy),
        SH_C2[3] * dirx * dirz,
        SH_C2[4] * (xx - yy),
        SH_C3[0] * diry * (3.0 * xx - yy),
        SH_C3[1] * dirx * diry * dirz,
        SH_C3[2] * diry * (4.0 * zz - xx - yy),
        SH_C3[3] * dirz * (2.0 * zz - 3.0 * xx - 3.0 * yy),
        SH_C3[4] * dirx * (4.0 * zz - xx - yy),
        SH_C3[5] * dirz * (xx - yy),
        SH_C3[6] * dirx * (xx - 3.0 * yy),
    ]


def project(pos, logscale, quat, sh, cam):
    rot, shift, centre = cam
    cpos = [rot[i][0] * pos[0] + rot[i][1] * pos[1] + rot[i][2] * pos[2] + shift[i] for i in range(3)]
    inverse = 1.0 / cpos[2]
    u, w = cpos[0] * inverse, cpos[1] * inverse
    tmat = [
        [inverse * (rot[0][j] - u * rot[2][j]) for j in range(3)],
        [inverse * (rot[1][j] - w * rot[2][j]) for j in range(3)],
    ]
    scale = [jnp.exp(s) for s in logscale]
    norm = lax.rsqrt(quat[0] * quat[0] + quat[1] * quat[1] + quat[2] * quat[2] + quat[3] * quat[3])
    qw, qa, qb, qc = [q * norm for q in quat]
    rgau = [
        [1 - 2 * (qb * qb + qc * qc), 2 * (qa * qb - qw * qc), 2 * (qa * qc + qw * qb)],
        [2 * (qa * qb + qw * qc), 1 - 2 * (qa * qa + qc * qc), 2 * (qb * qc - qw * qa)],
        [2 * (qa * qc - qw * qb), 2 * (qb * qc + qw * qa), 1 - 2 * (qa * qa + qb * qb)],
    ]
    trs = [
        [(tmat[r][0] * rgau[0][k] + tmat[r][1] * rgau[1][k] + tmat[r][2] * rgau[2][k]) * scale[k] for k in range(3)]
        for r in range(2)
    ]
    sig_a = trs[0][0] * trs[0][0] + trs[0][1] * trs[0][1] + trs[0][2] * trs[0][2] + BLUR
    sig_b = trs[0][0] * trs[1][0] + trs[0][1] * trs[1][1] + trs[0][2] * trs[1][2]
    sig_c = trs[1][0] * trs[1][0] + trs[1][1] * trs[1][1] + trs[1][2] * trs[1][2] + BLUR
    det_inv = 1.0 / (sig_a * sig_c - sig_b * sig_b)
    dirs = [pos[j] - centre[j] for j in range(3)]
    norm_inv = lax.rsqrt(dirs[0] * dirs[0] + dirs[1] * dirs[1] + dirs[2] * dirs[2])
    basis = harmonics(dirs[0] * norm_inv, dirs[1] * norm_inv, dirs[2] * norm_inv)
    colors = []
    for ch in range(3):
        color = 0.5 + SH_C0 * sh[ch]
        for k in range(1, 16):
            color = color + basis[k - 1] * sh[3 * k + ch]
        colors.append(color)
    return [u, w, sig_c * det_inv, -sig_b * det_inv, sig_a * det_inv] + colors


def spread_attributes(attr_ref, wide_ref):
    for j in range(4):
        part = attr_ref[:, 128 * j : 128 * (j + 1)]
        wide_ref[pl.ds(j, ATTR, stride=8), :] = part
        wide_ref[pl.ds(j + 4, ATTR, stride=8), :] = part


def split_attributes(wide_ref):
    attrs = [wide_ref[8 * a : 8 * (a + 1), :] for a in range(ATTR)]
    return attrs[0:3], attrs[3:6], attrs[6:10], attrs[10], attrs[11:]


def dot(a, b, ca, cb):
    return lax.dot_general(a, b, (((ca,), (cb,)), ((), ())), preferred_element_type=F32)


def lane_gather(x, idx):
    return jnp.take_along_axis(x, idx, axis=1, mode="promise_in_bounds")


def split2(x):
    hi = x.astype(BF16)
    return hi, (x - hi.astype(F32)).astype(BF16)


def split3(x):
    hi = x.astype(BF16)
    rest = x - hi.astype(F32)
    mid = rest.astype(BF16)
    return hi, mid, (rest - mid.astype(F32)).astype(BF16)


def route_kernel(owner_ref, local_ref, attr_ref, cam_ref, asked_ref, rank_ref, inv_ref, rows_ref, wide_ref, tmp_ref):
    before = (
        lax.broadcasted_iota(I32, (SLOTS, SLOTS), 0) < lax.broadcasted_iota(I32, (SLOTS, SLOTS), 1)
    ).astype(F32).astype(BF16)
    every = jnp.ones((SLOTS, SLOTS), BF16)
    oid = lax.broadcasted_iota(I32, (OWNERS, SLOTS), 0)
    kid = lax.broadcasted_iota(I32, (CAP, SLOTS), 0)
    lane = lax.broadcasted_iota(I32, (1, SLOTS), 1)
    base = jnp.zeros((OWNERS, SLOTS), F32)
    table = jnp.zeros((4 * CAP, OWNERS), F32)
    for t in range(TILES):
        owner = owner_ref[:, SLOTS * t : SLOTS * (t + 1)]
        hot = (oid == owner).astype(F32)
        hot16 = hot.astype(BF16)
        count = dot(hot16, before, 1, 0) + base
        base = base + dot(hot16, every, 1, 0)
        rank = jnp.sum(hot * count, axis=0, keepdims=True).astype(I32)
        rank_ref[:, SLOTS * t : SLOTS * (t + 1)] = rank
        place = (kid == rank).astype(F32)
        local = local_ref[t : t + 1, :]
        slot = lane + (SLOTS * t + 1)
        parts = [local & 255, local >> 8, slot & 255, slot >> 8]
        vals = jnp.concatenate([place * p.astype(F32) for p in parts], axis=0).astype(BF16)
        table = table + dot(vals, hot16, 1, 1)
    asked = table[0:CAP] + 256.0 * table[CAP : 2 * CAP]
    inv_ref[...] = (table[2 * CAP : 3 * CAP] + 256.0 * table[3 * CAP :]).astype(I32)
    asked = jnp.concatenate([asked, jnp.zeros((128 - CAP, OWNERS), F32)], axis=0)
    asked_ref[...] = jnp.transpose(asked)
    spread_attributes(attr_ref, wide_ref)
    pos, logscale, quat, logit, sh = split_attributes(wide_ref)
    cam = [jnp.broadcast_to(cam_ref[:, j : j + 1], (8, 128)) for j in range(6)]
    rows = project(pos, logscale, quat, sh, camera_terms(cam[:3], cam[3:]))
    log_opacity = -LOG2E * jnp.log(1.0 + jnp.exp(-logit))
    for c, row in enumerate(rows[:5] + [log_opacity] + rows[5:]):
        tmp_ref[8 * c : 8 * (c + 1), :] = row
    for j in range(4):
        rows_ref[:, 128 * j : 128 * (j + 1)] = tmp_ref[pl.ds(j, 16, stride=8), :]


def serve_kernel(asked_ref, rows_ref, out_ref, ids_ref):
    ids = jnp.transpose(asked_ref[...])[0:CAP].astype(I32)
    ids_ref[...] = ids
    rows = [rows_ref[0:8, 128 * j : 128 * (j + 1)] for j in range(4)]
    last = [jnp.broadcast_to(rows_ref[8:9, 128 * j : 128 * (j + 1)], (8, 128)) for j in range(4)]

    def pick(tables, idx):
        low, high = idx & 127, idx >> 7
        got = lane_gather(tables[0], low)
        for j in range(1, 4):
            got = jnp.where(high == j, lane_gather(tables[j], low), got)
        return got

    main = [pick(rows, jnp.broadcast_to(ids[k : k + 1], (8, 128))) for k in range(CAP)]
    out_ref[pl.ds(0, OWNERS, stride=2), :] = jnp.transpose(jnp.concatenate(main, axis=0))
    more = [pick(last, ids[0:8]), pick(last, ids[8:16]), jnp.zeros((128 - CAP, 128), F32)]
    out_ref[pl.ds(1, OWNERS, stride=2), :] = jnp.transpose(jnp.concatenate(more, axis=0))


def composite_kernel(
    tile_ref, got_ref, owner_ref, rank_ref, inv_ref, depth_ref, cot_ref, image_ref, out_ref,
    par_ref, alpha_ref, pull_ref, weight_ref, grad_ref, stack_ref,
):
    table = jnp.transpose(got_ref[pl.ds(0, OWNERS, stride=2), :])
    table_last = jnp.transpose(got_ref[pl.ds(1, OWNERS, stride=2), :])[0:CAP]
    sub = lax.broadcasted_iota(I32, (8, 128), 0)
    for b in range(8):
        owner = jnp.broadcast_to(owner_ref[:, 128 * b : 128 * (b + 1)], (8, 128))
        rank = jnp.broadcast_to(rank_ref[:, 128 * b : 128 * (b + 1)], (8, 128))
        got = lane_gather(table[0:8], owner)
        for k in range(1, CAP):
            got = jnp.where(rank == k, lane_gather(table[8 * k : 8 * (k + 1)], owner), got)
        par_ref[0:8, 128 * b : 128 * (b + 1)] = got
        low = jnp.where(rank == sub, lane_gather(table_last[0:8], owner), 0.0)
        high = jnp.where(rank == sub + 8, lane_gather(table_last[8:16], owner), 0.0)
        par_ref[8:9, 128 * b : 128 * (b + 1)] = jnp.sum(low + high, axis=0, keepdims=True)

    q = lax.broadcasted_iota(I32, (16, 128), 1)
    row16 = lax.broadcasted_iota(I32, (16, 128), 0)
    X = (q & 15).astype(F32) - 7.5
    Y = (q >> 4).astype(F32) - 3.5
    mono = jnp.where(row16 == 0, 1.0, 0.0)
    for n, m in enumerate([X, Y, X * X, X * Y, Y * Y]):
        mono = jnp.where(row16 == n + 1, m, mono)
    mono8 = mono[0:8]
    mono16 = mono.astype(BF16)
    mono_twice = jnp.concatenate([mono16, mono16], axis=1)
    ex, ey = 1.0 / (16.0 * TILE_COLS), 1.0 / (16.0 * (TILES * OWNERS // TILE_COLS))

    zero = jnp.zeros((1, SLOTS), F32)
    zero5 = jnp.zeros((5, SLOTS), F32)
    blank = jnp.zeros((8, 128), F32)
    cots = []
    geometry = []
    for t in range(TILES):
        par = [par_ref[c : c + 1, SLOTS * t : SLOTS * (t + 1)] for c in range(9)]
        u, w, ca, cb, cc, log_op = par[:6]
        tile = tile_ref[0] + t
        cx = ((tile % TILE_COLS) * 16 + 8).astype(F32) * ex - 0.5
        dx0 = cx - u
        A, B, C = -0.5 * LOG2E * ca, -LOG2E * cb, -0.5 * LOG2E * cc
        colors = jnp.concatenate([par[6], par[7], par[8], zero5], axis=0)
        chi, cmid, clo = [c.astype(F32) for c in split3(colors)]
        dy0s = []
        for h in range(2):
            th = 4 * h + t
            cy = ((tile // TILE_COLS) * 16 + 8 * h + 4).astype(F32) * ey - 0.5
            dy0 = cy - w
            dy0s.append(dy0)
            coef = jnp.concatenate(
                [
                    (A * dx0 + B * dy0) * dx0 + C * dy0 * dy0 + log_op,
                    (2.0 * A * dx0 + B * dy0) * ex,
                    (B * dx0 + 2.0 * C * dy0) * ey,
                    A * (ex * ex),
                    B * (ex * ey),
                    C * (ey * ey),
                    zero,
                    zero,
                ],
                axis=0,
            )
            khi, kmid, klo = [k.astype(F32) for k in split3(coef)]
            left = jnp.concatenate([khi, kmid, klo, chi, chi, chi, cmid, cmid, clo], axis=0)
            left = jnp.concatenate([left, jnp.zeros((128 - 72, SLOTS), F32)], axis=0)
            g = jnp.concatenate([cot_ref[c, t : t + 1, 128 * h : 128 * (h + 1)] for c in range(3)] + [blank[0:5]], axis=0)
            ghi, gmid, glo = [x.astype(F32) for x in split3(g)]
            cots.append((th, ghi, gmid))
            right = jnp.concatenate(
                [
                    jnp.concatenate([mono8, mono8, mono8, blank, blank, blank, blank, blank, blank], axis=0),
                    jnp.concatenate([blank, blank, blank, ghi, gmid, glo, ghi, gmid, ghi], axis=0),
                ],
                axis=1,
            )
            right = jnp.concatenate([right, jnp.zeros((128 - 72, 256), F32)], axis=0)
            both = dot(jnp.transpose(left).astype(BF16), right.astype(BF16), 1, 0)
            alpha_ref[pl.ds(th, SLOTS, stride=8), :] = both[:, :128]
            pull_ref[pl.ds(th, SLOTS, stride=8), :] = both[:, 128:]
        geometry.append((ca, cb, cc, dx0, dy0s, chi, cmid))

    depth = jnp.concatenate([depth_ref[:, 0:128], depth_ref[:, 128:256]], axis=0)
    unroll = 8

    def forward(j, trans):
        for i in range(unroll):
            s = j * unroll + i
            at = pl.ds(pl.multiple_of(s * 8, 8), 8)
            alpha = jnp.where(s < depth, jnp.exp2(alpha_ref[at, :]), 0.0)
            weight = trans * alpha
            alpha_ref[at, :] = alpha
            weight_ref[at, :] = weight
            trans = trans - weight
        return trans

    lax.fori_loop(0, SLOTS // unroll, forward, jnp.ones((8, 128), F32))

    def backward(j, rest):
        for i in range(unroll):
            s = SLOTS - 1 - (j * unroll + i)
            at = pl.ds(pl.multiple_of(s * 8, 8), 8)
            more = pull_ref[at, :] - rest
            rest = rest + alpha_ref[at, :] * more
            pull_ref[at, :] = weight_ref[at, :] * more
        return rest

    lax.fori_loop(0, SLOTS // unroll, backward, jnp.zeros((8, 128), F32))

    cots = {th: (ghi, gmid) for th, ghi, gmid in cots}
    for t in range(TILES):
        ca, cb, cc, dx0, dy0s, chi, cmid = geometry[t]
        color_rows = jnp.concatenate([chi, cmid], axis=0).astype(BF16)
        total = [jnp.zeros((1, SLOTS), F32) for _ in range(6)]
        dcolor = jnp.zeros((3, SLOTS), F32)
        for h in range(2):
            th = 4 * h + t
            dy0 = dy0s[h]
            whi, wlo = split2(weight_ref[pl.ds(th, SLOTS, stride=8), :])
            weights = jnp.concatenate([whi, wlo], axis=1)
            ghi, glo = split2(pull_ref[pl.ds(th, SLOTS, stride=8), :])
            grads = jnp.concatenate([ghi, glo], axis=1)
            seen = dot(color_rows, weights, 1, 0)
            seen = seen[:, :128] + seen[:, 128:]
            seen = seen[0:8] + seen[8:16]
            for c in range(3):
                image_ref[c, t : t + 1, 128 * h : 128 * (h + 1)] = seen[c : c + 1]
            cot = jnp.concatenate(cots[th], axis=0).astype(BF16)
            dcol = dot(jnp.concatenate([cot, cot], axis=1), weights, 1, 1)
            dcolor = dcolor + dcol[0:3] + dcol[8:11]
            mom = dot(mono_twice, grads, 1, 1)
            m0 = mom[0:1]
            mx, my = ex * mom[1:2], ey * mom[2:3]
            total[0] = total[0] + m0
            total[1] = total[1] + dx0 * m0 + mx
            total[2] = total[2] + dy0 * m0 + my
            total[3] = total[3] + dx0 * (dx0 * m0 + 2.0 * mx) + (ex * ex) * mom[3:4]
            total[4] = total[4] + dx0 * (dy0 * m0 + my) + dy0 * mx + (ex * ey) * mom[4:5]
            total[5] = total[5] + dy0 * (dy0 * m0 + 2.0 * my) + (ey * ey) * mom[5:6]
        s0, sx, sy, sxx, sxy, syy = total
        made = [ca * sx + cb * sy, cb * sx + cc * sy, -0.5 * sxx, -sxy, -0.5 * syy, s0, dcolor]
        grad_ref[0:9, SLOTS * t : SLOTS * (t + 1)] = jnp.concatenate(made, axis=0)

    inv = inv_ref[...]

    def pick(tables, idx):
        at = jnp.maximum(idx - 1, 0)
        low, high = at & 127, at >> 7
        got = lane_gather(tables[0], low)
        for j in range(1, 8):
            got = jnp.where(high == j, lane_gather(tables[j], low), got)
        return jnp.where(idx > 0, got, 0.0)

    tables = [grad_ref[0:8, 128 * j : 128 * (j + 1)] for j in range(8)]
    last = [jnp.broadcast_to(grad_ref[8:9, 128 * j : 128 * (j + 1)], (8, 128)) for j in range(8)]
    main = [pick(tables, jnp.broadcast_to(inv[k : k + 1], (8, 128))) for k in range(CAP)]
    out_ref[pl.ds(0, OWNERS, stride=2), :] = jnp.transpose(jnp.concatenate(main, axis=0))
    more = [pick(last, inv[0:8]), pick(last, inv[8:16]), jnp.zeros((128 - CAP, 128), F32)]
    out_ref[pl.ds(1, OWNERS, stride=2), :] = jnp.transpose(jnp.concatenate(more, axis=0))


def collect_kernel(back_ref, ids_ref, cam_ref, out_ref):
    table = jnp.transpose(back_ref[pl.ds(0, OWNERS, stride=2), :])
    table_last = jnp.transpose(back_ref[pl.ds(1, OWNERS, stride=2), :])[0:CAP]
    lid = lax.broadcasted_iota(I32, (G_DEV, 128), 0)
    acc = jnp.zeros((48, G_DEV), F32)
    pad = jnp.zeros((7, 128), F32)
    for k in range(0, CAP, 2):
        lefts, hots = [], []
        for kk in (k, k + 1):
            both = jnp.concatenate([table[8 * kk : 8 * (kk + 1)], table_last[kk : kk + 1], pad], axis=0)
            lefts.append(jnp.concatenate(split3(both), axis=0))
            hots.append((lid == ids_ref[kk : kk + 1, :]).astype(F32).astype(BF16))
        acc = acc + dot(jnp.concatenate(lefts, axis=1), jnp.concatenate(hots, axis=1), 1, 1)
    rows = acc[0:16] + acc[16:32] + acc[32:48]
    blank = jnp.zeros((8, 128), F32)
    for v in range(VIEWS):
        for j in range(4):
            out_ref[pl.ds(40 * v + j, 9, stride=4), :] = rows[0:9, 128 * j : 128 * (j + 1)]
        out_ref[40 * v + 36 : 40 * v + 40, :] = blank[0:4]
        out_ref[40 * v + 36 : 40 * v + 37, 0:6] = cam_ref[...]


def pull_kernel(all_ref, attr_ref, out_ref, wide_ref, res_ref):
    spread_attributes(attr_ref, wide_ref)
    pos, logscale, quat, logit, sh = split_attributes(wide_ref)
    total = None
    opacity_grad = None
    for pair in range(VIEWS // 2):
        starts = (80 * pair, 80 * pair + 40)
        cot = [
            jnp.concatenate([all_ref[s + 4 * c : s + 4 * c + 4, :] for s in starts], axis=0) for c in range(9)
        ]
        cam = [
            jnp.concatenate(
                [jnp.broadcast_to(all_ref[s + 36 : s + 37, j : j + 1], (4, 128)) for s in starts], axis=0
            )
            for j in range(6)
        ]
        terms = camera_terms(cam[:3], cam[3:])
        _, pull = jax.vjp(lambda a, b, c, d: project(a, b, c, d, terms), pos, logscale, quat, sh)
        grads = jax.tree.leaves(pull(cot[:5] + cot[6:]))
        total = grads if total is None else [a + b for a, b in zip(total, grads)]
        opacity_grad = cot[5] if opacity_grad is None else opacity_grad + cot[5]
    grads = total[:10] + [opacity_grad / (1.0 + jnp.exp(logit))] + total[10:]
    for a in range(ATTR):
        res_ref[4 * a : 4 * a + 4, :] = grads[a][0:4] + grads[a][4:8]
    for j in range(4):
        out_ref[:, 128 * j : 128 * (j + 1)] = res_ref[pl.ds(j, ATTR, stride=4), :]


VMEM = pl.BlockSpec(memory_space=pltpu.VMEM)
SMEM = pl.BlockSpec(memory_space=pltpu.SMEM)
PARAMS = pltpu.CompilerParams(vmem_limit_bytes=24 * 1024 * 1024)


def call(kernel, outs, args, scratch=(), in_specs=None):
    return pl.pallas_call(
        kernel,
        out_shape=[jax.ShapeDtypeStruct(s, d) for s, d in outs],
        in_specs=in_specs or [VMEM] * len(args),
        out_specs=[VMEM] * len(outs),
        scratch_shapes=[pltpu.VMEM(s, F32) for s in scratch],
        compiler_params=PARAMS,
    )(*args)


def route(owner, local, attributes, camera):
    return call(
        route_kernel,
        [((OWNERS, 128), F32), ((1, TILES * SLOTS), I32), ((CAP, OWNERS), I32), ((16, G_DEV), F32)],
        (owner, local, attributes, camera),
        [(ATTR * 8, 128), (128, 128)],
    )


def serve(asked, rows):
    return call(serve_kernel, [((2 * OWNERS, 128), F32), ((CAP, OWNERS), I32)], (asked, rows))


def composite(first_tile, got, owner, rank, inv, depth, cot):
    big = (SLOTS * 8, 128)
    return call(
        composite_kernel,
        [((3, TILES, 256), F32), ((2 * OWNERS, 128), F32)],
        (first_tile, got, owner, rank, inv, depth, cot),
        [(16, TILES * SLOTS), big, big, big, (16, TILES * SLOTS), (8, 128)],
        [SMEM] + [VMEM] * 6,
    )


def collect(back, ids, camera):
    return call(collect_kernel, [((40 * VIEWS, 128), F32)], (back, ids, camera))[0]


def pull_back(everything, attributes):
    return call(
        pull_kernel, [((ATTR, G_DEV), F32)], (everything, attributes), [(ATTR * 8, 128), (ATTR * 4, 128)]
    )[0]


def exchange(x, axis="dev"):
    return lax.all_to_all(x, axis, split_axis=0, concat_axis=0, tiled=True)


def per_device(attributes, camera, list_owner, list_local, term_depth, image_cot):
    owner = list_owner.reshape(1, -1)
    asked, rank, inv, rows = route(owner, list_local[0], attributes, camera)
    asked = exchange(asked.reshape(OWNERS, 1, 128)).reshape(OWNERS, 128)
    sent, ids = serve(asked, rows)
    got = exchange(sent.reshape(OWNERS, 2, 128)).reshape(2 * OWNERS, 128)
    first_tile = (lax.axis_index("dev") * TILES).astype(I32).reshape(1)
    image, grads = composite(first_tile, got, owner, rank, inv, term_depth[0], image_cot[0])
    back = exchange(grads.reshape(OWNERS, 2, 128)).reshape(2 * OWNERS, 128)
    mine = collect(back, ids, camera)
    everything = exchange(mine.reshape(VIEWS, 40, 128), "view").reshape(VIEWS * 40, 128)
    return image[None], pull_back(everything, attributes)


def solution(mesh):
    in_specs = (
        P(None, "dev"),
        P("view", None),
        P("view", "dev", None, None),
        P("view", "dev", None),
        P("view", "dev", None),
        P("view", None, "dev", None),
    )
    out_specs = (P("view", None, "dev", None), P(None, "dev"))
    return jax.shard_map(
        per_device, mesh=mesh, in_specs=in_specs, out_specs=out_specs, check_vma=False
    )
```

```python
import jax
import jax.numpy as jnp
from jax import lax
from jax.experimental import pallas as pl
from jax.experimental.pallas import tpu as pltpu
from jax.sharding import PartitionSpec as P

TILE_COLS = 16
TILES = 4
SLOTS = 256
CAP = 16
OWNERS = 128
PLANES = 16
G_DEV = 512
ATTR = 59
VIEWS = 4
LOG2E = 1.4426950408889634

SH_C0 = 0.28209479177387814
SH_C1 = 0.4886025119029199
SH_C2 = (
    1.0925484305920792,
    -1.0925484305920792,
    0.31539156525252005,
    -1.0925484305920792,
    0.5462742152960396,
)
SH_C3 = (
    -0.5900435899266435,
    2.890611442640554,
    -0.4570457994644658,
    0.3731763325901154,
    -0.4570457994644658,
    1.445305721320277,
    -0.5900435899266435,
)
BLUR = 1e-05

F32 = jnp.float32
BF16 = jnp.bfloat16
I32 = jnp.int32


def camera_terms(angles, shift):
    cosx, sinx = jnp.cos(angles[0]), jnp.sin(angles[0])
    cosy, siny = jnp.cos(angles[1]), jnp.sin(angles[1])
    cosz, sinz = jnp.cos(angles[2]), jnp.sin(angles[2])
    yx = [
        [cosy, siny * sinx, siny * cosx],
        [None, cosx, -sinx],
        [-siny, cosy * sinx, cosy * cosx],
    ]
    rot = [
        [cosz * yx[0][0]] + [cosz * yx[0][j] - sinz * yx[1][j] for j in (1, 2)],
        [sinz * yx[0][0]] + [sinz * yx[0][j] + cosz * yx[1][j] for j in (1, 2)],
        yx[2],
    ]
    centre = [-(rot[0][j] * shift[0] + rot[1][j] * shift[1] + rot[2][j] * shift[2]) for j in range(3)]
    return rot, shift, centre


def harmonics(dirx, diry, dirz):
    xx, yy, zz = (dirx * dirx, diry * diry, dirz * dirz)
    return [
        -SH_C1 * diry,
        SH_C1 * dirz,
        -SH_C1 * dirx,
        SH_C2[0] * dirx * diry,
        SH_C2[1] * diry * dirz,
        SH_C2[2] * (2.0 * zz - xx - yy),
        SH_C2[3] * dirx * dirz,
        SH_C2[4] * (xx - yy),
        SH_C3[0] * diry * (3.0 * xx - yy),
        SH_C3[1] * dirx * diry * dirz,
        SH_C3[2] * diry * (4.0 * zz - xx - yy),
        SH_C3[3] * dirz * (2.0 * zz - 3.0 * xx - 3.0 * yy),
        SH_C3[4] * dirx * (4.0 * zz - xx - yy),
        SH_C3[5] * dirz * (xx - yy),
        SH_C3[6] * dirx * (xx - 3.0 * yy),
    ]


def project(pos, logscale, quat, sh, cam):
    rot, shift, centre = cam
    cpos = [rot[i][0] * pos[0] + rot[i][1] * pos[1] + rot[i][2] * pos[2] + shift[i] for i in range(3)]
    inverse = 1.0 / cpos[2]
    u, w = cpos[0] * inverse, cpos[1] * inverse
    tmat = [
        [inverse * (rot[0][j] - u * rot[2][j]) for j in range(3)],
        [inverse * (rot[1][j] - w * rot[2][j]) for j in range(3)],
    ]
    scale = [jnp.exp(s) for s in logscale]
    norm = lax.rsqrt(quat[0] * quat[0] + quat[1] * quat[1] + quat[2] * quat[2] + quat[3] * quat[3])
    qw, qa, qb, qc = [q * norm for q in quat]
    rgau = [
        [1 - 2 * (qb * qb + qc * qc), 2 * (qa * qb - qw * qc), 2 * (qa * qc + qw * qb)],
        [2 * (qa * qb + qw * qc), 1 - 2 * (qa * qa + qc * qc), 2 * (qb * qc - qw * qa)],
        [2 * (qa * qc - qw * qb), 2 * (qb * qc + qw * qa), 1 - 2 * (qa * qa + qb * qb)],
    ]
    trs = [
        [(tmat[r][0] * rgau[0][k] + tmat[r][1] * rgau[1][k] + tmat[r][2] * rgau[2][k]) * scale[k] for k in range(3)]
        for r in range(2)
    ]
    sig_a = trs[0][0] * trs[0][0] + trs[0][1] * trs[0][1] + trs[0][2] * trs[0][2] + BLUR
    sig_b = trs[0][0] * trs[1][0] + trs[0][1] * trs[1][1] + trs[0][2] * trs[1][2]
    sig_c = trs[1][0] * trs[1][0] + trs[1][1] * trs[1][1] + trs[1][2] * trs[1][2] + BLUR
    det_inv = 1.0 / (sig_a * sig_c - sig_b * sig_b)
    dirs = [pos[j] - centre[j] for j in range(3)]
    norm_inv = lax.rsqrt(dirs[0] * dirs[0] + dirs[1] * dirs[1] + dirs[2] * dirs[2])
    basis = harmonics(dirs[0] * norm_inv, dirs[1] * norm_inv, dirs[2] * norm_inv)
    colors = []
    for ch in range(3):
        color = 0.5 + SH_C0 * sh[ch]
        for k in range(1, 16):
            color = color + basis[k - 1] * sh[3 * k + ch]
        colors.append(color)
    return [u, w, sig_c * det_inv, -sig_b * det_inv, sig_a * det_inv] + colors


def spread_attributes(attr_ref, wide_ref):
    for j in range(4):
        part = attr_ref[:, 128 * j : 128 * (j + 1)]
        wide_ref[pl.ds(j, ATTR, stride=8), :] = part
        wide_ref[pl.ds(j + 4, ATTR, stride=8), :] = part


def split_attributes(wide_ref):
    attrs = [wide_ref[8 * a : 8 * (a + 1), :] for a in range(ATTR)]
    return attrs[0:3], attrs[3:6], attrs[6:10], attrs[10], attrs[11:]


def dot(a, b, ca, cb):
    return lax.dot_general(a, b, (((ca,), (cb,)), ((), ())), preferred_element_type=F32)


def lane_gather(x, idx):
    return jnp.take_along_axis(x, idx, axis=1, mode="promise_in_bounds")


def split2(x):
    hi = x.astype(BF16)
    return hi, (x - hi.astype(F32)).astype(BF16)


def split3(x):
    hi = x.astype(BF16)
    rest = x - hi.astype(F32)
    mid = rest.astype(BF16)
    return hi, mid, (rest - mid.astype(F32)).astype(BF16)


def route_kernel(
    owner_hbm, local_hbm, attr_hbm, cam_hbm, asked_ref, inv_ref, place_ref, rows_ref,
    owner_ref, local_ref, attr_ref, cam_ref, wide_ref, sem,
):
    pairs = [(owner_hbm, owner_ref), (local_hbm, local_ref), (attr_hbm, attr_ref), (cam_hbm, cam_ref)]
    copies = [pltpu.make_async_copy(src, dst, sem.at[n]) for n, (src, dst) in enumerate(pairs)]
    for copy in copies:
        copy.start()
    before = (
        lax.broadcasted_iota(I32, (SLOTS, SLOTS), 0) < lax.broadcasted_iota(I32, (SLOTS, SLOTS), 1)
    ).astype(F32).astype(BF16)
    every = jnp.ones((SLOTS, SLOTS), BF16)
    oid = lax.broadcasted_iota(I32, (OWNERS, SLOTS), 0)
    zid = lax.broadcasted_iota(I32, (PLANES, SLOTS), 0)
    lane = lax.broadcasted_iota(I32, (1, SLOTS), 1)
    base = jnp.zeros((OWNERS, SLOTS), F32)
    table = jnp.zeros((4 * PLANES, 128), F32)
    copies[0].wait()
    copies[1].wait()
    for t in range(TILES):
        owner = owner_ref[:, SLOTS * t : SLOTS * (t + 1)]
        hot = (oid == owner).astype(F32)
        hot16 = hot.astype(BF16)
        count = dot(hot16, before, 1, 0) + base
        base = base + dot(hot16, every, 1, 0)
        rank = jnp.sum(hot * count, axis=0, keepdims=True).astype(I32)
        plane = owner >> 3
        lanes = (owner & 7) * CAP + rank
        place_ref[0:1, SLOTS * t : SLOTS * (t + 1)] = plane
        place_ref[1:2, SLOTS * t : SLOTS * (t + 1)] = lanes
        hot_plane = (zid == plane).astype(F32)
        hot_lane = (oid == lanes).astype(F32).astype(BF16)
        local = local_ref[t : t + 1, :]
        slot = lane + (SLOTS * t + 1)
        parts = [local & 255, local >> 8, slot & 255, slot >> 8]
        vals = jnp.concatenate([hot_plane * p.astype(F32) for p in parts], axis=0).astype(BF16)
        table = table + dot(vals, hot_lane, 1, 1)
    n = PLANES
    asked_ref[...] = table[0:n] + 256.0 * table[n : 2 * n]
    inv_ref[...] = (table[2 * n : 3 * n] + 256.0 * table[3 * n :]).astype(I32)
    copies[2].wait()
    copies[3].wait()
    spread_attributes(attr_ref, wide_ref)
    pos, logscale, quat, logit, sh = split_attributes(wide_ref)
    cam = [jnp.broadcast_to(cam_ref[:, j : j + 1], (8, 128)) for j in range(6)]
    rows = project(pos, logscale, quat, sh, camera_terms(cam[:3], cam[3:]))
    log_opacity = -LOG2E * jnp.log(1.0 + jnp.exp(-logit))
    rows = rows[:5] + [log_opacity] + rows[5:]
    for c in range(8):
        rows_ref[pl.ds(c, 4, stride=8), :] = rows[c][0:4]
    rows_ref[32:36, :] = rows[8][0:4]
    rows_ref[36:40, :] = jnp.zeros((4, 128), F32)


def serve_kernel(asked_ref, rows_ref, out_ref):
    table = []
    for j in range(4):
        part = [rows_ref[40 * r + 8 * j : 40 * r + 8 * j + 8, :] for r in range(8)]
        part.append(rows_ref[pl.ds(32 + j, 8, stride=40), :])
        table.append(jnp.concatenate(part, axis=0))
    table = [x.astype(F32) for x in split3(jnp.concatenate(table, axis=1))]
    table = jnp.concatenate(table + [jnp.zeros((8, G_DEV), F32)], axis=0).astype(BF16)
    lid = lax.broadcasted_iota(I32, (G_DEV, 256), 0)
    sub = lax.broadcasted_iota(I32, (8, 128), 0)
    near = lax.broadcasted_iota(I32, (8, 128), 1) >> 4
    for z in range(0, PLANES, 2):
        ids = jnp.concatenate([asked_ref[z : z + 1, :], asked_ref[z + 1 : z + 2, :]], axis=1).astype(I32)
        hot = (lid == ids).astype(F32).astype(BF16)
        got = dot(table, hot, 1, 0)
        got = got[0:72] + got[72:144] + got[144:216]
        for i in range(2):
            half = got[:, 128 * i : 128 * (i + 1)]
            main = half[0:8]
            for r in range(1, 8):
                main = jnp.where(near == r, half[8 * r : 8 * (r + 1)], main)
            out_ref[9 * (z + i) : 9 * (z + i) + 8, :] = main
            last = jnp.sum(jnp.where(near == sub, half[64:72], 0.0), axis=0, keepdims=True)
            out_ref[9 * (z + i) + 8 : 9 * (z + i) + 9, :] = last


def composite_kernel(
    tile_ref, got_ref, place_ref, inv_ref, depth_ref, cot_ref, image_ref, out_ref,
    par_ref, alpha_ref, pull_ref, weight_ref, grad_ref,
):
    last = got_ref[pl.ds(8, PLANES, stride=9), :]
    sub = lax.broadcasted_iota(I32, (8, 128), 0)
    for b in range(8):
        plane = jnp.broadcast_to(place_ref[0:1, 128 * b : 128 * (b + 1)], (8, 128))
        lanes = jnp.broadcast_to(place_ref[1:2, 128 * b : 128 * (b + 1)], (8, 128))
        got = lane_gather(got_ref[0:8, :], lanes)
        for z in range(1, PLANES):
            got = jnp.where(plane == z, lane_gather(got_ref[9 * z : 9 * z + 8, :], lanes), got)
        par_ref[0:8, 128 * b : 128 * (b + 1)] = got
        low = jnp.where(plane == sub, lane_gather(last[0:8], lanes), 0.0)
        high = jnp.where(plane == sub + 8, lane_gather(last[8:16], lanes), 0.0)
        par_ref[8:9, 128 * b : 128 * (b + 1)] = jnp.sum(low + high, axis=0, keepdims=True)

    q = lax.broadcasted_iota(I32, (16, 128), 1)
    row16 = lax.broadcasted_iota(I32, (16, 128), 0)
    X = (q & 15).astype(F32) - 7.5
    Y = (q >> 4).astype(F32) - 3.5
    mono = jnp.where(row16 == 0, 1.0, 0.0)
    for n, m in enumerate([X, Y, X * X, X * Y, Y * Y]):
        mono = jnp.where(row16 == n + 1, m, mono)
    mono8 = mono[0:8]
    mono16 = mono.astype(BF16)
    mono_twice = jnp.concatenate([mono16, mono16], axis=1)
    ex, ey = 1.0 / (16.0 * TILE_COLS), 1.0 / (16.0 * (TILES * OWNERS // TILE_COLS))

    zero = jnp.zeros((1, SLOTS), F32)
    zero5 = jnp.zeros((5, SLOTS), F32)
    blank = jnp.zeros((8, 128), F32)
    cots = []
    geometry = []
    for t in range(TILES):
        par = [par_ref[c : c + 1, SLOTS * t : SLOTS * (t + 1)] for c in range(9)]
        u, w, ca, cb, cc, log_op = par[:6]
        tile = tile_ref[0] + t
        cx = ((tile % TILE_COLS) * 16 + 8).astype(F32) * ex - 0.5
        dx0 = cx - u
        A, B, C = -0.5 * LOG2E * ca, -LOG2E * cb, -0.5 * LOG2E * cc
        colors = jnp.concatenate([par[6], par[7], par[8], zero5], axis=0)
        chi, cmid, clo = [c.astype(F32) for c in split3(colors)]
        dy0s = []
        for h in range(2):
            th = 4 * h + t
            cy = ((tile // TILE_COLS) * 16 + 8 * h + 4).astype(F32) * ey - 0.5
            dy0 = cy - w
            dy0s.append(dy0)
            coef = jnp.concatenate(
                [
                    (A * dx0 + B * dy0) * dx0 + C * dy0 * dy0 + log_op,
                    (2.0 * A * dx0 + B * dy0) * ex,
                    (B * dx0 + 2.0 * C * dy0) * ey,
                    A * (ex * ex),
                    B * (ex * ey),
                    C * (ey * ey),
                    zero,
                    zero,
                ],
                axis=0,
            )
            khi, kmid, klo = [k.astype(F32) for k in split3(coef)]
            left = jnp.concatenate([khi, kmid, klo, chi, chi, chi, cmid, cmid, clo], axis=0)
            left = jnp.concatenate([left, jnp.zeros((128 - 72, SLOTS), F32)], axis=0)
            g = jnp.concatenate([cot_ref[c, t : t + 1, 128 * h : 128 * (h + 1)] for c in range(3)] + [blank[0:5]], axis=0)
            ghi, gmid, glo = [x.astype(F32) for x in split3(g)]
            cots.append((th, ghi, gmid))
            right = jnp.concatenate(
                [
                    jnp.concatenate([mono8, mono8, mono8, blank, blank, blank, blank, blank, blank], axis=0),
                    jnp.concatenate([blank, blank, blank, ghi, gmid, glo, ghi, gmid, ghi], axis=0),
                ],
                axis=1,
            )
            right = jnp.concatenate([right, jnp.zeros((128 - 72, 256), F32)], axis=0)
            both = dot(jnp.transpose(left).astype(BF16), right.astype(BF16), 1, 0)
            alpha_ref[pl.ds(th, SLOTS, stride=8), :] = both[:, :128]
            pull_ref[pl.ds(th, SLOTS, stride=8), :] = both[:, 128:]
        geometry.append((ca, cb, cc, dx0, dy0s, chi, cmid))

    depth = jnp.concatenate([depth_ref[:, 0:128], depth_ref[:, 128:256]], axis=0)
    unroll = 8

    def forward(j, trans):
        for i in range(unroll):
            s = j * unroll + i
            at = pl.ds(pl.multiple_of(s * 8, 8), 8)
            alpha = jnp.where(s < depth, jnp.exp2(alpha_ref[at, :]), 0.0)
            weight = trans * alpha
            alpha_ref[at, :] = alpha
            weight_ref[at, :] = weight
            trans = trans - weight
        return trans

    lax.fori_loop(0, SLOTS // unroll, forward, jnp.ones((8, 128), F32))

    def backward(j, rest):
        for i in range(unroll):
            s = SLOTS - 1 - (j * unroll + i)
            at = pl.ds(pl.multiple_of(s * 8, 8), 8)
            more = pull_ref[at, :] - rest
            rest = rest + alpha_ref[at, :] * more
            pull_ref[at, :] = weight_ref[at, :] * more
        return rest

    lax.fori_loop(0, SLOTS // unroll, backward, jnp.zeros((8, 128), F32))

    cots = {th: (ghi, gmid) for th, ghi, gmid in cots}
    for t in range(TILES):
        ca, cb, cc, dx0, dy0s, chi, cmid = geometry[t]
        color_rows = jnp.concatenate([chi, cmid], axis=0).astype(BF16)
        total = [jnp.zeros((1, SLOTS), F32) for _ in range(6)]
        dcolor = jnp.zeros((3, SLOTS), F32)
        for h in range(2):
            th = 4 * h + t
            dy0 = dy0s[h]
            whi, wlo = split2(weight_ref[pl.ds(th, SLOTS, stride=8), :])
            weights = jnp.concatenate([whi, wlo], axis=1)
            ghi, glo = split2(pull_ref[pl.ds(th, SLOTS, stride=8), :])
            grads = jnp.concatenate([ghi, glo], axis=1)
            seen = dot(color_rows, weights, 1, 0)
            seen = seen[:, :128] + seen[:, 128:]
            seen = seen[0:8] + seen[8:16]
            for c in range(3):
                image_ref[c, t : t + 1, 128 * h : 128 * (h + 1)] = seen[c : c + 1]
            cot = jnp.concatenate(cots[th], axis=0).astype(BF16)
            dcol = dot(jnp.concatenate([cot, cot], axis=1), weights, 1, 1)
            dcolor = dcolor + dcol[0:3] + dcol[8:11]
            mom = dot(mono_twice, grads, 1, 1)
            m0 = mom[0:1]
            mx, my = ex * mom[1:2], ey * mom[2:3]
            total[0] = total[0] + m0
            total[1] = total[1] + dx0 * m0 + mx
            total[2] = total[2] + dy0 * m0 + my
            total[3] = total[3] + dx0 * (dx0 * m0 + 2.0 * mx) + (ex * ex) * mom[3:4]
            total[4] = total[4] + dx0 * (dy0 * m0 + my) + dy0 * mx + (ex * ey) * mom[4:5]
            total[5] = total[5] + dy0 * (dy0 * m0 + 2.0 * my) + (ey * ey) * mom[5:6]
        s0, sx, sy, sxx, sxy, syy = total
        made = [ca * sx + cb * sy, cb * sx + cc * sy, -0.5 * sxx, -sxy, -0.5 * syy, s0, dcolor]
        grad_ref[0:9, SLOTS * t : SLOTS * (t + 1)] = jnp.concatenate(made, axis=0)

    inv = inv_ref[...]

    def pick(tables, idx):
        at = jnp.maximum(idx - 1, 0)
        low, high = at & 127, at >> 7
        got = lane_gather(tables[0], low)
        for j in range(1, 8):
            got = jnp.where(high == j, lane_gather(tables[j], low), got)
        return jnp.where(idx > 0, got, 0.0)

    tables = [grad_ref[0:8, 128 * j : 128 * (j + 1)] for j in range(8)]
    last = [jnp.broadcast_to(grad_ref[8:9, 128 * j : 128 * (j + 1)], (8, 128)) for j in range(8)]
    for z in range(PLANES):
        out_ref[9 * z : 9 * z + 8, :] = pick(tables, jnp.broadcast_to(inv[z : z + 1], (8, 128)))
    more = jnp.concatenate([pick(last, inv[0:8]), pick(last, inv[8:16])], axis=0)
    out_ref[pl.ds(8, PLANES, stride=9), :] = more


def collect_kernel(back_ref, asked_ref, cam_ref, out_ref):
    lid = lax.broadcasted_iota(I32, (G_DEV, 256), 0)
    sub = lax.broadcasted_iota(I32, (8, 128), 0)
    near = lax.broadcasted_iota(I32, (8, 128), 1) >> 4
    acc = jnp.zeros((144, G_DEV), F32)
    for z in range(0, PLANES, 2):
        ids = jnp.concatenate([asked_ref[z : z + 1, :], asked_ref[z + 1 : z + 2, :]], axis=1).astype(I32)
        hot = (lid == ids).astype(F32).astype(BF16)
        left = []
        for i in range(2):
            at = 9 * (z + i)
            main = [x.astype(F32) for x in split2(back_ref[at : at + 8, :])]
            last = [x.astype(F32) for x in split2(jnp.broadcast_to(back_ref[at + 8 : at + 9, :], (8, 128)))]
            rows = []
            for m, l in zip(main, last):
                rows += [jnp.where(near == r, m, 0.0) for r in range(8)] + [jnp.where(near == sub, l, 0.0)]
            left.append(jnp.concatenate(rows, axis=0).astype(BF16))
        acc = acc + dot(jnp.concatenate(left, axis=1), hot, 1, 1)
    rows = acc[0:72] + acc[72:144]
    cam = jnp.concatenate([cam_ref[...], jnp.zeros((1, 122), F32)], axis=1)
    tail = jnp.concatenate([cam, jnp.zeros((3, 128), F32)], axis=0)
    for r in range(8):
        part = [rows[8 * r : 8 * r + 8, 128 * j : 128 * (j + 1)] for j in range(4)]
        part += [rows[64 + r : 65 + r, 128 * j : 128 * (j + 1)] for j in range(4)] + [tail]
        part = jnp.concatenate(part, axis=0)
        for v in range(VIEWS):
            out_ref[40 * (8 * v + r) : 40 * (8 * v + r + 1), :] = part


def pull_kernel(parts_ref, attr_ref, out_ref, wide_ref, res_ref, all_ref):
    for v in range(VIEWS):
        start = 320 * v
        total = parts_ref[start : start + 36, :]
        for r in range(1, 8):
            total = total + parts_ref[start + 40 * r : start + 40 * r + 36, :]
        all_ref[40 * v : 40 * v + 36, :] = total
        all_ref[40 * v + 36 : 40 * v + 40, :] = parts_ref[start + 36 : start + 40, :]
    spread_attributes(attr_ref, wide_ref)
    pos, logscale, quat, logit, sh = split_attributes(wide_ref)
    total = None
    opacity_grad = None
    for pair in range(VIEWS // 2):
        starts = (80 * pair, 80 * pair + 40)
        cot = [
            jnp.concatenate([all_ref[pl.ds(s + c, 4, stride=8), :] for s in starts], axis=0) for c in range(8)
        ]
        cot.append(jnp.concatenate([all_ref[s + 32 : s + 36, :] for s in starts], axis=0))
        cam = [
            jnp.concatenate(
                [jnp.broadcast_to(all_ref[s + 36 : s + 37, j : j + 1], (4, 128)) for s in starts], axis=0
            )
            for j in range(6)
        ]
        terms = camera_terms(cam[:3], cam[3:])
        _, pull = jax.vjp(lambda a, b, c, d: project(a, b, c, d, terms), pos, logscale, quat, sh)
        grads = jax.tree.leaves(pull(cot[:5] + cot[6:]))
        total = grads if total is None else [a + b for a, b in zip(total, grads)]
        opacity_grad = cot[5] if opacity_grad is None else opacity_grad + cot[5]
    grads = total[:10] + [opacity_grad / (1.0 + jnp.exp(logit))] + total[10:]
    for a in range(ATTR):
        res_ref[4 * a : 4 * a + 4, :] = grads[a][0:4] + grads[a][4:8]
    for j in range(4):
        out_ref[:, 128 * j : 128 * (j + 1)] = res_ref[pl.ds(j, ATTR, stride=4), :]


VMEM = pl.BlockSpec(memory_space=pltpu.VMEM)
SMEM = pl.BlockSpec(memory_space=pltpu.SMEM)
HBM = pl.BlockSpec(memory_space=pl.ANY)
MIB = 1024 * 1024


def call(kernel, outs, args, scratch=(), in_specs=None, limit=24):
    return pl.pallas_call(
        kernel,
        out_shape=[jax.ShapeDtypeStruct(s, d) for s, d in outs],
        in_specs=in_specs or [VMEM] * len(args),
        out_specs=[VMEM] * len(outs),
        scratch_shapes=list(scratch),
        compiler_params=pltpu.CompilerParams(vmem_limit_bytes=limit * MIB),
    )(*args)


def vmem(*shape, dtype=F32):
    return pltpu.VMEM(shape, dtype)


def route(owner, local, attributes, camera):
    return call(
        route_kernel,
        [((PLANES, 128), F32), ((PLANES, 128), I32), ((8, TILES * SLOTS), I32), ((40, 128), F32)],
        (owner, local, attributes, camera),
        [
            vmem(1, TILES * SLOTS, dtype=I32), vmem(TILES, SLOTS, dtype=I32), vmem(ATTR, G_DEV), vmem(1, 6),
            vmem(ATTR * 8, 128), pltpu.SemaphoreType.DMA((4,)),
        ],
        [HBM] * 4,
        60,
    )


def serve(asked, rows):
    return call(serve_kernel, [((9 * PLANES, 128), F32)], (asked, rows))[0]


def composite(first_tile, got, place, inv, depth, cot):
    big = vmem(SLOTS * 8, 128)
    return call(
        composite_kernel,
        [((3, TILES, 256), F32), ((9 * PLANES, 128), F32)],
        (first_tile, got, place, inv, depth, cot),
        [vmem(16, TILES * SLOTS), big, big, big, vmem(16, TILES * SLOTS)],
        [SMEM] + [VMEM] * 5,
    )


def collect(back, asked, camera):
    return call(collect_kernel, [((32 * 40, 128), F32)], (back, asked, camera))[0]


def pull_back(parts, attributes):
    return call(
        pull_kernel,
        [((ATTR, G_DEV), F32)],
        (parts, attributes),
        [vmem(ATTR * 8, 128), vmem(ATTR * 4, 128), vmem(40 * VIEWS, 128)],
    )[0]


def exchange(x, axis, groups):
    return lax.all_to_all(x, axis, split_axis=0, concat_axis=0, tiled=True, axis_index_groups=groups)


ACROSS = [[8 * z + r for z in range(PLANES)] for r in range(8)]
WITHIN = [[8 * z + r for r in range(8)] for z in range(PLANES)]
VIEWS_WITHIN = [[OWNERS * v + d for v in range(VIEWS) for d in group] for group in WITHIN]


def per_device(attributes, camera, list_owner, list_local, term_depth, image_cot):
    owner = list_owner.reshape(1, -1)
    asked, inv, place, rows = route(owner, list_local[0], attributes, camera)
    asked = exchange(asked.reshape(PLANES, 1, 128), "dev", ACROSS).reshape(PLANES, 128)
    rows = lax.all_gather(rows, "dev", axis_index_groups=WITHIN, tiled=True)
    sent = serve(asked, rows)
    got = exchange(sent.reshape(PLANES, 1, 1152), "dev", ACROSS).reshape(9 * PLANES, 128)
    first_tile = (lax.axis_index("dev") * TILES).astype(I32).reshape(1)
    image, grads = composite(first_tile, got, place, inv, term_depth[0], image_cot[0])
    back = exchange(grads.reshape(PLANES, 1, 1152), "dev", ACROSS).reshape(9 * PLANES, 128)
    mine = collect(back, asked, camera)
    parts = exchange(mine.reshape(32, 40, 128), ("view", "dev"), VIEWS_WITHIN).reshape(32 * 40, 128)
    return image[None], pull_back(parts, attributes)


def solution(mesh):
    in_specs = (
        P(None, "dev"),
        P("view", None),
        P("view", "dev", None, None),
        P("view", "dev", None),
        P("view", "dev", None),
        P("view", None, "dev", None),
    )
    out_specs = (P("view", None, "dev", None), P(None, "dev"))
    return jax.shard_map(
        per_device, mesh=mesh, in_specs=in_specs, out_specs=out_specs, check_vma=False
    )
```

```python
import jax
import jax.numpy as jnp
from jax import lax
from jax.experimental import pallas as pl
from jax.experimental.pallas import tpu as pltpu
from jax.sharding import PartitionSpec as P

TILE_COLS = 16
TILES = 4
SLOTS = 256
CAP = 16
OWNERS = 128
PEERS = 32
NEAR = 4
G_DEV = 512
ATTR = 59
VIEWS = 4
LOG2E = 1.4426950408889634

SH_C0 = 0.28209479177387814
SH_C1 = 0.4886025119029199
SH_C2 = (
    1.0925484305920792,
    -1.0925484305920792,
    0.31539156525252005,
    -1.0925484305920792,
    0.5462742152960396,
)
SH_C3 = (
    -0.5900435899266435,
    2.890611442640554,
    -0.4570457994644658,
    0.3731763325901154,
    -0.4570457994644658,
    1.445305721320277,
    -0.5900435899266435,
)
BLUR = 1e-05

F32 = jnp.float32
BF16 = jnp.bfloat16
I32 = jnp.int32


def camera_terms(angles, shift):
    cosx, sinx = jnp.cos(angles[0]), jnp.sin(angles[0])
    cosy, siny = jnp.cos(angles[1]), jnp.sin(angles[1])
    cosz, sinz = jnp.cos(angles[2]), jnp.sin(angles[2])
    yx = [
        [cosy, siny * sinx, siny * cosx],
        [None, cosx, -sinx],
        [-siny, cosy * sinx, cosy * cosx],
    ]
    rot = [
        [cosz * yx[0][0]] + [cosz * yx[0][j] - sinz * yx[1][j] for j in (1, 2)],
        [sinz * yx[0][0]] + [sinz * yx[0][j] + cosz * yx[1][j] for j in (1, 2)],
        yx[2],
    ]
    centre = [-(rot[0][j] * shift[0] + rot[1][j] * shift[1] + rot[2][j] * shift[2]) for j in range(3)]
    return rot, shift, centre


def harmonics(dirx, diry, dirz):
    xx, yy, zz = (dirx * dirx, diry * diry, dirz * dirz)
    return [
        -SH_C1 * diry,
        SH_C1 * dirz,
        -SH_C1 * dirx,
        SH_C2[0] * dirx * diry,
        SH_C2[1] * diry * dirz,
        SH_C2[2] * (2.0 * zz - xx - yy),
        SH_C2[3] * dirx * dirz,
        SH_C2[4] * (xx - yy),
        SH_C3[0] * diry * (3.0 * xx - yy),
        SH_C3[1] * dirx * diry * dirz,
        SH_C3[2] * diry * (4.0 * zz - xx - yy),
        SH_C3[3] * dirz * (2.0 * zz - 3.0 * xx - 3.0 * yy),
        SH_C3[4] * dirx * (4.0 * zz - xx - yy),
        SH_C3[5] * dirz * (xx - yy),
        SH_C3[6] * dirx * (xx - 3.0 * yy),
    ]


def project(pos, logscale, quat, sh, cam):
    rot, shift, centre = cam
    cpos = [rot[i][0] * pos[0] + rot[i][1] * pos[1] + rot[i][2] * pos[2] + shift[i] for i in range(3)]
    inverse = 1.0 / cpos[2]
    u, w = cpos[0] * inverse, cpos[1] * inverse
    tmat = [
        [inverse * (rot[0][j] - u * rot[2][j]) for j in range(3)],
        [inverse * (rot[1][j] - w * rot[2][j]) for j in range(3)],
    ]
    scale = [jnp.exp(s) for s in logscale]
    norm = lax.rsqrt(quat[0] * quat[0] + quat[1] * quat[1] + quat[2] * quat[2] + quat[3] * quat[3])
    qw, qa, qb, qc = [q * norm for q in quat]
    rgau = [
        [1 - 2 * (qb * qb + qc * qc), 2 * (qa * qb - qw * qc), 2 * (qa * qc + qw * qb)],
        [2 * (qa * qb + qw * qc), 1 - 2 * (qa * qa + qc * qc), 2 * (qb * qc - qw * qa)],
        [2 * (qa * qc - qw * qb), 2 * (qb * qc + qw * qa), 1 - 2 * (qa * qa + qb * qb)],
    ]
    trs = [
        [(tmat[r][0] * rgau[0][k] + tmat[r][1] * rgau[1][k] + tmat[r][2] * rgau[2][k]) * scale[k] for k in range(3)]
        for r in range(2)
    ]
    sig_a = trs[0][0] * trs[0][0] + trs[0][1] * trs[0][1] + trs[0][2] * trs[0][2] + BLUR
    sig_b = trs[0][0] * trs[1][0] + trs[0][1] * trs[1][1] + trs[0][2] * trs[1][2]
    sig_c = trs[1][0] * trs[1][0] + trs[1][1] * trs[1][1] + trs[1][2] * trs[1][2] + BLUR
    det_inv = 1.0 / (sig_a * sig_c - sig_b * sig_b)
    dirs = [pos[j] - centre[j] for j in range(3)]
    norm_inv = lax.rsqrt(dirs[0] * dirs[0] + dirs[1] * dirs[1] + dirs[2] * dirs[2])
    basis = harmonics(dirs[0] * norm_inv, dirs[1] * norm_inv, dirs[2] * norm_inv)
    colors = []
    for ch in range(3):
        color = 0.5 + SH_C0 * sh[ch]
        for k in range(1, 16):
            color = color + basis[k - 1] * sh[3 * k + ch]
        colors.append(color)
    return [u, w, sig_c * det_inv, -sig_b * det_inv, sig_a * det_inv] + colors


def spread_attributes(attr_ref, wide_ref):
    for j in range(4):
        part = attr_ref[:, 128 * j : 128 * (j + 1)]
        wide_ref[pl.ds(j, ATTR, stride=8), :] = part
        wide_ref[pl.ds(j + 4, ATTR, stride=8), :] = part


def split_attributes(wide_ref):
    attrs = [wide_ref[8 * a : 8 * (a + 1), :] for a in range(ATTR)]
    return attrs[0:3], attrs[3:6], attrs[6:10], attrs[10], attrs[11:]


def dot(a, b, ca, cb):
    return lax.dot_general(a, b, (((ca,), (cb,)), ((), ())), preferred_element_type=F32)


def lane_gather(x, idx):
    return jnp.take_along_axis(x, idx, axis=1, mode="promise_in_bounds")


def split2(x):
    hi = x.astype(BF16)
    return hi, (x - hi.astype(F32)).astype(BF16)


def split3(x):
    hi = x.astype(BF16)
    rest = x - hi.astype(F32)
    mid = rest.astype(BF16)
    return hi, mid, (rest - mid.astype(F32)).astype(BF16)


def route_kernel(
    tile_ref, owner_hbm, local_hbm, attr_hbm, cam_hbm, asked_ref, inv_ref, place_ref, rows_ref,
    owner_ref, local_ref, attr_ref, cam_ref, wide_ref, sem,
):
    pairs = [(owner_hbm, owner_ref), (local_hbm, local_ref), (attr_hbm, attr_ref), (cam_hbm, cam_ref)]
    copies = [pltpu.make_async_copy(src, dst, sem.at[n]) for n, (src, dst) in enumerate(pairs)]
    for copy in copies:
        copy.start()
    before = (
        lax.broadcasted_iota(I32, (SLOTS, SLOTS), 0) < lax.broadcasted_iota(I32, (SLOTS, SLOTS), 1)
    ).astype(F32).astype(BF16)
    every = jnp.ones((SLOTS, SLOTS), BF16)
    oid = lax.broadcasted_iota(I32, (OWNERS, SLOTS), 0)
    pid = lax.broadcasted_iota(I32, (PEERS, SLOTS), 0)
    lane = lax.broadcasted_iota(I32, (1, SLOTS), 1)
    base = jnp.zeros((OWNERS, SLOTS), F32)
    table = jnp.zeros((4 * PEERS, 128), F32)
    copies[0].wait()
    copies[1].wait()
    for t in range(TILES):
        owner = owner_ref[:, SLOTS * t : SLOTS * (t + 1)]
        hot = (oid == owner).astype(F32)
        hot16 = hot.astype(BF16)
        count = dot(hot16, before, 1, 0) + base
        base = base + dot(hot16, every, 1, 0)
        rank = jnp.sum(hot * count, axis=0, keepdims=True).astype(I32)
        peer = (owner >> 3) * 2 + (owner & 1)
        lanes = ((owner >> 1) & 3) * CAP + rank
        place_ref[0:1, SLOTS * t : SLOTS * (t + 1)] = peer
        place_ref[1:2, SLOTS * t : SLOTS * (t + 1)] = lanes
        hot_peer = (pid == peer).astype(F32)
        hot_lane = ((oid & 63) == lanes).astype(F32).astype(BF16)
        local = local_ref[t : t + 1, :]
        slot = lane + (SLOTS * t + 1)
        parts = [local & 255, local >> 8, slot & 255, slot >> 8]
        vals = jnp.concatenate([hot_peer * p.astype(F32) for p in parts], axis=0).astype(BF16)
        table = table + dot(vals, hot_lane, 1, 1)
    place_ref[2:3, :] = jnp.full((1, TILES * SLOTS), tile_ref[0], I32)
    n = PEERS
    asked_ref[...] = table[0:n] + 256.0 * table[n : 2 * n]
    inv_ref[...] = (table[2 * n : 3 * n] + 256.0 * table[3 * n :]).astype(I32)
    copies[2].wait()
    copies[3].wait()
    spread_attributes(attr_ref, wide_ref)
    pos, logscale, quat, logit, sh = split_attributes(wide_ref)
    cam = [jnp.broadcast_to(cam_ref[:, j : j + 1], (8, 128)) for j in range(6)]
    rows = project(pos, logscale, quat, sh, camera_terms(cam[:3], cam[3:]))
    log_opacity = -LOG2E * jnp.log(1.0 + jnp.exp(-logit))
    rows = rows[:5] + [log_opacity] + rows[5:]
    for c in range(8):
        rows_ref[pl.ds(c, 4, stride=8), :] = rows[c][0:4]
    rows_ref[32:36, :] = rows[8][0:4]
    rows_ref[36:40, :] = jnp.zeros((4, 128), F32)


def serve_kernel(asked_ref, rows_ref, *refs):
    kept, (out_ref, *outs) = refs[:5], refs[5:]
    for src, dst in zip(kept, outs):
        dst[...] = src[...]
    blank = jnp.zeros((4, 128), F32)
    table = []
    for j in range(4):
        part = [rows_ref[40 * r + 8 * j : 40 * r + 8 * j + 8, :] for r in range(NEAR)]
        part += [rows_ref[pl.ds(32 + j, NEAR, stride=40), :], blank]
        table.append(jnp.concatenate(part, axis=0))
    table = [x.astype(F32) for x in split3(jnp.concatenate(table, axis=1))]
    table = jnp.concatenate(table + [jnp.zeros((8, G_DEV), F32)], axis=0).astype(BF16)
    lid = lax.broadcasted_iota(I32, (G_DEV, 256), 0)
    sub = lax.broadcasted_iota(I32, (8, 128), 0)
    lane = lax.broadcasted_iota(I32, (8, 128), 1)
    near, left = (lane & 63) >> 4, lane < 64
    for n in range(0, PEERS, 4):
        hot = (lid == pair_ids(asked_ref, n)).astype(F32).astype(BF16)
        got = dot(table, hot, 1, 0)
        got = got[0:40] + got[40:80] + got[80:120]
        for i in range(2):
            half = got[:, 128 * i : 128 * (i + 1)]
            main = half[0:8]
            for r in range(1, NEAR):
                main = jnp.where(near == r, half[8 * r : 8 * (r + 1)], main)
            turned = pltpu.roll(main, 64, 1)
            last = jnp.sum(jnp.where(near == sub, half[32:40], 0.0), axis=0, keepdims=True)
            at = 5 * (n + 2 * i)
            out_ref[at : at + 4, :] = jnp.where(left[0:4], main[0:4], turned[4:8])
            out_ref[at + 4 : at + 5, :] = last
            out_ref[at + 5 : at + 9, :] = jnp.where(left[0:4], turned[0:4], main[4:8])
            out_ref[at + 9 : at + 10, :] = pltpu.roll(jnp.broadcast_to(last, (8, 128)), 64, 1)[0:1]


def pair_ids(asked_ref, n):
    left = lax.broadcasted_iota(I32, (1, 128), 1) < 64
    rows = [asked_ref[n + i : n + i + 1, :] for i in range(4)]
    pairs = [jnp.where(left, rows[0], rows[1]), jnp.where(left, rows[2], rows[3])]
    return jnp.concatenate(pairs, axis=1).astype(I32)


def composite_kernel(
    got_ref, place_ref, inv_ref, depth_ref, cot_ref, image_ref, out_ref,
    par_ref, alpha_ref, pull_ref, weight_ref, grad_ref,
):
    last = got_ref[pl.ds(4, PEERS, stride=5), :]
    sub = lax.broadcasted_iota(I32, (8, 128), 0)
    tables = []
    for n in range(PEERS):
        rows = got_ref[5 * n : 5 * n + 4, :]
        tables.append(jnp.concatenate([rows, rows], axis=0))
    for b in range(8):
        peer = jnp.broadcast_to(place_ref[0:1, 128 * b : 128 * (b + 1)], (8, 128))
        lanes = jnp.broadcast_to(place_ref[1:2, 128 * b : 128 * (b + 1)], (8, 128))
        both = jnp.where(sub < 4, lanes, lanes + 64)
        got = lane_gather(tables[0], both)
        for n in range(1, PEERS):
            got = jnp.where(peer == n, lane_gather(tables[n], both), got)
        par_ref[0:8, 128 * b : 128 * (b + 1)] = got
        final = jnp.zeros((8, 128), F32)
        for n in range(0, PEERS, 8):
            final = final + jnp.where(peer == sub + n, lane_gather(last[n : n + 8], lanes), 0.0)
        par_ref[8:9, 128 * b : 128 * (b + 1)] = jnp.sum(final, axis=0, keepdims=True)

    q = lax.broadcasted_iota(I32, (16, 128), 1)
    row16 = lax.broadcasted_iota(I32, (16, 128), 0)
    X = (q & 15).astype(F32) - 7.5
    Y = (q >> 4).astype(F32) - 3.5
    mono = jnp.where(row16 == 0, 1.0, 0.0)
    for n, m in enumerate([X, Y, X * X, X * Y, Y * Y]):
        mono = jnp.where(row16 == n + 1, m, mono)
    mono8 = mono[0:8]
    mono16 = mono.astype(BF16)
    mono_twice = jnp.concatenate([mono16, mono16], axis=1)
    ex, ey = 1.0 / (16.0 * TILE_COLS), 1.0 / (16.0 * (TILES * OWNERS // TILE_COLS))

    zero = jnp.zeros((1, SLOTS), F32)
    zero5 = jnp.zeros((5, SLOTS), F32)
    blank = jnp.zeros((8, 128), F32)
    cots = []
    geometry = []
    for t in range(TILES):
        par = [par_ref[c : c + 1, SLOTS * t : SLOTS * (t + 1)] for c in range(9)]
        u, w, ca, cb, cc, log_op = par[:6]
        tile = place_ref[2:3, 0:SLOTS] + t
        cx = ((tile & (TILE_COLS - 1)) * 16 + 8).astype(F32) * ex - 0.5
        dx0 = cx - u
        A, B, C = -0.5 * LOG2E * ca, -LOG2E * cb, -0.5 * LOG2E * cc
        colors = jnp.concatenate([par[6], par[7], par[8], zero5], axis=0)
        chi, cmid, clo = [c.astype(F32) for c in split3(colors)]
        dy0s = []
        for h in range(2):
            th = 4 * h + t
            cy = ((tile >> 4) * 16 + 8 * h + 4).astype(F32) * ey - 0.5
            dy0 = cy - w
            dy0s.append(dy0)
            coef = jnp.concatenate(
                [
                    (A * dx0 + B * dy0) * dx0 + C * dy0 * dy0 + log_op,
                    (2.0 * A * dx0 + B * dy0) * ex,
                    (B * dx0 + 2.0 * C * dy0) * ey,
                    A * (ex * ex),
                    B * (ex * ey),
                    C * (ey * ey),
                    zero,
                    zero,
                ],
                axis=0,
            )
            khi, kmid, klo = [k.astype(F32) for k in split3(coef)]
            left = jnp.concatenate([khi, kmid, klo, chi, chi, chi, cmid, cmid, clo], axis=0)
            left = jnp.concatenate([left, jnp.zeros((128 - 72, SLOTS), F32)], axis=0)
            g = jnp.concatenate([cot_ref[c, t : t + 1, 128 * h : 128 * (h + 1)] for c in range(3)] + [blank[0:5]], axis=0)
            ghi, gmid, glo = [x.astype(F32) for x in split3(g)]
            cots.append((th, ghi, gmid))
            right = jnp.concatenate(
                [
                    jnp.concatenate([mono8, mono8, mono8, blank, blank, blank, blank, blank, blank], axis=0),
                    jnp.concatenate([blank, blank, blank, ghi, gmid, glo, ghi, gmid, ghi], axis=0),
                ],
                axis=1,
            )
            right = jnp.concatenate([right, jnp.zeros((128 - 72, 256), F32)], axis=0)
            both = dot(jnp.transpose(left).astype(BF16), right.astype(BF16), 1, 0)
            alpha_ref[pl.ds(th, SLOTS, stride=8), :] = both[:, :128]
            pull_ref[pl.ds(th, SLOTS, stride=8), :] = both[:, 128:]
        geometry.append((ca, cb, cc, dx0, dy0s, chi, cmid))

    depth = jnp.concatenate([depth_ref[:, 0:128], depth_ref[:, 128:256]], axis=0)
    unroll = 8

    def forward(j, trans):
        for i in range(unroll):
            s = j * unroll + i
            at = pl.ds(pl.multiple_of(s * 8, 8), 8)
            alpha = jnp.where(s < depth, jnp.exp2(alpha_ref[at, :]), 0.0)
            weight = trans * alpha
            alpha_ref[at, :] = alpha
            weight_ref[at, :] = weight
            trans = trans - weight
        return trans

    lax.fori_loop(0, SLOTS // unroll, forward, jnp.ones((8, 128), F32))

    def backward(j, rest):
        for i in range(unroll):
            s = SLOTS - 1 - (j * unroll + i)
            at = pl.ds(pl.multiple_of(s * 8, 8), 8)
            more = pull_ref[at, :] - rest
            rest = rest + alpha_ref[at, :] * more
            pull_ref[at, :] = weight_ref[at, :] * more
        return rest

    lax.fori_loop(0, SLOTS // unroll, backward, jnp.zeros((8, 128), F32))

    cots = {th: (ghi, gmid) for th, ghi, gmid in cots}
    for t in range(TILES):
        ca, cb, cc, dx0, dy0s, chi, cmid = geometry[t]
        color_rows = jnp.concatenate([chi, cmid], axis=0).astype(BF16)
        total = [jnp.zeros((1, SLOTS), F32) for _ in range(6)]
        dcolor = jnp.zeros((3, SLOTS), F32)
        for h in range(2):
            th = 4 * h + t
            dy0 = dy0s[h]
            whi, wlo = split2(weight_ref[pl.ds(th, SLOTS, stride=8), :])
            weights = jnp.concatenate([whi, wlo], axis=1)
            ghi, glo = split2(pull_ref[pl.ds(th, SLOTS, stride=8), :])
            grads = jnp.concatenate([ghi, glo], axis=1)
            seen = dot(color_rows, weights, 1, 0)
            seen = seen[:, :128] + seen[:, 128:]
            seen = seen[0:8] + seen[8:16]
            for c in range(3):
                image_ref[c, t : t + 1, 128 * h : 128 * (h + 1)] = seen[c : c + 1]
            cot = jnp.concatenate(cots[th], axis=0).astype(BF16)
            dcol = dot(jnp.concatenate([cot, cot], axis=1), weights, 1, 1)
            dcolor = dcolor + dcol[0:3] + dcol[8:11]
            mom = dot(mono_twice, grads, 1, 1)
            m0 = mom[0:1]
            mx, my = ex * mom[1:2], ey * mom[2:3]
            total[0] = total[0] + m0
            total[1] = total[1] + dx0 * m0 + mx
            total[2] = total[2] + dy0 * m0 + my
            total[3] = total[3] + dx0 * (dx0 * m0 + 2.0 * mx) + (ex * ex) * mom[3:4]
            total[4] = total[4] + dx0 * (dy0 * m0 + my) + dy0 * mx + (ex * ey) * mom[4:5]
            total[5] = total[5] + dy0 * (dy0 * m0 + 2.0 * my) + (ey * ey) * mom[5:6]
        s0, sx, sy, sxx, sxy, syy = total
        made = [ca * sx + cb * sy, cb * sx + cc * sy, -0.5 * sxx, -sxy, -0.5 * syy, s0, dcolor]
        grad_ref[0:9, SLOTS * t : SLOTS * (t + 1)] = jnp.concatenate(made, axis=0)

    inv = inv_ref[...]

    def pick(tables, idx):
        at = jnp.maximum(idx - 1, 0)
        low, high = at & 127, at >> 7
        got = lane_gather(tables[0], low)
        for j in range(1, 8):
            got = jnp.where(high == j, lane_gather(tables[j], low), got)
        return jnp.where(idx > 0, got, 0.0)

    tables = [grad_ref[0:8, 128 * j : 128 * (j + 1)] for j in range(8)]
    last = [jnp.broadcast_to(grad_ref[8:9, 128 * j : 128 * (j + 1)], (8, 128)) for j in range(8)]
    left = lax.broadcasted_iota(I32, (4, 128), 1) < 64
    for n in range(PEERS):
        got = pick(tables, jnp.broadcast_to(inv[n : n + 1], (8, 128)))
        out_ref[5 * n : 5 * n + 4, :] = jnp.where(left, got[0:4], got[4:8])
    more = [pick(last, inv[n : n + 8]) for n in range(0, PEERS, 8)]
    out_ref[pl.ds(4, PEERS, stride=5), :] = jnp.concatenate(more, axis=0)


def collect_kernel(back_ref, asked_ref, cam_ref, out_ref):
    lid = lax.broadcasted_iota(I32, (G_DEV, 256), 0)
    sub = lax.broadcasted_iota(I32, (8, 128), 0)
    lane = lax.broadcasted_iota(I32, (8, 128), 1)
    near, left = (lane & 63) >> 4, lane < 64
    acc = jnp.zeros((80, G_DEV), F32)
    for n in range(0, PEERS, 4):
        hot = (lid == pair_ids(asked_ref, n)).astype(F32).astype(BF16)
        pairs = []
        for i in range(2):
            at = 5 * (n + 2 * i)
            one = jnp.concatenate([back_ref[at : at + 4, :]] * 2, axis=0)
            two = jnp.concatenate([back_ref[at + 5 : at + 9, :]] * 2, axis=0)
            other = jnp.where(left, pltpu.roll(one, 64, 1), two)
            straight = jnp.where(left, one, pltpu.roll(two, 64, 1))
            main = jnp.where(sub < 4, straight, other)
            last_one = jnp.broadcast_to(back_ref[at + 4 : at + 5, :], (8, 128))
            last_two = jnp.broadcast_to(back_ref[at + 9 : at + 10, :], (8, 128))
            last = jnp.where(left, last_one, pltpu.roll(last_two, 64, 1))
            rows = []
            for m, l in zip(split2(main), split2(last)):
                m, l = m.astype(F32), l.astype(F32)
                rows += [jnp.where(near == r, m, 0.0) for r in range(NEAR)] + [jnp.where(near == sub, l, 0.0)]
            pairs.append(jnp.concatenate(rows, axis=0).astype(BF16))
        acc = acc + dot(jnp.concatenate(pairs, axis=1), hot, 1, 1)
    rows = acc[0:40] + acc[40:80]
    cam = jnp.concatenate([cam_ref[...], jnp.zeros((1, 122), F32)], axis=1)
    tail = jnp.concatenate([cam, jnp.zeros((3, 128), F32)], axis=0)
    for r in range(NEAR):
        part = [rows[8 * r : 8 * r + 8, 128 * j : 128 * (j + 1)] for j in range(4)]
        part += [rows[32 + r : 33 + r, 128 * j : 128 * (j + 1)] for j in range(4)] + [tail]
        part = jnp.concatenate(part, axis=0)
        for v in range(VIEWS):
            out_ref[40 * (NEAR * v + r) : 40 * (NEAR * v + r + 1), :] = part


def pull_kernel(parts_ref, attr_ref, out_ref, wide_ref, res_ref, all_ref):
    for v in range(VIEWS):
        start = 40 * NEAR * v
        total = parts_ref[start : start + 36, :]
        for r in range(1, NEAR):
            total = total + parts_ref[start + 40 * r : start + 40 * r + 36, :]
        all_ref[40 * v : 40 * v + 36, :] = total
        all_ref[40 * v + 36 : 40 * v + 40, :] = parts_ref[start + 36 : start + 40, :]
    spread_attributes(attr_ref, wide_ref)
    pos, logscale, quat, logit, sh = split_attributes(wide_ref)
    total = None
    opacity_grad = None
    for pair in range(VIEWS // 2):
        starts = (80 * pair, 80 * pair + 40)
        cot = [
            jnp.concatenate([all_ref[pl.ds(s + c, 4, stride=8), :] for s in starts], axis=0) for c in range(8)
        ]
        cot.append(jnp.concatenate([all_ref[s + 32 : s + 36, :] for s in starts], axis=0))
        cam = [
            jnp.concatenate(
                [jnp.broadcast_to(all_ref[s + 36 : s + 37, j : j + 1], (4, 128)) for s in starts], axis=0
            )
            for j in range(6)
        ]
        terms = camera_terms(cam[:3], cam[3:])
        _, pull = jax.vjp(lambda a, b, c, d: project(a, b, c, d, terms), pos, logscale, quat, sh)
        grads = jax.tree.leaves(pull(cot[:5] + cot[6:]))
        total = grads if total is None else [a + b for a, b in zip(total, grads)]
        opacity_grad = cot[5] if opacity_grad is None else opacity_grad + cot[5]
    grads = total[:10] + [opacity_grad / (1.0 + jnp.exp(logit))] + total[10:]
    for a in range(ATTR):
        res_ref[4 * a : 4 * a + 4, :] = grads[a][0:4] + grads[a][4:8]
    for j in range(4):
        out_ref[:, 128 * j : 128 * (j + 1)] = res_ref[pl.ds(j, ATTR, stride=4), :]


VMEM = pl.BlockSpec(memory_space=pltpu.VMEM)
SMEM = pl.BlockSpec(memory_space=pltpu.SMEM)
HBM = pl.BlockSpec(memory_space=pl.ANY)
MIB = 1024 * 1024


def call(kernel, outs, args, scratch=(), in_specs=None, limit=24):
    return pl.pallas_call(
        kernel,
        out_shape=[jax.ShapeDtypeStruct(s, d) for s, d in outs],
        in_specs=in_specs or [VMEM] * len(args),
        out_specs=[VMEM] * len(outs),
        scratch_shapes=list(scratch),
        compiler_params=pltpu.CompilerParams(vmem_limit_bytes=limit * MIB),
    )(*args)


def vmem(*shape, dtype=F32):
    return pltpu.VMEM(shape, dtype)


def route(first_tile, owner, local, attributes, camera):
    return call(
        route_kernel,
        [((PEERS, 128), F32), ((PEERS, 128), I32), ((8, TILES * SLOTS), I32), ((40, 128), F32)],
        (first_tile, owner, local, attributes, camera),
        [
            vmem(1, TILES * SLOTS, dtype=I32), vmem(TILES, SLOTS, dtype=I32), vmem(ATTR, G_DEV), vmem(1, 6),
            vmem(ATTR * 8, 128), pltpu.SemaphoreType.DMA((4,)),
        ],
        [SMEM] + [HBM] * 4,
        60,
    )


def serve(asked, rows, *kept):
    outs = [((5 * PEERS, 128), F32)] + [(k.shape, k.dtype) for k in kept]
    return call(serve_kernel, outs, (asked, rows, *kept))


def composite(got, place, inv, depth, cot):
    big = vmem(SLOTS * 8, 128)
    return call(
        composite_kernel,
        [((3, TILES, 256), F32), ((5 * PEERS, 128), F32)],
        (got, place, inv, depth, cot),
        [vmem(16, TILES * SLOTS), big, big, big, vmem(16, TILES * SLOTS)],
    )


def collect(back, asked, camera):
    return call(collect_kernel, [((VIEWS * NEAR * 40, 128), F32)], (back, asked, camera))[0]


def pull_back(parts, attributes):
    return call(
        pull_kernel,
        [((ATTR, G_DEV), F32)],
        (parts, attributes),
        [vmem(ATTR * 8, 128), vmem(ATTR * 4, 128), vmem(40 * VIEWS, 128)],
    )[0]


def exchange(x, axis, groups):
    return lax.all_to_all(x, axis, split_axis=0, concat_axis=0, tiled=True, axis_index_groups=groups)


ACROSS = [[8 * z + 2 * y + c for z in range(16) for c in range(2)] for y in range(NEAR)]
WITHIN = [[8 * z + 2 * y + c for y in range(NEAR)] for z in range(16) for c in range(2)]
VIEWS_WITHIN = [[OWNERS * v + d for v in range(VIEWS) for d in group] for group in WITHIN]


def per_device(attributes, camera, list_owner, list_local, term_depth, image_cot):
    owner = list_owner.reshape(1, -1)
    first_tile = (lax.axis_index("dev") * TILES).astype(I32).reshape(1)
    asked, inv, place, rows = route(first_tile, owner, list_local[0], attributes, camera)
    asked = exchange(asked.reshape(PEERS, 1, 128), "dev", ACROSS).reshape(PEERS, 128)
    rows = lax.all_gather(rows, "dev", axis_index_groups=WITHIN, tiled=True)
    sent, place, inv, depth, cot, camera = serve(asked, rows, place, inv, term_depth[0], image_cot[0], camera)
    got = exchange(sent.reshape(PEERS, 1, 640), "dev", ACROSS).reshape(5 * PEERS, 128)
    image, grads = composite(got, place, inv, depth, cot)
    back = exchange(grads.reshape(PEERS, 1, 640), "dev", ACROSS).reshape(5 * PEERS, 128)
    mine = collect(back, asked, camera)
    parts = exchange(mine.reshape(VIEWS * NEAR, 40, 128), ("view", "dev"), VIEWS_WITHIN)
    return image[None], pull_back(parts.reshape(VIEWS * NEAR * 40, 128), attributes)


def solution(mesh):
    in_specs = (
        P(None, "dev"),
        P("view", None),
        P("view", "dev", None, None),
        P("view", "dev", None),
        P("view", "dev", None),
        P("view", None, "dev", None),
    )
    out_specs = (P("view", None, "dev", None), P(None, "dev"))
    return jax.shard_map(
        per_device, mesh=mesh, in_specs=in_specs, out_specs=out_specs, check_vma=False
    )
```

```python
import jax
import jax.numpy as jnp
from jax import lax
from jax.experimental import pallas as pl
from jax.experimental.pallas import tpu as pltpu
from jax.sharding import PartitionSpec as P

TILE_COLS = 16
TILES = 4
SLOTS = 256
CAP = 16
OWNERS = 128
PEERS = 32
NEAR = 4
G_DEV = 512
ATTR = 59
VIEWS = 4
LOG2E = 1.4426950408889634

SH_C0 = 0.28209479177387814
SH_C1 = 0.4886025119029199
SH_C2 = (
    1.0925484305920792,
    -1.0925484305920792,
    0.31539156525252005,
    -1.0925484305920792,
    0.5462742152960396,
)
SH_C3 = (
    -0.5900435899266435,
    2.890611442640554,
    -0.4570457994644658,
    0.3731763325901154,
    -0.4570457994644658,
    1.445305721320277,
    -0.5900435899266435,
)
BLUR = 1e-05

F32 = jnp.float32
BF16 = jnp.bfloat16
I32 = jnp.int32


def camera_terms(angles, shift):
    cosx, sinx = jnp.cos(angles[0]), jnp.sin(angles[0])
    cosy, siny = jnp.cos(angles[1]), jnp.sin(angles[1])
    cosz, sinz = jnp.cos(angles[2]), jnp.sin(angles[2])
    yx = [
        [cosy, siny * sinx, siny * cosx],
        [None, cosx, -sinx],
        [-siny, cosy * sinx, cosy * cosx],
    ]
    rot = [
        [cosz * yx[0][0]] + [cosz * yx[0][j] - sinz * yx[1][j] for j in (1, 2)],
        [sinz * yx[0][0]] + [sinz * yx[0][j] + cosz * yx[1][j] for j in (1, 2)],
        yx[2],
    ]
    centre = [-(rot[0][j] * shift[0] + rot[1][j] * shift[1] + rot[2][j] * shift[2]) for j in range(3)]
    return rot, shift, centre


def harmonics(dirx, diry, dirz):
    xx, yy, zz = (dirx * dirx, diry * diry, dirz * dirz)
    return [
        -SH_C1 * diry,
        SH_C1 * dirz,
        -SH_C1 * dirx,
        SH_C2[0] * dirx * diry,
        SH_C2[1] * diry * dirz,
        SH_C2[2] * (2.0 * zz - xx - yy),
        SH_C2[3] * dirx * dirz,
        SH_C2[4] * (xx - yy),
        SH_C3[0] * diry * (3.0 * xx - yy),
        SH_C3[1] * dirx * diry * dirz,
        SH_C3[2] * diry * (4.0 * zz - xx - yy),
        SH_C3[3] * dirz * (2.0 * zz - 3.0 * xx - 3.0 * yy),
        SH_C3[4] * dirx * (4.0 * zz - xx - yy),
        SH_C3[5] * dirz * (xx - yy),
        SH_C3[6] * dirx * (xx - 3.0 * yy),
    ]


def project(pos, logscale, quat, sh, cam):
    rot, shift, centre = cam
    cpos = [rot[i][0] * pos[0] + rot[i][1] * pos[1] + rot[i][2] * pos[2] + shift[i] for i in range(3)]
    inverse = 1.0 / cpos[2]
    u, w = cpos[0] * inverse, cpos[1] * inverse
    tmat = [
        [inverse * (rot[0][j] - u * rot[2][j]) for j in range(3)],
        [inverse * (rot[1][j] - w * rot[2][j]) for j in range(3)],
    ]
    scale = [jnp.exp(s) for s in logscale]
    norm = lax.rsqrt(quat[0] * quat[0] + quat[1] * quat[1] + quat[2] * quat[2] + quat[3] * quat[3])
    qw, qa, qb, qc = [q * norm for q in quat]
    rgau = [
        [1 - 2 * (qb * qb + qc * qc), 2 * (qa * qb - qw * qc), 2 * (qa * qc + qw * qb)],
        [2 * (qa * qb + qw * qc), 1 - 2 * (qa * qa + qc * qc), 2 * (qb * qc - qw * qa)],
        [2 * (qa * qc - qw * qb), 2 * (qb * qc + qw * qa), 1 - 2 * (qa * qa + qb * qb)],
    ]
    trs = [
        [(tmat[r][0] * rgau[0][k] + tmat[r][1] * rgau[1][k] + tmat[r][2] * rgau[2][k]) * scale[k] for k in range(3)]
        for r in range(2)
    ]
    sig_a = trs[0][0] * trs[0][0] + trs[0][1] * trs[0][1] + trs[0][2] * trs[0][2] + BLUR
    sig_b = trs[0][0] * trs[1][0] + trs[0][1] * trs[1][1] + trs[0][2] * trs[1][2]
    sig_c = trs[1][0] * trs[1][0] + trs[1][1] * trs[1][1] + trs[1][2] * trs[1][2] + BLUR
    det_inv = 1.0 / (sig_a * sig_c - sig_b * sig_b)
    dirs = [pos[j] - centre[j] for j in range(3)]
    norm_inv = lax.rsqrt(dirs[0] * dirs[0] + dirs[1] * dirs[1] + dirs[2] * dirs[2])
    basis = harmonics(dirs[0] * norm_inv, dirs[1] * norm_inv, dirs[2] * norm_inv)
    colors = []
    for ch in range(3):
        color = 0.5 + SH_C0 * sh[ch]
        for k in range(1, 16):
            color = color + basis[k - 1] * sh[3 * k + ch]
        colors.append(color)
    return [u, w, sig_c * det_inv, -sig_b * det_inv, sig_a * det_inv] + colors


def spread_attributes(attr_ref, wide_ref):
    for j in range(4):
        part = attr_ref[:, 128 * j : 128 * (j + 1)]
        wide_ref[pl.ds(j, ATTR, stride=8), :] = part
        wide_ref[pl.ds(j + 4, ATTR, stride=8), :] = part


def split_attributes(wide_ref):
    attrs = [wide_ref[8 * a : 8 * (a + 1), :] for a in range(ATTR)]
    return attrs[0:3], attrs[3:6], attrs[6:10], attrs[10], attrs[11:]


def dot(a, b, ca, cb):
    return lax.dot_general(a, b, (((ca,), (cb,)), ((), ())), preferred_element_type=F32)


def lane_gather(x, idx):
    return jnp.take_along_axis(x, idx, axis=1, mode="promise_in_bounds")


def split2(x):
    hi = x.astype(BF16)
    return hi, (x - hi.astype(F32)).astype(BF16)


def split3(x):
    hi = x.astype(BF16)
    rest = x - hi.astype(F32)
    mid = rest.astype(BF16)
    return hi, mid, (rest - mid.astype(F32)).astype(BF16)


def route_kernel(
    tile_ref, owner_hbm, local_hbm, attr_hbm, cam_hbm, depth_hbm, cot_hbm,
    asked_ref, inv_ref, place_ref, rows_ref, kept_ref,
    owner_ref, local_ref, attr_ref, cam_ref, depth_ref, cot_ref, wide_ref, sem,
):
    pairs = [
        (owner_hbm, owner_ref), (local_hbm, local_ref), (attr_hbm, attr_ref), (cam_hbm, cam_ref),
        (depth_hbm, depth_ref), (cot_hbm, cot_ref),
    ]
    copies = [pltpu.make_async_copy(src, dst, sem.at[n]) for n, (src, dst) in enumerate(pairs)]
    for copy in copies:
        copy.start()
    before = (
        lax.broadcasted_iota(I32, (SLOTS, SLOTS), 0) < lax.broadcasted_iota(I32, (SLOTS, SLOTS), 1)
    ).astype(F32).astype(BF16)
    every = jnp.ones((SLOTS, SLOTS), BF16)
    oid = lax.broadcasted_iota(I32, (OWNERS, SLOTS), 0)
    pid = lax.broadcasted_iota(I32, (PEERS, SLOTS), 0)
    lane = lax.broadcasted_iota(I32, (1, SLOTS), 1)
    base = jnp.zeros((OWNERS, SLOTS), F32)
    table = jnp.zeros((4 * PEERS, 128), F32)
    for copy in copies:
        copy.wait()
    for t in range(TILES):
        owner = owner_ref[:, SLOTS * t : SLOTS * (t + 1)]
        hot = (oid == owner).astype(F32)
        hot16 = hot.astype(BF16)
        count = dot(hot16, before, 1, 0) + base
        base = base + dot(hot16, every, 1, 0)
        rank = jnp.sum(hot * count, axis=0, keepdims=True).astype(I32)
        peer = (owner >> 3) * 2 + (owner & 1)
        lanes = ((owner >> 1) & 3) * CAP + rank
        place_ref[0:1, SLOTS * t : SLOTS * (t + 1)] = peer
        place_ref[1:2, SLOTS * t : SLOTS * (t + 1)] = lanes
        hot_peer = (pid == peer).astype(F32)
        hot_lane = ((oid & 63) == lanes).astype(F32).astype(BF16)
        local = local_ref[t : t + 1, :]
        slot = lane + (SLOTS * t + 1)
        parts = [local & 255, local >> 8, slot & 255, slot >> 8]
        vals = jnp.concatenate([hot_peer * p.astype(F32) for p in parts], axis=0).astype(BF16)
        table = table + dot(vals, hot_lane, 1, 1)
    place_ref[2:3, :] = jnp.full((1, TILES * SLOTS), tile_ref[0], I32)
    n = PEERS
    asked_ref[...] = table[0:n] + 256.0 * table[n : 2 * n]
    inv_ref[...] = (table[2 * n : 3 * n] + 256.0 * table[3 * n :]).astype(I32)
    for c in range(3):
        kept_ref[4 * c : 4 * c + 4, :] = cot_ref[c]
    kept_ref[12:16, :] = jnp.zeros((4, SLOTS), F32)
    kept_ref[12:13, 0:6] = cam_ref[...]
    for t in range(TILES):
        place_ref[3:4, SLOTS * t : SLOTS * (t + 1)] = depth_ref[t : t + 1, :]
    spread_attributes(attr_ref, wide_ref)
    pos, logscale, quat, logit, sh = split_attributes(wide_ref)
    cam = [jnp.broadcast_to(cam_ref[:, j : j + 1], (8, 128)) for j in range(6)]
    rows = project(pos, logscale, quat, sh, camera_terms(cam[:3], cam[3:]))
    log_opacity = -LOG2E * jnp.log(1.0 + jnp.exp(-logit))
    rows = rows[:5] + [log_opacity] + rows[5:]
    for c in range(8):
        rows_ref[pl.ds(c, 4, stride=8), :] = rows[c][0:4]
    rows_ref[32:36, :] = rows[8][0:4]
    rows_ref[36:40, :] = jnp.zeros((4, 128), F32)


def serve_kernel(asked_ref, rows_ref, *refs):
    kept, (out_ref, *outs) = refs[:3], refs[3:]
    for src, dst in zip(kept, outs):
        dst[...] = src[...]
    blank = jnp.zeros((4, 128), F32)
    table = []
    for j in range(4):
        part = [rows_ref[40 * r + 8 * j : 40 * r + 8 * j + 8, :] for r in range(NEAR)]
        part += [rows_ref[pl.ds(32 + j, NEAR, stride=40), :], blank]
        table.append(jnp.concatenate(part, axis=0))
    table = [x.astype(F32) for x in split3(jnp.concatenate(table, axis=1))]
    table = jnp.concatenate(table + [jnp.zeros((8, G_DEV), F32)], axis=0).astype(BF16)
    lid = lax.broadcasted_iota(I32, (G_DEV, 256), 0)
    sub = lax.broadcasted_iota(I32, (8, 128), 0)
    lane = lax.broadcasted_iota(I32, (8, 128), 1)
    near, left = (lane & 63) >> 4, lane < 64
    for n in range(0, PEERS, 4):
        hot = (lid == pair_ids(asked_ref, n)).astype(F32).astype(BF16)
        got = dot(table, hot, 1, 0)
        got = got[0:40] + got[40:80] + got[80:120]
        for i in range(2):
            half = got[:, 128 * i : 128 * (i + 1)]
            main = half[0:8]
            for r in range(1, NEAR):
                main = jnp.where(near == r, half[8 * r : 8 * (r + 1)], main)
            turned = pltpu.roll(main, 64, 1)
            last = jnp.sum(jnp.where(near == sub, half[32:40], 0.0), axis=0, keepdims=True)
            at = 5 * (n + 2 * i)
            out_ref[at : at + 4, :] = jnp.where(left[0:4], main[0:4], turned[4:8])
            out_ref[at + 4 : at + 5, :] = last
            out_ref[at + 5 : at + 9, :] = jnp.where(left[0:4], turned[0:4], main[4:8])
            out_ref[at + 9 : at + 10, :] = pltpu.roll(jnp.broadcast_to(last, (8, 128)), 64, 1)[0:1]


def pair_ids(asked_ref, n):
    left = lax.broadcasted_iota(I32, (1, 128), 1) < 64
    rows = [asked_ref[n + i : n + i + 1, :] for i in range(4)]
    pairs = [jnp.where(left, rows[0], rows[1]), jnp.where(left, rows[2], rows[3])]
    return jnp.concatenate(pairs, axis=1).astype(I32)


def composite_kernel(
    got_ref, place_ref, inv_ref, kept_ref, image_ref, out_ref,
    par_ref, alpha_ref, pull_ref, weight_ref, grad_ref,
):
    last = got_ref[pl.ds(4, PEERS, stride=5), :]
    sub = lax.broadcasted_iota(I32, (8, 128), 0)
    tables = []
    for n in range(PEERS):
        rows = got_ref[5 * n : 5 * n + 4, :]
        tables.append(jnp.concatenate([rows, rows], axis=0))
    for b in range(8):
        peer = jnp.broadcast_to(place_ref[0:1, 128 * b : 128 * (b + 1)], (8, 128))
        lanes = jnp.broadcast_to(place_ref[1:2, 128 * b : 128 * (b + 1)], (8, 128))
        both = jnp.where(sub < 4, lanes, lanes + 64)
        got = lane_gather(tables[0], both)
        for n in range(1, PEERS):
            got = jnp.where(peer == n, lane_gather(tables[n], both), got)
        par_ref[0:8, 128 * b : 128 * (b + 1)] = got
        final = jnp.zeros((8, 128), F32)
        for n in range(0, PEERS, 8):
            final = final + jnp.where(peer == sub + n, lane_gather(last[n : n + 8], lanes), 0.0)
        par_ref[8:9, 128 * b : 128 * (b + 1)] = jnp.sum(final, axis=0, keepdims=True)

    q = lax.broadcasted_iota(I32, (16, 128), 1)
    row16 = lax.broadcasted_iota(I32, (16, 128), 0)
    X = (q & 15).astype(F32) - 7.5
    Y = (q >> 4).astype(F32) - 3.5
    mono = jnp.where(row16 == 0, 1.0, 0.0)
    for n, m in enumerate([X, Y, X * X, X * Y, Y * Y]):
        mono = jnp.where(row16 == n + 1, m, mono)
    mono8 = mono[0:8]
    mono16 = mono.astype(BF16)
    mono_twice = jnp.concatenate([mono16, mono16], axis=1)
    ex, ey = 1.0 / (16.0 * TILE_COLS), 1.0 / (16.0 * (TILES * OWNERS // TILE_COLS))

    zero = jnp.zeros((1, SLOTS), F32)
    zero5 = jnp.zeros((5, SLOTS), F32)
    blank = jnp.zeros((8, 128), F32)
    cots = []
    geometry = []
    for t in range(TILES):
        par = [par_ref[c : c + 1, SLOTS * t : SLOTS * (t + 1)] for c in range(9)]
        u, w, ca, cb, cc, log_op = par[:6]
        tile = place_ref[2:3, 0:SLOTS] + t
        cx = ((tile & (TILE_COLS - 1)) * 16 + 8).astype(F32) * ex - 0.5
        dx0 = cx - u
        A, B, C = -0.5 * LOG2E * ca, -LOG2E * cb, -0.5 * LOG2E * cc
        colors = jnp.concatenate([par[6], par[7], par[8], zero5], axis=0)
        chi, cmid, clo = [c.astype(F32) for c in split3(colors)]
        dy0s = []
        coefs, pulls = [], []
        for h in range(2):
            cy = ((tile >> 4) * 16 + 8 * h + 4).astype(F32) * ey - 0.5
            dy0 = cy - w
            dy0s.append(dy0)
            coef = [
                (A * dx0 + B * dy0) * dx0 + C * dy0 * dy0 + log_op,
                (2.0 * A * dx0 + B * dy0) * ex,
                (B * dx0 + 2.0 * C * dy0) * ey,
                A * (ex * ex),
                B * (ex * ey),
                C * (ey * ey),
                zero,
                zero,
            ]
            coefs += [k.astype(F32) for k in split3(jnp.concatenate(coef, axis=0))]
            g = [kept_ref[4 * c + t : 4 * c + t + 1, 128 * h : 128 * (h + 1)] for c in range(3)]
            ghi, gmid, glo = [x.astype(F32) for x in split3(jnp.concatenate(g + [blank[0:5]], axis=0))]
            cots.append((4 * h + t, ghi, gmid))
            pulls.append([ghi, gmid, glo, ghi, gmid, ghi])
        left = coefs + [chi, chi, chi, cmid, cmid, clo] + [jnp.zeros((32, SLOTS), F32)]
        left = jnp.transpose(jnp.concatenate(left, axis=0)).astype(BF16)
        right = []
        for h in range(2):
            right.append([blank] * (3 * h) + [mono8] * 3 + [blank] * (13 - 3 * h))
            right.append([blank] * 6 + pulls[h] + [blank] * 4)
        right = jnp.concatenate([jnp.concatenate(r, axis=0) for r in right], axis=1).astype(BF16)
        both = dot(left, right, 1, 0)
        for h in range(2):
            at = pl.ds(4 * h + t, SLOTS, stride=8)
            alpha_ref[at, :] = both[:, 256 * h : 256 * h + 128]
            pull_ref[at, :] = both[:, 256 * h + 128 : 256 * h + 256]
        geometry.append((ca, cb, cc, dx0, dy0s, chi, cmid))

    depth = jnp.concatenate(
        [place_ref[3:4, SLOTS * t + 128 * h : SLOTS * t + 128 * (h + 1)] for h in range(2) for t in range(TILES)], axis=0
    )
    segments, unroll = 4, 4
    length = SLOTS // segments

    def forward(j, state):
        trans, behind = list(state[0]), list(state[1])
        for i in range(unroll):
            for n in range(segments):
                s = n * length + j * unroll + i
                at = pl.ds(pl.multiple_of(s * 8, 8), 8)
                alpha = jnp.where(s < depth, jnp.exp2(alpha_ref[at, :]), 0.0)
                weight = trans[n] * alpha
                alpha_ref[at, :] = alpha
                weight_ref[at, :] = weight
                trans[n] = trans[n] - weight
                behind[n] = behind[n] + weight * pull_ref[at, :]
        return tuple(trans), tuple(behind)

    ones, zeros = jnp.ones((8, 128), F32), jnp.zeros((8, 128), F32)
    trans, behind = lax.fori_loop(0, length // unroll, forward, ((ones,) * segments, (zeros,) * segments))
    starts, rest = [ones], [zeros]
    for n in range(1, segments):
        starts.append(starts[-1] * trans[n - 1])
        rest.insert(0, behind[segments - n] + trans[segments - n] * rest[0])

    def backward(j, rest):
        rest = list(rest)
        for i in range(unroll):
            for n in range(segments):
                s = (n + 1) * length - 1 - (j * unroll + i)
                at = pl.ds(pl.multiple_of(s * 8, 8), 8)
                more = pull_ref[at, :] - rest[n]
                rest[n] = rest[n] + alpha_ref[at, :] * more
                weight = starts[n] * weight_ref[at, :]
                weight_ref[at, :] = weight
                pull_ref[at, :] = weight * more
        return tuple(rest)

    lax.fori_loop(0, length // unroll, backward, tuple(rest))

    cots = {th: (ghi, gmid) for th, ghi, gmid in cots}
    for t in range(TILES):
        ca, cb, cc, dx0, dy0s, chi, cmid = geometry[t]
        color_rows = jnp.concatenate([chi, cmid], axis=0).astype(BF16)
        total = [jnp.zeros((1, SLOTS), F32) for _ in range(6)]
        dcolor = jnp.zeros((3, SLOTS), F32)
        for h in range(2):
            th = 4 * h + t
            dy0 = dy0s[h]
            whi, wlo = split2(weight_ref[pl.ds(th, SLOTS, stride=8), :])
            weights = jnp.concatenate([whi, wlo], axis=1)
            ghi, glo = split2(pull_ref[pl.ds(th, SLOTS, stride=8), :])
            grads = jnp.concatenate([ghi, glo], axis=1)
            seen = dot(color_rows, weights, 1, 0)
            seen = seen[:, :128] + seen[:, 128:]
            seen = seen[0:8] + seen[8:16]
            for c in range(3):
                image_ref[c, t : t + 1, 128 * h : 128 * (h + 1)] = seen[c : c + 1]
            cot = jnp.concatenate(cots[th], axis=0).astype(BF16)
            dcol = dot(jnp.concatenate([cot, cot], axis=1), weights, 1, 1)
            dcolor = dcolor + dcol[0:3] + dcol[8:11]
            mom = dot(mono_twice, grads, 1, 1)
            m0 = mom[0:1]
            mx, my = ex * mom[1:2], ey * mom[2:3]
            total[0] = total[0] + m0
            total[1] = total[1] + dx0 * m0 + mx
            total[2] = total[2] + dy0 * m0 + my
            total[3] = total[3] + dx0 * (dx0 * m0 + 2.0 * mx) + (ex * ex) * mom[3:4]
            total[4] = total[4] + dx0 * (dy0 * m0 + my) + dy0 * mx + (ex * ey) * mom[4:5]
            total[5] = total[5] + dy0 * (dy0 * m0 + 2.0 * my) + (ey * ey) * mom[5:6]
        s0, sx, sy, sxx, sxy, syy = total
        made = [ca * sx + cb * sy, cb * sx + cc * sy, -0.5 * sxx, -sxy, -0.5 * syy, s0, dcolor]
        grad_ref[0:9, SLOTS * t : SLOTS * (t + 1)] = jnp.concatenate(made, axis=0)

    inv = inv_ref[...]

    def pick(tables, idx):
        at = jnp.maximum(idx - 1, 0)
        low, high = at & 127, at >> 7
        got = lane_gather(tables[0], low)
        for j in range(1, 8):
            got = jnp.where(high == j, lane_gather(tables[j], low), got)
        return jnp.where(idx > 0, got, 0.0)

    tables = [grad_ref[0:8, 128 * j : 128 * (j + 1)] for j in range(8)]
    last = [jnp.broadcast_to(grad_ref[8:9, 128 * j : 128 * (j + 1)], (8, 128)) for j in range(8)]
    left = lax.broadcasted_iota(I32, (4, 128), 1) < 64
    for n in range(PEERS):
        got = pick(tables, jnp.broadcast_to(inv[n : n + 1], (8, 128)))
        out_ref[5 * n : 5 * n + 4, :] = jnp.where(left, got[0:4], got[4:8])
    more = [pick(last, inv[n : n + 8]) for n in range(0, PEERS, 8)]
    out_ref[pl.ds(4, PEERS, stride=5), :] = jnp.concatenate(more, axis=0)


def collect_kernel(back_ref, asked_ref, kept_ref, out_ref):
    lid = lax.broadcasted_iota(I32, (G_DEV, 256), 0)
    sub = lax.broadcasted_iota(I32, (8, 128), 0)
    lane = lax.broadcasted_iota(I32, (8, 128), 1)
    near, left = (lane & 63) >> 4, lane < 64
    acc = jnp.zeros((80, G_DEV), F32)
    for n in range(0, PEERS, 4):
        hot = (lid == pair_ids(asked_ref, n)).astype(F32).astype(BF16)
        pairs = []
        for i in range(2):
            at = 5 * (n + 2 * i)
            one = jnp.concatenate([back_ref[at : at + 4, :]] * 2, axis=0)
            two = jnp.concatenate([back_ref[at + 5 : at + 9, :]] * 2, axis=0)
            other = jnp.where(left, pltpu.roll(one, 64, 1), two)
            straight = jnp.where(left, one, pltpu.roll(two, 64, 1))
            main = jnp.where(sub < 4, straight, other)
            last_one = jnp.broadcast_to(back_ref[at + 4 : at + 5, :], (8, 128))
            last_two = jnp.broadcast_to(back_ref[at + 9 : at + 10, :], (8, 128))
            last = jnp.where(left, last_one, pltpu.roll(last_two, 64, 1))
            rows = []
            for m, l in zip(split2(main), split2(last)):
                m, l = m.astype(F32), l.astype(F32)
                rows += [jnp.where(near == r, m, 0.0) for r in range(NEAR)] + [jnp.where(near == sub, l, 0.0)]
            pairs.append(jnp.concatenate(rows, axis=0).astype(BF16))
        acc = acc + dot(jnp.concatenate(pairs, axis=1), hot, 1, 1)
    rows = acc[0:40] + acc[40:80]
    tail = kept_ref[12:16, 0:128]
    for r in range(NEAR):
        part = [rows[8 * r : 8 * r + 8, 128 * j : 128 * (j + 1)] for j in range(4)]
        part += [rows[32 + r : 33 + r, 128 * j : 128 * (j + 1)] for j in range(4)] + [tail]
        part = jnp.concatenate(part, axis=0)
        for v in range(VIEWS):
            out_ref[40 * (NEAR * v + r) : 40 * (NEAR * v + r + 1), :] = part


def pull_kernel(parts_ref, attr_ref, image_in_ref, out_ref, image_ref, wide_ref, res_ref, all_ref):
    image_ref[...] = image_in_ref[...]
    for v in range(VIEWS):
        start = 40 * NEAR * v
        total = parts_ref[start : start + 36, :]
        for r in range(1, NEAR):
            total = total + parts_ref[start + 40 * r : start + 40 * r + 36, :]
        all_ref[40 * v : 40 * v + 36, :] = total
        all_ref[40 * v + 36 : 40 * v + 40, :] = parts_ref[start + 36 : start + 40, :]
    spread_attributes(attr_ref, wide_ref)
    pos, logscale, quat, logit, sh = split_attributes(wide_ref)
    total = None
    opacity_grad = None
    for pair in range(VIEWS // 2):
        starts = (80 * pair, 80 * pair + 40)
        cot = [
            jnp.concatenate([all_ref[pl.ds(s + c, 4, stride=8), :] for s in starts], axis=0) for c in range(8)
        ]
        cot.append(jnp.concatenate([all_ref[s + 32 : s + 36, :] for s in starts], axis=0))
        cam = [
            jnp.concatenate(
                [jnp.broadcast_to(all_ref[s + 36 : s + 37, j : j + 1], (4, 128)) for s in starts], axis=0
            )
            for j in range(6)
        ]
        terms = camera_terms(cam[:3], cam[3:])
        _, pull = jax.vjp(lambda a, b, c, d: project(a, b, c, d, terms), pos, logscale, quat, sh)
        grads = jax.tree.leaves(pull(cot[:5] + cot[6:]))
        total = grads if total is None else [a + b for a, b in zip(total, grads)]
        opacity_grad = cot[5] if opacity_grad is None else opacity_grad + cot[5]
    grads = total[:10] + [opacity_grad / (1.0 + jnp.exp(logit))] + total[10:]
    for a in range(ATTR):
        res_ref[4 * a : 4 * a + 4, :] = grads[a][0:4] + grads[a][4:8]
    for j in range(4):
        out_ref[:, 128 * j : 128 * (j + 1)] = res_ref[pl.ds(j, ATTR, stride=4), :]


VMEM = pl.BlockSpec(memory_space=pltpu.VMEM)
SMEM = pl.BlockSpec(memory_space=pltpu.SMEM)
HBM = pl.BlockSpec(memory_space=pl.ANY)
MIB = 1024 * 1024


def call(kernel, outs, args, scratch=(), in_specs=None, limit=24):
    return pl.pallas_call(
        kernel,
        out_shape=[jax.ShapeDtypeStruct(s, d) for s, d in outs],
        in_specs=in_specs or [VMEM] * len(args),
        out_specs=[VMEM] * len(outs),
        scratch_shapes=list(scratch),
        compiler_params=pltpu.CompilerParams(vmem_limit_bytes=limit * MIB),
    )(*args)


def vmem(*shape, dtype=F32):
    return pltpu.VMEM(shape, dtype)


def route(first_tile, owner, local, attributes, camera, depth, cot):
    return call(
        route_kernel,
        [
            ((PEERS, 128), F32), ((PEERS, 128), I32), ((8, TILES * SLOTS), I32), ((40, 128), F32), ((16, SLOTS), F32),
        ],
        (first_tile, owner, local, attributes, camera, depth, cot),
        [
            vmem(1, TILES * SLOTS, dtype=I32), vmem(TILES, SLOTS, dtype=I32), vmem(ATTR, G_DEV), vmem(1, 6),
            vmem(TILES, SLOTS, dtype=I32), vmem(3, TILES, SLOTS), vmem(ATTR * 8, 128), pltpu.SemaphoreType.DMA((6,)),
        ],
        [SMEM] + [HBM] * 6,
        60,
    )


def serve(asked, rows, *kept):
    outs = [((5 * PEERS, 128), F32)] + [(k.shape, k.dtype) for k in kept]
    return call(serve_kernel, outs, (asked, rows, *kept))


def composite(got, place, inv, kept):
    big = vmem(SLOTS * 8, 128)
    return call(
        composite_kernel,
        [((3, TILES, 256), F32), ((5 * PEERS, 128), F32)],
        (got, place, inv, kept),
        [vmem(16, TILES * SLOTS), big, big, big, vmem(16, TILES * SLOTS)],
    )


def collect(back, asked, kept):
    return call(collect_kernel, [((VIEWS * NEAR * 40, 128), F32)], (back, asked, kept))[0]


def pull_back(parts, attributes, image):
    return call(
        pull_kernel,
        [((ATTR, G_DEV), F32), (image.shape, F32)],
        (parts, attributes, image),
        [vmem(ATTR * 8, 128), vmem(ATTR * 4, 128), vmem(40 * VIEWS, 128)],
    )


def exchange(x, axis, groups):
    return lax.all_to_all(x, axis, split_axis=0, concat_axis=0, tiled=True, axis_index_groups=groups)


ACROSS = [[8 * z + 2 * y + c for z in range(16) for c in range(2)] for y in range(NEAR)]
WITHIN = [[8 * z + 2 * y + c for y in range(NEAR)] for z in range(16) for c in range(2)]
VIEWS_WITHIN = [[OWNERS * v + d for v in range(VIEWS) for d in group] for group in WITHIN]


def per_device(attributes, camera, list_owner, list_local, term_depth, image_cot):
    owner = list_owner.reshape(1, -1)
    first_tile = (lax.axis_index("dev") * TILES).astype(I32).reshape(1)
    asked, inv, place, rows, kept = route(
        first_tile, owner, list_local[0], attributes, camera, term_depth[0], image_cot[0]
    )
    asked = exchange(asked.reshape(PEERS, 1, 128), "dev", ACROSS).reshape(PEERS, 128)
    rows = lax.all_gather(rows, "dev", axis_index_groups=WITHIN, tiled=True)
    sent, place, inv, kept = serve(asked, rows, place, inv, kept)
    got = exchange(sent.reshape(PEERS, 1, 640), "dev", ACROSS).reshape(5 * PEERS, 128)
    image, grads = composite(got, place, inv, kept)
    back = exchange(grads.reshape(PEERS, 1, 640), "dev", ACROSS).reshape(5 * PEERS, 128)
    mine = collect(back, asked, kept)
    parts = exchange(mine.reshape(VIEWS * NEAR, 40, 128), ("view", "dev"), VIEWS_WITHIN)
    grad, image = pull_back(parts.reshape(VIEWS * NEAR * 40, 128), attributes, image)
    return image[None], grad


def solution(mesh):
    in_specs = (
        P(None, "dev"),
        P("view", None),
        P("view", "dev", None, None),
        P("view", "dev", None),
        P("view", "dev", None),
        P("view", None, "dev", None),
    )
    out_specs = (P("view", None, "dev", None), P(None, "dev"))
    return jax.shard_map(
        per_device, mesh=mesh, in_specs=in_specs, out_specs=out_specs, check_vma=False
    )
```

```python
import jax
import jax.numpy as jnp
from jax import lax
from jax.experimental import pallas as pl
from jax.experimental.pallas import tpu as pltpu
from jax.sharding import PartitionSpec as P

TILE_COLS = 16
TILES = 4
SLOTS = 256
CAP = 16
OWNERS = 128
PEERS = 32
NEAR = 4
PLANES = 16
RANKS = 8
G_DEV = 512
ATTR = 59
VIEWS = 4
LOG2E = 1.4426950408889634

SH_C0 = 0.28209479177387814
SH_C1 = 0.4886025119029199
SH_C2 = (
    1.0925484305920792,
    -1.0925484305920792,
    0.31539156525252005,
    -1.0925484305920792,
    0.5462742152960396,
)
SH_C3 = (
    -0.5900435899266435,
    2.890611442640554,
    -0.4570457994644658,
    0.3731763325901154,
    -0.4570457994644658,
    1.445305721320277,
    -0.5900435899266435,
)
BLUR = 1e-05

F32 = jnp.float32
BF16 = jnp.bfloat16
I32 = jnp.int32


def camera_terms(angles, shift):
    cosx, sinx = jnp.cos(angles[0]), jnp.sin(angles[0])
    cosy, siny = jnp.cos(angles[1]), jnp.sin(angles[1])
    cosz, sinz = jnp.cos(angles[2]), jnp.sin(angles[2])
    yx = [
        [cosy, siny * sinx, siny * cosx],
        [None, cosx, -sinx],
        [-siny, cosy * sinx, cosy * cosx],
    ]
    rot = [
        [cosz * yx[0][0]] + [cosz * yx[0][j] - sinz * yx[1][j] for j in (1, 2)],
        [sinz * yx[0][0]] + [sinz * yx[0][j] + cosz * yx[1][j] for j in (1, 2)],
        yx[2],
    ]
    centre = [-(rot[0][j] * shift[0] + rot[1][j] * shift[1] + rot[2][j] * shift[2]) for j in range(3)]
    return rot, shift, centre


def harmonics(dirx, diry, dirz):
    xx, yy, zz = (dirx * dirx, diry * diry, dirz * dirz)
    return [
        -SH_C1 * diry,
        SH_C1 * dirz,
        -SH_C1 * dirx,
        SH_C2[0] * dirx * diry,
        SH_C2[1] * diry * dirz,
        SH_C2[2] * (2.0 * zz - xx - yy),
        SH_C2[3] * dirx * dirz,
        SH_C2[4] * (xx - yy),
        SH_C3[0] * diry * (3.0 * xx - yy),
        SH_C3[1] * dirx * diry * dirz,
        SH_C3[2] * diry * (4.0 * zz - xx - yy),
        SH_C3[3] * dirz * (2.0 * zz - 3.0 * xx - 3.0 * yy),
        SH_C3[4] * dirx * (4.0 * zz - xx - yy),
        SH_C3[5] * dirz * (xx - yy),
        SH_C3[6] * dirx * (xx - 3.0 * yy),
    ]


def project(pos, logscale, quat, sh, cam):
    rot, shift, centre = cam
    cpos = [rot[i][0] * pos[0] + rot[i][1] * pos[1] + rot[i][2] * pos[2] + shift[i] for i in range(3)]
    inverse = 1.0 / cpos[2]
    u, w = cpos[0] * inverse, cpos[1] * inverse
    tmat = [
        [inverse * (rot[0][j] - u * rot[2][j]) for j in range(3)],
        [inverse * (rot[1][j] - w * rot[2][j]) for j in range(3)],
    ]
    scale = [jnp.exp(s) for s in logscale]
    norm = lax.rsqrt(quat[0] * quat[0] + quat[1] * quat[1] + quat[2] * quat[2] + quat[3] * quat[3])
    qw, qa, qb, qc = [q * norm for q in quat]
    rgau = [
        [1 - 2 * (qb * qb + qc * qc), 2 * (qa * qb - qw * qc), 2 * (qa * qc + qw * qb)],
        [2 * (qa * qb + qw * qc), 1 - 2 * (qa * qa + qc * qc), 2 * (qb * qc - qw * qa)],
        [2 * (qa * qc - qw * qb), 2 * (qb * qc + qw * qa), 1 - 2 * (qa * qa + qb * qb)],
    ]
    trs = [
        [(tmat[r][0] * rgau[0][k] + tmat[r][1] * rgau[1][k] + tmat[r][2] * rgau[2][k]) * scale[k] for k in range(3)]
        for r in range(2)
    ]
    sig_a = trs[0][0] * trs[0][0] + trs[0][1] * trs[0][1] + trs[0][2] * trs[0][2] + BLUR
    sig_b = trs[0][0] * trs[1][0] + trs[0][1] * trs[1][1] + trs[0][2] * trs[1][2]
    sig_c = trs[1][0] * trs[1][0] + trs[1][1] * trs[1][1] + trs[1][2] * trs[1][2] + BLUR
    det_inv = 1.0 / (sig_a * sig_c - sig_b * sig_b)
    dirs = [pos[j] - centre[j] for j in range(3)]
    norm_inv = lax.rsqrt(dirs[0] * dirs[0] + dirs[1] * dirs[1] + dirs[2] * dirs[2])
    basis = harmonics(dirs[0] * norm_inv, dirs[1] * norm_inv, dirs[2] * norm_inv)
    colors = []
    for ch in range(3):
        color = 0.5 + SH_C0 * sh[ch]
        for k in range(1, 16):
            color = color + basis[k - 1] * sh[3 * k + ch]
        colors.append(color)
    return [u, w, sig_c * det_inv, -sig_b * det_inv, sig_a * det_inv] + colors


def spread_attributes(attr_ref, wide_ref):
    for j in range(4):
        part = attr_ref[:, 128 * j : 128 * (j + 1)]
        wide_ref[pl.ds(j, ATTR, stride=8), :] = part
        wide_ref[pl.ds(j + 4, ATTR, stride=8), :] = part


def split_attributes(wide_ref):
    attrs = [wide_ref[8 * a : 8 * (a + 1), :] for a in range(ATTR)]
    return attrs[0:3], attrs[3:6], attrs[6:10], attrs[10], attrs[11:]


def dot(a, b, ca, cb):
    return lax.dot_general(a, b, (((ca,), (cb,)), ((), ())), preferred_element_type=F32)


def lane_gather(x, idx):
    return jnp.take_along_axis(x, idx, axis=1, mode="promise_in_bounds")


def split2(x):
    hi = x.astype(BF16)
    return hi, (x - hi.astype(F32)).astype(BF16)


def split3(x):
    hi = x.astype(BF16)
    rest = x - hi.astype(F32)
    mid = rest.astype(BF16)
    return hi, mid, (rest - mid.astype(F32)).astype(BF16)


def route_kernel(
    tile_ref, owner_hbm, local_hbm, attr_hbm, cam_hbm, depth_hbm, cot_hbm,
    asked_ref, inv_ref, place_ref, rows_ref, kept_ref, names_ref,
    owner_ref, local_ref, attr_ref, cam_ref, depth_ref, cot_ref, wide_ref, tmp_ref, sem,
):
    pairs = [
        (owner_hbm, owner_ref), (local_hbm, local_ref), (attr_hbm, attr_ref), (cam_hbm, cam_ref),
        (depth_hbm, depth_ref), (cot_hbm, cot_ref),
    ]
    copies = [pltpu.make_async_copy(src, dst, sem.at[n]) for n, (src, dst) in enumerate(pairs)]
    for copy in copies:
        copy.start()
    before = (
        lax.broadcasted_iota(I32, (SLOTS, SLOTS), 0) < lax.broadcasted_iota(I32, (SLOTS, SLOTS), 1)
    ).astype(F32).astype(BF16)
    every = jnp.ones((SLOTS, SLOTS), BF16)
    oid = lax.broadcasted_iota(I32, (OWNERS, SLOTS), 0)
    pid = lax.broadcasted_iota(I32, (PEERS, SLOTS), 0)
    lane = lax.broadcasted_iota(I32, (1, SLOTS), 1)
    base = jnp.zeros((OWNERS, SLOTS), F32)
    gid = lax.broadcasted_iota(I32, (2 * RANKS, SLOTS), 0)
    table = jnp.zeros((4 * PEERS, 128), F32)
    request = jnp.zeros((4 * RANKS, 128), F32)
    for copy in copies:
        copy.wait()
    for t in range(TILES):
        owner = owner_ref[:, SLOTS * t : SLOTS * (t + 1)]
        hot = (oid == owner).astype(F32)
        hot16 = hot.astype(BF16)
        count = dot(hot16, before, 1, 0) + base
        base = base + dot(hot16, every, 1, 0)
        rank = jnp.sum(hot * count, axis=0, keepdims=True).astype(I32)
        local = local_ref[t : t + 1, :]
        local_parts = [local & 255, local >> 8]
        slot = lane + (SLOTS * t + 1)
        group = (owner & 7) * 2 + (owner >> 6)
        lanes = ((owner >> 3) & 7) * CAP + rank
        place_ref[0:1, SLOTS * t : SLOTS * (t + 1)] = group
        place_ref[1:2, SLOTS * t : SLOTS * (t + 1)] = lanes
        hot_group = (gid == group).astype(F32)
        vals = jnp.concatenate([hot_group * p.astype(F32) for p in local_parts], axis=0).astype(BF16)
        request = request + dot(vals, (oid == lanes).astype(F32).astype(BF16), 1, 1)
        peer = (owner >> 3) * 2 + (owner & 1)
        lanes = ((owner >> 1) & 3) * CAP + rank
        hot_peer = (pid == peer).astype(F32)
        parts = local_parts + [slot & 255, slot >> 8]
        vals = jnp.concatenate([hot_peer * p.astype(F32) for p in parts], axis=0).astype(BF16)
        table = table + dot(vals, ((oid & 63) == lanes).astype(F32).astype(BF16), 1, 1)
    place_ref[2:3, :] = jnp.full((1, TILES * SLOTS), tile_ref[0], I32)
    n = PEERS
    asked_ref[...] = request[0 : 2 * RANKS] + 256.0 * request[2 * RANKS :]
    names_ref[...] = table[0:n] + 256.0 * table[n : 2 * n]
    inv_ref[...] = (table[2 * n : 3 * n] + 256.0 * table[3 * n :]).astype(I32)
    for c in range(3):
        kept_ref[4 * c : 4 * c + 4, :] = cot_ref[c]
    kept_ref[12:16, :] = jnp.zeros((4, SLOTS), F32)
    kept_ref[12:13, 0:6] = cam_ref[...]
    for t in range(TILES):
        place_ref[3:4, SLOTS * t : SLOTS * (t + 1)] = depth_ref[t : t + 1, :]
    spread_attributes(attr_ref, wide_ref)
    pos, logscale, quat, logit, sh = split_attributes(wide_ref)
    cam = [jnp.broadcast_to(cam_ref[:, j : j + 1], (8, 128)) for j in range(6)]
    rows = project(pos, logscale, quat, sh, camera_terms(cam[:3], cam[3:]))
    log_opacity = -LOG2E * jnp.log(1.0 + jnp.exp(-logit))
    rows = rows[:5] + [log_opacity] + rows[5:]
    for c in range(8):
        tmp_ref[pl.ds(c, 4, stride=8), :] = rows[c][0:4]
    tmp_ref[32:36, :] = rows[8][0:4]
    tmp_ref[36:40, :] = jnp.zeros((4, 128), F32)
    rows = tmp_ref[...]
    for z in range(PLANES):
        rows_ref[40 * z : 40 * (z + 1), :] = rows


def serve_kernel(tile_ref, asked_ref, rows_ref, *refs):
    kept, (out_ref, *outs) = refs[:4], refs[4:]
    for src, dst in zip(kept, outs):
        dst[...] = src[...]
    mine = 2 * ((tile_ref[0] // TILES) & (RANKS - 1))
    lid = lax.broadcasted_iota(I32, (G_DEV, 256), 0)
    sub = lax.broadcasted_iota(I32, (8, 128), 0)
    near = lax.broadcasted_iota(I32, (8, 128), 1) >> 4
    for half in range(2):
        start = 320 * half
        table = []
        for j in range(4):
            part = [rows_ref[start + 40 * r + 8 * j : start + 40 * r + 8 * j + 8, :] for r in range(8)]
            part.append(rows_ref[pl.ds(start + 32 + j, 8, stride=40), :])
            table.append(jnp.concatenate(part, axis=0))
        table = [x.astype(F32) for x in split3(jnp.concatenate(table, axis=1))]
        table = jnp.concatenate(table + [jnp.zeros((8, G_DEV), F32)], axis=0).astype(BF16)
        for r in range(0, RANKS, 2):
            ids = [asked_ref[pl.ds(16 * (r + i) + mine + half, 1), :] for i in range(2)]
            hot = (lid == jnp.concatenate(ids, axis=1).astype(I32)).astype(F32).astype(BF16)
            got = dot(table, hot, 1, 0)
            got = got[0:72] + got[72:144] + got[144:216]
            for i in range(2):
                part = got[:, 128 * i : 128 * (i + 1)]
                main = part[0:8]
                for n in range(1, 8):
                    main = jnp.where(near == n, part[8 * n : 8 * (n + 1)], main)
                at = 9 * (2 * (r + i) + half)
                out_ref[at : at + 8, :] = main
                last = jnp.sum(jnp.where(near == sub, part[64:72], 0.0), axis=0, keepdims=True)
                out_ref[at + 8 : at + 9, :] = last


def pair_ids(back_ref, n):
    left = lax.broadcasted_iota(I32, (8, 128), 1) < 64
    rows = [jnp.broadcast_to(back_ref[5 * (n + i) + 4 : 5 * (n + i) + 5, :], (8, 128)) for i in range(4)]
    pairs = [jnp.where(left, pltpu.roll(rows[i], 64, 1), rows[i + 1]) for i in (0, 2)]
    return jnp.concatenate(pairs, axis=1)[0:1].astype(I32)


def composite_kernel(
    got_ref, place_ref, inv_ref, kept_ref, names_ref, image_ref, out_ref,
    par_ref, alpha_ref, pull_ref, weight_ref, grad_ref,
):
    groups = 2 * RANKS
    last = got_ref[pl.ds(8, groups, stride=9), :]
    sub = lax.broadcasted_iota(I32, (8, 128), 0)
    for b in range(8):
        group = jnp.broadcast_to(place_ref[0:1, 128 * b : 128 * (b + 1)], (8, 128))
        lanes = jnp.broadcast_to(place_ref[1:2, 128 * b : 128 * (b + 1)], (8, 128))
        got = lane_gather(got_ref[0:8, :], lanes)
        for n in range(1, groups):
            got = jnp.where(group == n, lane_gather(got_ref[9 * n : 9 * n + 8, :], lanes), got)
        par_ref[0:8, 128 * b : 128 * (b + 1)] = got
        low = jnp.where(group == sub, lane_gather(last[0:8], lanes), 0.0)
        high = jnp.where(group == sub + 8, lane_gather(last[8:16], lanes), 0.0)
        par_ref[8:9, 128 * b : 128 * (b + 1)] = jnp.sum(low + high, axis=0, keepdims=True)

    q = lax.broadcasted_iota(I32, (16, 128), 1)
    row16 = lax.broadcasted_iota(I32, (16, 128), 0)
    X = (q & 15).astype(F32) - 7.5
    Y = (q >> 4).astype(F32) - 3.5
    mono = jnp.where(row16 == 0, 1.0, 0.0)
    for n, m in enumerate([X, Y, X * X, X * Y, Y * Y]):
        mono = jnp.where(row16 == n + 1, m, mono)
    mono8 = mono[0:8]
    mono16 = mono.astype(BF16)
    mono_twice = jnp.concatenate([mono16, mono16], axis=1)
    ex, ey = 1.0 / (16.0 * TILE_COLS), 1.0 / (16.0 * (TILES * OWNERS // TILE_COLS))

    zero = jnp.zeros((1, SLOTS), F32)
    zero5 = jnp.zeros((5, SLOTS), F32)
    blank = jnp.zeros((8, 128), F32)
    cots = []
    geometry = []
    for t in range(TILES):
        par = [par_ref[c : c + 1, SLOTS * t : SLOTS * (t + 1)] for c in range(9)]
        u, w, ca, cb, cc, log_op = par[:6]
        tile = place_ref[2:3, 0:SLOTS] + t
        cx = ((tile & (TILE_COLS - 1)) * 16 + 8).astype(F32) * ex - 0.5
        dx0 = cx - u
        A, B, C = -0.5 * LOG2E * ca, -LOG2E * cb, -0.5 * LOG2E * cc
        colors = jnp.concatenate([par[6], par[7], par[8], zero5], axis=0)
        chi, cmid, clo = [c.astype(F32) for c in split3(colors)]
        dy0s = []
        coefs, pulls = [], []
        for h in range(2):
            cy = ((tile >> 4) * 16 + 8 * h + 4).astype(F32) * ey - 0.5
            dy0 = cy - w
            dy0s.append(dy0)
            coef = [
                (A * dx0 + B * dy0) * dx0 + C * dy0 * dy0 + log_op,
                (2.0 * A * dx0 + B * dy0) * ex,
                (B * dx0 + 2.0 * C * dy0) * ey,
                A * (ex * ex),
                B * (ex * ey),
                C * (ey * ey),
                zero,
                zero,
            ]
            coefs += [k.astype(F32) for k in split3(jnp.concatenate(coef, axis=0))]
            g = [kept_ref[4 * c + t : 4 * c + t + 1, 128 * h : 128 * (h + 1)] for c in range(3)]
            ghi, gmid, glo = [x.astype(F32) for x in split3(jnp.concatenate(g + [blank[0:5]], axis=0))]
            cots.append((4 * h + t, ghi, gmid))
            pulls.append([ghi, gmid, glo, ghi, gmid, ghi])
        left = coefs + [chi, chi, chi, cmid, cmid, clo] + [jnp.zeros((32, SLOTS), F32)]
        left = jnp.transpose(jnp.concatenate(left, axis=0)).astype(BF16)
        right = []
        for h in range(2):
            right.append([blank] * (3 * h) + [mono8] * 3 + [blank] * (13 - 3 * h))
            right.append([blank] * 6 + pulls[h] + [blank] * 4)
        right = jnp.concatenate([jnp.concatenate(r, axis=0) for r in right], axis=1).astype(BF16)
        both = dot(left, right, 1, 0)
        for h in range(2):
            at = pl.ds(4 * h + t, SLOTS, stride=8)
            alpha_ref[at, :] = both[:, 256 * h : 256 * h + 128]
            pull_ref[at, :] = both[:, 256 * h + 128 : 256 * h + 256]
        geometry.append((ca, cb, cc, dx0, dy0s, chi, cmid))

    depth = jnp.concatenate(
        [place_ref[3:4, SLOTS * t + 128 * h : SLOTS * t + 128 * (h + 1)] for h in range(2) for t in range(TILES)], axis=0
    )
    segments, unroll = 4, 4
    length = SLOTS // segments

    def forward(j, state):
        trans, behind = list(state[0]), list(state[1])
        for i in range(unroll):
            for n in range(segments):
                s = n * length + j * unroll + i
                at = pl.ds(pl.multiple_of(s * 8, 8), 8)
                alpha = jnp.where(s < depth, jnp.exp2(alpha_ref[at, :]), 0.0)
                weight = trans[n] * alpha
                alpha_ref[at, :] = alpha
                weight_ref[at, :] = weight
                trans[n] = trans[n] - weight
                behind[n] = behind[n] + weight * pull_ref[at, :]
        return tuple(trans), tuple(behind)

    ones, zeros = jnp.ones((8, 128), F32), jnp.zeros((8, 128), F32)
    trans, behind = lax.fori_loop(0, length // unroll, forward, ((ones,) * segments, (zeros,) * segments))
    starts, rest = [ones], [zeros]
    for n in range(1, segments):
        starts.append(starts[-1] * trans[n - 1])
        rest.insert(0, behind[segments - n] + trans[segments - n] * rest[0])

    def backward(j, rest):
        rest = list(rest)
        for i in range(unroll):
            for n in range(segments):
                s = (n + 1) * length - 1 - (j * unroll + i)
                at = pl.ds(pl.multiple_of(s * 8, 8), 8)
                more = pull_ref[at, :] - rest[n]
                rest[n] = rest[n] + alpha_ref[at, :] * more
                weight = starts[n] * weight_ref[at, :]
                weight_ref[at, :] = weight
                pull_ref[at, :] = weight * more
        return tuple(rest)

    lax.fori_loop(0, length // unroll, backward, tuple(rest))

    cots = {th: (ghi, gmid) for th, ghi, gmid in cots}
    for t in range(TILES):
        ca, cb, cc, dx0, dy0s, chi, cmid = geometry[t]
        color_rows = jnp.concatenate([chi, cmid], axis=0).astype(BF16)
        total = [jnp.zeros((1, SLOTS), F32) for _ in range(6)]
        dcolor = jnp.zeros((3, SLOTS), F32)
        for h in range(2):
            th = 4 * h + t
            dy0 = dy0s[h]
            whi, wlo = split2(weight_ref[pl.ds(th, SLOTS, stride=8), :])
            weights = jnp.concatenate([whi, wlo], axis=1)
            ghi, glo = split2(pull_ref[pl.ds(th, SLOTS, stride=8), :])
            grads = jnp.concatenate([ghi, glo], axis=1)
            seen = dot(color_rows, weights, 1, 0)
            seen = seen[:, :128] + seen[:, 128:]
            seen = seen[0:8] + seen[8:16]
            for c in range(3):
                image_ref[c, t : t + 1, 128 * h : 128 * (h + 1)] = seen[c : c + 1]
            cot = jnp.concatenate(cots[th], axis=0).astype(BF16)
            dcol = dot(jnp.concatenate([cot, cot], axis=1), weights, 1, 1)
            dcolor = dcolor + dcol[0:3] + dcol[8:11]
            mom = dot(mono_twice, grads, 1, 1)
            m0 = mom[0:1]
            mx, my = ex * mom[1:2], ey * mom[2:3]
            total[0] = total[0] + m0
            total[1] = total[1] + dx0 * m0 + mx
            total[2] = total[2] + dy0 * m0 + my
            total[3] = total[3] + dx0 * (dx0 * m0 + 2.0 * mx) + (ex * ex) * mom[3:4]
            total[4] = total[4] + dx0 * (dy0 * m0 + my) + dy0 * mx + (ex * ey) * mom[4:5]
            total[5] = total[5] + dy0 * (dy0 * m0 + 2.0 * my) + (ey * ey) * mom[5:6]
        s0, sx, sy, sxx, sxy, syy = total
        made = [ca * sx + cb * sy, cb * sx + cc * sy, -0.5 * sxx, -sxy, -0.5 * syy, s0, dcolor]
        grad_ref[0:9, SLOTS * t : SLOTS * (t + 1)] = jnp.concatenate(made, axis=0)

    inv = inv_ref[...]

    def pick(tables, idx):
        at = jnp.maximum(idx - 1, 0)
        low, high = at & 127, at >> 7
        got = lane_gather(tables[0], low)
        for j in range(1, 8):
            got = jnp.where(high == j, lane_gather(tables[j], low), got)
        return jnp.where(idx > 0, got, 0.0)

    tables = [grad_ref[0:8, 128 * j : 128 * (j + 1)] for j in range(8)]
    last = [jnp.broadcast_to(grad_ref[8:9, 128 * j : 128 * (j + 1)], (8, 128)) for j in range(8)]
    left = lax.broadcasted_iota(I32, (4, 128), 1) < 64
    for n in range(PEERS):
        got = pick(tables, jnp.broadcast_to(inv[n : n + 1], (8, 128)))
        out_ref[5 * n : 5 * n + 4, :] = jnp.where(left, got[0:4], got[4:8])
    more = [pick(last, inv[n : n + 8]) for n in range(0, PEERS, 8)]
    left = lax.broadcasted_iota(I32, (PEERS, 128), 1) < 64
    out_ref[pl.ds(4, PEERS, stride=5), :] = jnp.where(left, jnp.concatenate(more, axis=0), names_ref[...])


def collect_kernel(back_ref, kept_ref, out_ref):
    lid = lax.broadcasted_iota(I32, (G_DEV, 256), 0)
    sub = lax.broadcasted_iota(I32, (8, 128), 0)
    lane = lax.broadcasted_iota(I32, (8, 128), 1)
    near, left = (lane & 63) >> 4, lane < 64
    acc = jnp.zeros((80, G_DEV), F32)
    for n in range(0, PEERS, 4):
        hot = (lid == pair_ids(back_ref, n)).astype(F32).astype(BF16)
        pairs = []
        for i in range(2):
            at = 5 * (n + 2 * i)
            one = jnp.concatenate([back_ref[at : at + 4, :]] * 2, axis=0)
            two = jnp.concatenate([back_ref[at + 5 : at + 9, :]] * 2, axis=0)
            other = jnp.where(left, pltpu.roll(one, 64, 1), two)
            straight = jnp.where(left, one, pltpu.roll(two, 64, 1))
            main = jnp.where(sub < 4, straight, other)
            last_one = jnp.broadcast_to(back_ref[at + 4 : at + 5, :], (8, 128))
            last_two = jnp.broadcast_to(back_ref[at + 9 : at + 10, :], (8, 128))
            last = jnp.where(left, last_one, pltpu.roll(last_two, 64, 1))
            rows = []
            for m, l in zip(split2(main), split2(last)):
                m, l = m.astype(F32), l.astype(F32)
                rows += [jnp.where(near == r, m, 0.0) for r in range(NEAR)] + [jnp.where(near == sub, l, 0.0)]
            pairs.append(jnp.concatenate(rows, axis=0).astype(BF16))
        acc = acc + dot(jnp.concatenate(pairs, axis=1), hot, 1, 1)
    rows = acc[0:40] + acc[40:80]
    tail = kept_ref[12:16, 0:128]
    for r in range(NEAR):
        part = [rows[8 * r : 8 * r + 8, 128 * j : 128 * (j + 1)] for j in range(4)]
        part += [rows[32 + r : 33 + r, 128 * j : 128 * (j + 1)] for j in range(4)] + [tail]
        part = jnp.concatenate(part, axis=0)
        for v in range(VIEWS):
            out_ref[40 * (NEAR * v + r) : 40 * (NEAR * v + r + 1), :] = part


def pull_kernel(parts_ref, attr_ref, image_in_ref, out_ref, image_ref, wide_ref, res_ref, all_ref):
    image_ref[...] = image_in_ref[...]
    for v in range(VIEWS):
        start = 40 * NEAR * v
        total = parts_ref[start : start + 36, :]
        for r in range(1, NEAR):
            total = total + parts_ref[start + 40 * r : start + 40 * r + 36, :]
        all_ref[40 * v : 40 * v + 36, :] = total
        all_ref[40 * v + 36 : 40 * v + 40, :] = parts_ref[start + 36 : start + 40, :]
    spread_attributes(attr_ref, wide_ref)
    pos, logscale, quat, logit, sh = split_attributes(wide_ref)
    total = None
    opacity_grad = None
    for pair in range(VIEWS // 2):
        starts = (80 * pair, 80 * pair + 40)
        cot = [
            jnp.concatenate([all_ref[pl.ds(s + c, 4, stride=8), :] for s in starts], axis=0) for c in range(8)
        ]
        cot.append(jnp.concatenate([all_ref[s + 32 : s + 36, :] for s in starts], axis=0))
        cam = [
            jnp.concatenate(
                [jnp.broadcast_to(all_ref[s + 36 : s + 37, j : j + 1], (4, 128)) for s in starts], axis=0
            )
            for j in range(6)
        ]
        terms = camera_terms(cam[:3], cam[3:])
        _, pull = jax.vjp(lambda a, b, c, d: project(a, b, c, d, terms), pos, logscale, quat, sh)
        grads = jax.tree.leaves(pull(cot[:5] + cot[6:]))
        total = grads if total is None else [a + b for a, b in zip(total, grads)]
        opacity_grad = cot[5] if opacity_grad is None else opacity_grad + cot[5]
    grads = total[:10] + [opacity_grad / (1.0 + jnp.exp(logit))] + total[10:]
    for a in range(ATTR):
        res_ref[4 * a : 4 * a + 4, :] = grads[a][0:4] + grads[a][4:8]
    for j in range(4):
        out_ref[:, 128 * j : 128 * (j + 1)] = res_ref[pl.ds(j, ATTR, stride=4), :]


VMEM = pl.BlockSpec(memory_space=pltpu.VMEM)
SMEM = pl.BlockSpec(memory_space=pltpu.SMEM)
HBM = pl.BlockSpec(memory_space=pl.ANY)
MIB = 1024 * 1024


def call(kernel, outs, args, scratch=(), in_specs=None, limit=24):
    return pl.pallas_call(
        kernel,
        out_shape=[jax.ShapeDtypeStruct(s, d) for s, d in outs],
        in_specs=in_specs or [VMEM] * len(args),
        out_specs=[VMEM] * len(outs),
        scratch_shapes=list(scratch),
        compiler_params=pltpu.CompilerParams(vmem_limit_bytes=limit * MIB),
    )(*args)


def vmem(*shape, dtype=F32):
    return pltpu.VMEM(shape, dtype)


def route(first_tile, owner, local, attributes, camera, depth, cot):
    return call(
        route_kernel,
        [
            ((2 * RANKS, 128), F32), ((PEERS, 128), I32), ((8, TILES * SLOTS), I32), ((40 * PLANES, 128), F32),
            ((16, SLOTS), F32), ((PEERS, 128), F32),
        ],
        (first_tile, owner, local, attributes, camera, depth, cot),
        [
            vmem(1, TILES * SLOTS, dtype=I32), vmem(TILES, SLOTS, dtype=I32), vmem(ATTR, G_DEV), vmem(1, 6),
            vmem(TILES, SLOTS, dtype=I32), vmem(3, TILES, SLOTS), vmem(ATTR * 8, 128), vmem(40, 128),
            pltpu.SemaphoreType.DMA((6,)),
        ],
        [SMEM] + [HBM] * 6,
        60,
    )


def serve(first_tile, asked, rows, *kept):
    outs = [((18 * RANKS, 128), F32)] + [(k.shape, k.dtype) for k in kept]
    return call(serve_kernel, outs, (first_tile, asked, rows, *kept), (), [SMEM] + [VMEM] * (2 + len(kept)))


def composite(got, place, inv, kept, names):
    big = vmem(SLOTS * 8, 128)
    return call(
        composite_kernel,
        [((3, TILES, 256), F32), ((5 * PEERS, 128), F32)],
        (got, place, inv, kept, names),
        [vmem(16, TILES * SLOTS), big, big, big, vmem(16, TILES * SLOTS)],
    )


def collect(back, kept):
    return call(collect_kernel, [((VIEWS * NEAR * 40, 128), F32)], (back, kept))[0]


def pull_back(parts, attributes, image):
    return call(
        pull_kernel,
        [((ATTR, G_DEV), F32), (image.shape, F32)],
        (parts, attributes, image),
        [vmem(ATTR * 8, 128), vmem(ATTR * 4, 128), vmem(40 * VIEWS, 128)],
    )


def exchange(x, axis, groups):
    return lax.all_to_all(x, axis, split_axis=0, concat_axis=0, tiled=True, axis_index_groups=groups)


ALONG = [[8 * z + r for z in range(PLANES)] for r in range(RANKS)]
PLANE = [[8 * z + r for r in range(RANKS)] for z in range(PLANES)]
ACROSS = [[8 * z + 2 * y + c for z in range(PLANES) for c in range(2)] for y in range(NEAR)]
WITHIN = [[8 * z + 2 * y + c for y in range(NEAR)] for z in range(PLANES) for c in range(2)]
VIEWS_WITHIN = [[OWNERS * v + d for v in range(VIEWS) for d in group] for group in WITHIN]


def per_device(attributes, camera, list_owner, list_local, term_depth, image_cot):
    owner = list_owner.reshape(1, -1)
    first_tile = (lax.axis_index("dev") * TILES).astype(I32).reshape(1)
    asked, inv, place, rows, kept, names = route(
        first_tile, owner, list_local[0], attributes, camera, term_depth[0], image_cot[0]
    )
    rows = exchange(rows.reshape(PLANES, 40, 128), "dev", ALONG).reshape(PLANES * 40, 128)
    asked = lax.all_gather(asked, "dev", axis_index_groups=PLANE, tiled=True)
    sent, place, inv, kept, names = serve(first_tile, asked, rows, place, inv, kept, names)
    got = exchange(sent.reshape(RANKS, 1, 2304), "dev", PLANE).reshape(18 * RANKS, 128)
    image, grads = composite(got, place, inv, kept, names)
    back = exchange(grads.reshape(PEERS, 1, 640), "dev", ACROSS).reshape(5 * PEERS, 128)
    mine = collect(back, kept)
    parts = exchange(mine.reshape(VIEWS * NEAR, 40, 128), ("view", "dev"), VIEWS_WITHIN)
    grad, image = pull_back(parts.reshape(VIEWS * NEAR * 40, 128), attributes, image)
    return image[None], grad


def solution(mesh):
    in_specs = (
        P(None, "dev"),
        P("view", None),
        P("view", "dev", None, None),
        P("view", "dev", None),
        P("view", "dev", None),
        P("view", None, "dev", None),
    )
    out_specs = (P("view", None, "dev", None), P(None, "dev"))
    return jax.shard_map(
        per_device, mesh=mesh, in_specs=in_specs, out_specs=out_specs, check_vma=False
    )
```

```python
import jax
import jax.numpy as jnp
from jax import lax
from jax.experimental import pallas as pl
from jax.experimental.pallas import tpu as pltpu
from jax.sharding import PartitionSpec as P

TILE_COLS = 16
TILES = 4
SLOTS = 256
CAP = 16
OWNERS = 128
PEERS = 32
NEAR = 4
PLANES = 16
RANKS = 8
G_DEV = 512
ATTR = 59
VIEWS = 4
LOG2E = 1.4426950408889634

SH_C0 = 0.28209479177387814
SH_C1 = 0.4886025119029199
SH_C2 = (
    1.0925484305920792,
    -1.0925484305920792,
    0.31539156525252005,
    -1.0925484305920792,
    0.5462742152960396,
)
SH_C3 = (
    -0.5900435899266435,
    2.890611442640554,
    -0.4570457994644658,
    0.3731763325901154,
    -0.4570457994644658,
    1.445305721320277,
    -0.5900435899266435,
)
BLUR = 1e-05

F32 = jnp.float32
BF16 = jnp.bfloat16
I32 = jnp.int32


def camera_terms(angles, shift):
    cosx, sinx = jnp.cos(angles[0]), jnp.sin(angles[0])
    cosy, siny = jnp.cos(angles[1]), jnp.sin(angles[1])
    cosz, sinz = jnp.cos(angles[2]), jnp.sin(angles[2])
    yx = [
        [cosy, siny * sinx, siny * cosx],
        [None, cosx, -sinx],
        [-siny, cosy * sinx, cosy * cosx],
    ]
    rot = [
        [cosz * yx[0][0]] + [cosz * yx[0][j] - sinz * yx[1][j] for j in (1, 2)],
        [sinz * yx[0][0]] + [sinz * yx[0][j] + cosz * yx[1][j] for j in (1, 2)],
        yx[2],
    ]
    centre = [-(rot[0][j] * shift[0] + rot[1][j] * shift[1] + rot[2][j] * shift[2]) for j in range(3)]
    return rot, shift, centre


def harmonics(dirx, diry, dirz):
    xx, yy, zz = (dirx * dirx, diry * diry, dirz * dirz)
    return [
        -SH_C1 * diry,
        SH_C1 * dirz,
        -SH_C1 * dirx,
        SH_C2[0] * dirx * diry,
        SH_C2[1] * diry * dirz,
        SH_C2[2] * (2.0 * zz - xx - yy),
        SH_C2[3] * dirx * dirz,
        SH_C2[4] * (xx - yy),
        SH_C3[0] * diry * (3.0 * xx - yy),
        SH_C3[1] * dirx * diry * dirz,
        SH_C3[2] * diry * (4.0 * zz - xx - yy),
        SH_C3[3] * dirz * (2.0 * zz - 3.0 * xx - 3.0 * yy),
        SH_C3[4] * dirx * (4.0 * zz - xx - yy),
        SH_C3[5] * dirz * (xx - yy),
        SH_C3[6] * dirx * (xx - 3.0 * yy),
    ]


def project(pos, logscale, quat, sh, cam):
    rot, shift, centre = cam
    cpos = [rot[i][0] * pos[0] + rot[i][1] * pos[1] + rot[i][2] * pos[2] + shift[i] for i in range(3)]
    inverse = 1.0 / cpos[2]
    u, w = cpos[0] * inverse, cpos[1] * inverse
    tmat = [
        [inverse * (rot[0][j] - u * rot[2][j]) for j in range(3)],
        [inverse * (rot[1][j] - w * rot[2][j]) for j in range(3)],
    ]
    scale = [jnp.exp(s) for s in logscale]
    norm = lax.rsqrt(quat[0] * quat[0] + quat[1] * quat[1] + quat[2] * quat[2] + quat[3] * quat[3])
    qw, qa, qb, qc = [q * norm for q in quat]
    rgau = [
        [1 - 2 * (qb * qb + qc * qc), 2 * (qa * qb - qw * qc), 2 * (qa * qc + qw * qb)],
        [2 * (qa * qb + qw * qc), 1 - 2 * (qa * qa + qc * qc), 2 * (qb * qc - qw * qa)],
        [2 * (qa * qc - qw * qb), 2 * (qb * qc + qw * qa), 1 - 2 * (qa * qa + qb * qb)],
    ]
    trs = [
        [(tmat[r][0] * rgau[0][k] + tmat[r][1] * rgau[1][k] + tmat[r][2] * rgau[2][k]) * scale[k] for k in range(3)]
        for r in range(2)
    ]
    sig_a = trs[0][0] * trs[0][0] + trs[0][1] * trs[0][1] + trs[0][2] * trs[0][2] + BLUR
    sig_b = trs[0][0] * trs[1][0] + trs[0][1] * trs[1][1] + trs[0][2] * trs[1][2]
    sig_c = trs[1][0] * trs[1][0] + trs[1][1] * trs[1][1] + trs[1][2] * trs[1][2] + BLUR
    det_inv = 1.0 / (sig_a * sig_c - sig_b * sig_b)
    dirs = [pos[j] - centre[j] for j in range(3)]
    norm_inv = lax.rsqrt(dirs[0] * dirs[0] + dirs[1] * dirs[1] + dirs[2] * dirs[2])
    basis = harmonics(dirs[0] * norm_inv, dirs[1] * norm_inv, dirs[2] * norm_inv)
    colors = []
    for ch in range(3):
        color = 0.5 + SH_C0 * sh[ch]
        for k in range(1, 16):
            color = color + basis[k - 1] * sh[3 * k + ch]
        colors.append(color)
    return [u, w, sig_c * det_inv, -sig_b * det_inv, sig_a * det_inv] + colors


def spread_attributes(attr_ref, wide_ref):
    for j in range(4):
        part = attr_ref[:, 128 * j : 128 * (j + 1)]
        wide_ref[pl.ds(j, ATTR, stride=8), :] = part
        wide_ref[pl.ds(j + 4, ATTR, stride=8), :] = part


def split_attributes(wide_ref):
    attrs = [wide_ref[8 * a : 8 * (a + 1), :] for a in range(ATTR)]
    return attrs[0:3], attrs[3:6], attrs[6:10], attrs[10], attrs[11:]


def dot(a, b, ca, cb):
    return lax.dot_general(a, b, (((ca,), (cb,)), ((), ())), preferred_element_type=F32)


def lane_gather(x, idx):
    return jnp.take_along_axis(x, idx, axis=1, mode="promise_in_bounds")


def split2(x):
    hi = x.astype(BF16)
    return hi, (x - hi.astype(F32)).astype(BF16)


def split3(x):
    hi = x.astype(BF16)
    rest = x - hi.astype(F32)
    mid = rest.astype(BF16)
    return hi, mid, (rest - mid.astype(F32)).astype(BF16)


def route_kernel(
    tile_ref, owner_hbm, local_hbm, attr_hbm, cam_hbm, depth_hbm, cot_hbm,
    near_ref, far_ref, inv_ref, place_ref, rows_hbm, kept_ref, names_ref,
    owner_ref, local_ref, attr_ref, cam_ref, depth_ref, cot_ref, wide_ref, tmp_ref, rows_ref, sem,
):
    pairs = [
        (owner_hbm, owner_ref), (local_hbm, local_ref), (attr_hbm, attr_ref), (cam_hbm, cam_ref),
        (depth_hbm, depth_ref), (cot_hbm, cot_ref),
    ]
    copies = [pltpu.make_async_copy(src, dst, sem.at[n]) for n, (src, dst) in enumerate(pairs)]
    for copy in copies:
        copy.start()
    copies[2].wait()
    copies[3].wait()
    spread_attributes(attr_ref, wide_ref)
    pos, logscale, quat, logit, sh = split_attributes(wide_ref)
    cam = [jnp.broadcast_to(cam_ref[:, j : j + 1], (8, 128)) for j in range(6)]
    rows = project(pos, logscale, quat, sh, camera_terms(cam[:3], cam[3:]))
    log_opacity = -LOG2E * jnp.log(1.0 + jnp.exp(-logit))
    rows = rows[:5] + [log_opacity] + rows[5:]
    for c in range(8):
        tmp_ref[pl.ds(c, 4, stride=8), :] = rows[c][0:4]
    tmp_ref[32:36, :] = rows[8][0:4]
    tmp_ref[36:40, :] = jnp.zeros((4, 128), F32)
    rows = tmp_ref[...]
    for z in range(PLANES):
        rows_ref[40 * z : 40 * (z + 1), :] = rows
    rows_copy = pltpu.make_async_copy(rows_ref, rows_hbm, sem.at[6])
    rows_copy.start()
    before = (
        lax.broadcasted_iota(I32, (SLOTS, SLOTS), 0) < lax.broadcasted_iota(I32, (SLOTS, SLOTS), 1)
    ).astype(F32).astype(BF16)
    every = jnp.ones((SLOTS, SLOTS), BF16)
    oid = lax.broadcasted_iota(I32, (OWNERS, SLOTS), 0)
    pid = lax.broadcasted_iota(I32, (PEERS, SLOTS), 0)
    lane = lax.broadcasted_iota(I32, (1, SLOTS), 1)
    base = jnp.zeros((OWNERS, SLOTS), F32)
    gid = lax.broadcasted_iota(I32, (2 * RANKS, SLOTS), 0)
    table = jnp.zeros((4 * PEERS, 128), F32)
    request = jnp.zeros((4 * RANKS, 128), F32)
    for n in (0, 1, 4, 5):
        copies[n].wait()
    core = (tile_ref[0] // TILES) & 1
    for t in range(TILES):
        owner = owner_ref[:, SLOTS * t : SLOTS * (t + 1)]
        hot = (oid == owner).astype(F32)
        hot16 = hot.astype(BF16)
        count = dot(hot16, before, 1, 0) + base
        base = base + dot(hot16, every, 1, 0)
        rank = jnp.sum(hot * count, axis=0, keepdims=True).astype(I32)
        local = local_ref[t : t + 1, :]
        local_parts = [local & 255, local >> 8]
        slot = lane + (SLOTS * t + 1)
        group = (owner & 7) * 2 + (owner >> 6)
        lanes = ((owner >> 3) & 7) * CAP + rank
        place_ref[0:1, SLOTS * t : SLOTS * (t + 1)] = group
        place_ref[1:2, SLOTS * t : SLOTS * (t + 1)] = lanes
        hot_group = (gid == ((owner & 1) ^ core) * 8 + (owner & 6) + (owner >> 6)).astype(F32)
        vals = jnp.concatenate([hot_group * p.astype(F32) for p in local_parts], axis=0).astype(BF16)
        request = request + dot(vals, (oid == lanes).astype(F32).astype(BF16), 1, 1)
        peer = (owner >> 3) * 2 + (owner & 1)
        lanes = ((owner >> 1) & 3) * CAP + rank
        hot_peer = (pid == peer).astype(F32)
        parts = local_parts + [slot & 255, slot >> 8]
        vals = jnp.concatenate([hot_peer * p.astype(F32) for p in parts], axis=0).astype(BF16)
        table = table + dot(vals, ((oid & 63) == lanes).astype(F32).astype(BF16), 1, 1)
    place_ref[2:3, :] = jnp.full((1, TILES * SLOTS), tile_ref[0], I32)
    n = PEERS
    near_ref[...] = request[0:8] + 256.0 * request[16:24]
    far_ref[...] = request[8:16] + 256.0 * request[24:32]
    names_ref[...] = table[0:n] + 256.0 * table[n : 2 * n]
    inv_ref[...] = (table[2 * n : 3 * n] + 256.0 * table[3 * n :]).astype(I32)
    for c in range(3):
        kept_ref[4 * c : 4 * c + 4, :] = cot_ref[c]
    kept_ref[12:16, :] = jnp.zeros((4, SLOTS), F32)
    kept_ref[12:13, 0:6] = cam_ref[...]
    for t in range(TILES):
        place_ref[3:4, SLOTS * t : SLOTS * (t + 1)] = depth_ref[t : t + 1, :]
    rows_copy.wait()


def serve_kernel(tile_ref, asked_ref, rows_ref, *refs):
    kept, (out_ref, *outs) = refs[:4], refs[4:]
    for src, dst in zip(kept, outs):
        dst[...] = src[...]
    dev = tile_ref[0] // TILES
    core, mine = dev & 1, dev & 6
    lid = lax.broadcasted_iota(I32, (G_DEV, 256), 0)
    sub = lax.broadcasted_iota(I32, (8, 128), 0)
    near = lax.broadcasted_iota(I32, (8, 128), 1) >> 4
    for half in range(2):
        start = 320 * half
        table = []
        for j in range(4):
            part = [rows_ref[start + 40 * r + 8 * j : start + 40 * r + 8 * j + 8, :] for r in range(8)]
            part.append(rows_ref[pl.ds(start + 32 + j, 8, stride=40), :])
            table.append(jnp.concatenate(part, axis=0))
        table = [x.astype(F32) for x in split3(jnp.concatenate(table, axis=1))]
        table = jnp.concatenate(table + [jnp.zeros((8, G_DEV), F32)], axis=0).astype(BF16)
        for r in range(0, RANKS, 2):
            ids = [asked_ref[pl.ds(8 * r + 8 * (i ^ core) + mine + half, 1), :] for i in range(2)]
            hot = (lid == jnp.concatenate(ids, axis=1).astype(I32)).astype(F32).astype(BF16)
            got = dot(table, hot, 1, 0)
            got = got[0:72] + got[72:144] + got[144:216]
            for i in range(2):
                part = got[:, 128 * i : 128 * (i + 1)]
                main = part[0:8]
                for n in range(1, 8):
                    main = jnp.where(near == n, part[8 * n : 8 * (n + 1)], main)
                at = 9 * (2 * (r + i) + half)
                out_ref[at : at + 8, :] = main
                last = jnp.sum(jnp.where(near == sub, part[64:72], 0.0), axis=0, keepdims=True)
                out_ref[at + 8 : at + 9, :] = last


def pair_ids(back_ref, n):
    left = lax.broadcasted_iota(I32, (8, 128), 1) < 64
    rows = [jnp.broadcast_to(back_ref[5 * (n + i) + 4 : 5 * (n + i) + 5, :], (8, 128)) for i in range(4)]
    pairs = [jnp.where(left, pltpu.roll(rows[i], 64, 1), rows[i + 1]) for i in (0, 2)]
    return jnp.concatenate(pairs, axis=1)[0:1].astype(I32)


def composite_kernel(
    got_ref, place_ref, inv_ref, kept_ref, names_ref, image_ref, out_ref,
    par_ref, alpha_ref, pull_ref, weight_ref, grad_ref,
):
    groups = 2 * RANKS
    last = got_ref[pl.ds(8, groups, stride=9), :]
    sub = lax.broadcasted_iota(I32, (8, 128), 0)
    for b in range(8):
        group = jnp.broadcast_to(place_ref[0:1, 128 * b : 128 * (b + 1)], (8, 128))
        lanes = jnp.broadcast_to(place_ref[1:2, 128 * b : 128 * (b + 1)], (8, 128))
        got = lane_gather(got_ref[0:8, :], lanes)
        for n in range(1, groups):
            got = jnp.where(group == n, lane_gather(got_ref[9 * n : 9 * n + 8, :], lanes), got)
        par_ref[0:8, 128 * b : 128 * (b + 1)] = got
        low = jnp.where(group == sub, lane_gather(last[0:8], lanes), 0.0)
        high = jnp.where(group == sub + 8, lane_gather(last[8:16], lanes), 0.0)
        par_ref[8:9, 128 * b : 128 * (b + 1)] = jnp.sum(low + high, axis=0, keepdims=True)

    q = lax.broadcasted_iota(I32, (16, 128), 1)
    row16 = lax.broadcasted_iota(I32, (16, 128), 0)
    X = (q & 15).astype(F32) - 7.5
    Y = (q >> 4).astype(F32) - 3.5
    mono = jnp.where(row16 == 0, 1.0, 0.0)
    for n, m in enumerate([X, Y, X * X, X * Y, Y * Y]):
        mono = jnp.where(row16 == n + 1, m, mono)
    mono8 = mono[0:8]
    mono16 = mono.astype(BF16)
    mono_twice = jnp.concatenate([mono16, mono16], axis=1)
    ex, ey = 1.0 / (16.0 * TILE_COLS), 1.0 / (16.0 * (TILES * OWNERS // TILE_COLS))

    zero = jnp.zeros((1, SLOTS), F32)
    zero5 = jnp.zeros((5, SLOTS), F32)
    blank = jnp.zeros((8, 128), F32)
    cots = []
    geometry = []
    for t in range(TILES):
        par = [par_ref[c : c + 1, SLOTS * t : SLOTS * (t + 1)] for c in range(9)]
        u, w, ca, cb, cc, log_op = par[:6]
        tile = place_ref[2:3, 0:SLOTS] + t
        cx = ((tile & (TILE_COLS - 1)) * 16 + 8).astype(F32) * ex - 0.5
        dx0 = cx - u
        A, B, C = -0.5 * LOG2E * ca, -LOG2E * cb, -0.5 * LOG2E * cc
        colors = jnp.concatenate([par[6], par[7], par[8], zero5], axis=0)
        chi, cmid, clo = [c.astype(F32) for c in split3(colors)]
        dy0s = []
        coefs, pulls = [], []
        for h in range(2):
            cy = ((tile >> 4) * 16 + 8 * h + 4).astype(F32) * ey - 0.5
            dy0 = cy - w
            dy0s.append(dy0)
            coef = [
                (A * dx0 + B * dy0) * dx0 + C * dy0 * dy0 + log_op,
                (2.0 * A * dx0 + B * dy0) * ex,
                (B * dx0 + 2.0 * C * dy0) * ey,
                A * (ex * ex),
                B * (ex * ey),
                C * (ey * ey),
                zero,
                zero,
            ]
            coefs += [k.astype(F32) for k in split3(jnp.concatenate(coef, axis=0))]
            g = [kept_ref[4 * c + t : 4 * c + t + 1, 128 * h : 128 * (h + 1)] for c in range(3)]
            ghi, gmid, glo = [x.astype(F32) for x in split3(jnp.concatenate(g + [blank[0:5]], axis=0))]
            cots.append((4 * h + t, ghi, gmid))
            pulls.append([ghi, gmid, glo, ghi, gmid, ghi])
        left = coefs + [chi, chi, chi, cmid, cmid, clo] + [jnp.zeros((32, SLOTS), F32)]
        left = jnp.transpose(jnp.concatenate(left, axis=0)).astype(BF16)
        right = []
        for h in range(2):
            right.append([blank] * (3 * h) + [mono8] * 3 + [blank] * (13 - 3 * h))
            right.append([blank] * 6 + pulls[h] + [blank] * 4)
        right = jnp.concatenate([jnp.concatenate(r, axis=0) for r in right], axis=1).astype(BF16)
        both = dot(left, right, 1, 0)
        for h in range(2):
            at = pl.ds(4 * h + t, SLOTS, stride=8)
            alpha_ref[at, :] = both[:, 256 * h : 256 * h + 128]
            pull_ref[at, :] = both[:, 256 * h + 128 : 256 * h + 256]
        geometry.append((ca, cb, cc, dx0, dy0s, chi, cmid))

    depth = jnp.concatenate(
        [place_ref[3:4, SLOTS * t + 128 * h : SLOTS * t + 128 * (h + 1)] for h in range(2) for t in range(TILES)], axis=0
    )
    segments, unroll = 4, 4
    length = SLOTS // segments

    def forward(j, state):
        trans, behind = list(state[0]), list(state[1])
        for i in range(unroll):
            for n in range(segments):
                s = n * length + j * unroll + i
                at = pl.ds(pl.multiple_of(s * 8, 8), 8)
                alpha = jnp.where(s < depth, jnp.exp2(alpha_ref[at, :]), 0.0)
                weight = trans[n] * alpha
                alpha_ref[at, :] = alpha
                weight_ref[at, :] = weight
                trans[n] = trans[n] - weight
                behind[n] = behind[n] + weight * pull_ref[at, :]
        return tuple(trans), tuple(behind)

    ones, zeros = jnp.ones((8, 128), F32), jnp.zeros((8, 128), F32)
    trans, behind = lax.fori_loop(0, length // unroll, forward, ((ones,) * segments, (zeros,) * segments))
    starts, rest = [ones], [zeros]
    for n in range(1, segments):
        starts.append(starts[-1] * trans[n - 1])
        rest.insert(0, behind[segments - n] + trans[segments - n] * rest[0])

    def backward(j, rest):
        rest = list(rest)
        for i in range(unroll):
            for n in range(segments):
                s = (n + 1) * length - 1 - (j * unroll + i)
                at = pl.ds(pl.multiple_of(s * 8, 8), 8)
                more = pull_ref[at, :] - rest[n]
                rest[n] = rest[n] + alpha_ref[at, :] * more
                weight = starts[n] * weight_ref[at, :]
                weight_ref[at, :] = weight
                pull_ref[at, :] = weight * more
        return tuple(rest)

    lax.fori_loop(0, length // unroll, backward, tuple(rest))

    cots = {th: (ghi, gmid) for th, ghi, gmid in cots}
    for t in range(TILES):
        ca, cb, cc, dx0, dy0s, chi, cmid = geometry[t]
        color_rows = jnp.concatenate([chi, cmid], axis=0).astype(BF16)
        total = [jnp.zeros((1, SLOTS), F32) for _ in range(6)]
        dcolor = jnp.zeros((3, SLOTS), F32)
        for h in range(2):
            th = 4 * h + t
            dy0 = dy0s[h]
            whi, wlo = split2(weight_ref[pl.ds(th, SLOTS, stride=8), :])
            weights = jnp.concatenate([whi, wlo], axis=1)
            ghi, glo = split2(pull_ref[pl.ds(th, SLOTS, stride=8), :])
            grads = jnp.concatenate([ghi, glo], axis=1)
            seen = dot(color_rows, weights, 1, 0)
            seen = seen[:, :128] + seen[:, 128:]
            seen = seen[0:8] + seen[8:16]
            for c in range(3):
                image_ref[c, t : t + 1, 128 * h : 128 * (h + 1)] = seen[c : c + 1]
            cot = jnp.concatenate(cots[th], axis=0).astype(BF16)
            dcol = dot(jnp.concatenate([cot, cot], axis=1), weights, 1, 1)
            dcolor = dcolor + dcol[0:3] + dcol[8:11]
            mom = dot(mono_twice, grads, 1, 1)
            m0 = mom[0:1]
            mx, my = ex * mom[1:2], ey * mom[2:3]
            total[0] = total[0] + m0
            total[1] = total[1] + dx0 * m0 + mx
            total[2] = total[2] + dy0 * m0 + my
            total[3] = total[3] + dx0 * (dx0 * m0 + 2.0 * mx) + (ex * ex) * mom[3:4]
            total[4] = total[4] + dx0 * (dy0 * m0 + my) + dy0 * mx + (ex * ey) * mom[4:5]
            total[5] = total[5] + dy0 * (dy0 * m0 + 2.0 * my) + (ey * ey) * mom[5:6]
        s0, sx, sy, sxx, sxy, syy = total
        made = [ca * sx + cb * sy, cb * sx + cc * sy, -0.5 * sxx, -sxy, -0.5 * syy, s0, dcolor]
        grad_ref[0:9, SLOTS * t : SLOTS * (t + 1)] = jnp.concatenate(made, axis=0)

    inv = inv_ref[...]

    def pick(tables, idx):
        at = jnp.maximum(idx - 1, 0)
        low, high = at & 127, at >> 7
        got = lane_gather(tables[0], low)
        for j in range(1, 8):
            got = jnp.where(high == j, lane_gather(tables[j], low), got)
        return jnp.where(idx > 0, got, 0.0)

    tables = [grad_ref[0:8, 128 * j : 128 * (j + 1)] for j in range(8)]
    last = [jnp.broadcast_to(grad_ref[8:9, 128 * j : 128 * (j + 1)], (8, 128)) for j in range(8)]
    left = lax.broadcasted_iota(I32, (4, 128), 1) < 64
    for n in range(PEERS):
        got = pick(tables, jnp.broadcast_to(inv[n : n + 1], (8, 128)))
        out_ref[5 * n : 5 * n + 4, :] = jnp.where(left, got[0:4], got[4:8])
    more = [pick(last, inv[n : n + 8]) for n in range(0, PEERS, 8)]
    left = lax.broadcasted_iota(I32, (PEERS, 128), 1) < 64
    out_ref[pl.ds(4, PEERS, stride=5), :] = jnp.where(left, jnp.concatenate(more, axis=0), names_ref[...])


def collect_kernel(back_ref, kept_ref, out_ref):
    lid = lax.broadcasted_iota(I32, (G_DEV, 256), 0)
    sub = lax.broadcasted_iota(I32, (8, 128), 0)
    lane = lax.broadcasted_iota(I32, (8, 128), 1)
    near, left = (lane & 63) >> 4, lane < 64
    acc = jnp.zeros((80, G_DEV), F32)
    for n in range(0, PEERS, 4):
        hot = (lid == pair_ids(back_ref, n)).astype(F32).astype(BF16)
        pairs = []
        for i in range(2):
            at = 5 * (n + 2 * i)
            one = jnp.concatenate([back_ref[at : at + 4, :]] * 2, axis=0)
            two = jnp.concatenate([back_ref[at + 5 : at + 9, :]] * 2, axis=0)
            other = jnp.where(left, pltpu.roll(one, 64, 1), two)
            straight = jnp.where(left, one, pltpu.roll(two, 64, 1))
            main = jnp.where(sub < 4, straight, other)
            last_one = jnp.broadcast_to(back_ref[at + 4 : at + 5, :], (8, 128))
            last_two = jnp.broadcast_to(back_ref[at + 9 : at + 10, :], (8, 128))
            last = jnp.where(left, last_one, pltpu.roll(last_two, 64, 1))
            rows = []
            for m, l in zip(split2(main), split2(last)):
                m, l = m.astype(F32), l.astype(F32)
                rows += [jnp.where(near == r, m, 0.0) for r in range(NEAR)] + [jnp.where(near == sub, l, 0.0)]
            pairs.append(jnp.concatenate(rows, axis=0).astype(BF16))
        acc = acc + dot(jnp.concatenate(pairs, axis=1), hot, 1, 1)
    rows = acc[0:40] + acc[40:80]
    tail = kept_ref[12:16, 0:128]
    for r in range(NEAR):
        part = [rows[8 * r : 8 * r + 8, 128 * j : 128 * (j + 1)] for j in range(4)]
        part += [rows[32 + r : 33 + r, 128 * j : 128 * (j + 1)] for j in range(4)] + [tail]
        part = jnp.concatenate(part, axis=0)
        for v in range(VIEWS):
            out_ref[40 * (NEAR * v + r) : 40 * (NEAR * v + r + 1), :] = part


def pull_kernel(parts_ref, attr_ref, image_in_ref, out_ref, image_ref, wide_ref, res_ref, all_ref):
    image_ref[...] = image_in_ref[...]
    for v in range(VIEWS):
        start = 40 * NEAR * v
        total = parts_ref[start : start + 36, :]
        for r in range(1, NEAR):
            total = total + parts_ref[start + 40 * r : start + 40 * r + 36, :]
        all_ref[40 * v : 40 * v + 36, :] = total
        all_ref[40 * v + 36 : 40 * v + 40, :] = parts_ref[start + 36 : start + 40, :]
    spread_attributes(attr_ref, wide_ref)
    pos, logscale, quat, logit, sh = split_attributes(wide_ref)
    total = None
    opacity_grad = None
    for pair in range(VIEWS // 2):
        starts = (80 * pair, 80 * pair + 40)
        cot = [
            jnp.concatenate([all_ref[pl.ds(s + c, 4, stride=8), :] for s in starts], axis=0) for c in range(8)
        ]
        cot.append(jnp.concatenate([all_ref[s + 32 : s + 36, :] for s in starts], axis=0))
        cam = [
            jnp.concatenate(
                [jnp.broadcast_to(all_ref[s + 36 : s + 37, j : j + 1], (4, 128)) for s in starts], axis=0
            )
            for j in range(6)
        ]
        terms = camera_terms(cam[:3], cam[3:])
        _, pull = jax.vjp(lambda a, b, c, d: project(a, b, c, d, terms), pos, logscale, quat, sh)
        grads = jax.tree.leaves(pull(cot[:5] + cot[6:]))
        total = grads if total is None else [a + b for a, b in zip(total, grads)]
        opacity_grad = cot[5] if opacity_grad is None else opacity_grad + cot[5]
    grads = total[:10] + [opacity_grad / (1.0 + jnp.exp(logit))] + total[10:]
    for a in range(ATTR):
        res_ref[4 * a : 4 * a + 4, :] = grads[a][0:4] + grads[a][4:8]
    for j in range(4):
        out_ref[:, 128 * j : 128 * (j + 1)] = res_ref[pl.ds(j, ATTR, stride=4), :]


VMEM = pl.BlockSpec(memory_space=pltpu.VMEM)
SMEM = pl.BlockSpec(memory_space=pltpu.SMEM)
HBM = pl.BlockSpec(memory_space=pl.ANY)
MIB = 1024 * 1024


def call(kernel, outs, args, scratch=(), in_specs=None, out_specs=None, limit=24):
    return pl.pallas_call(
        kernel,
        out_shape=[jax.ShapeDtypeStruct(s, d) for s, d in outs],
        in_specs=in_specs or [VMEM] * len(args),
        out_specs=out_specs or [VMEM] * len(outs),
        scratch_shapes=list(scratch),
        compiler_params=pltpu.CompilerParams(vmem_limit_bytes=limit * MIB),
    )(*args)


def vmem(*shape, dtype=F32):
    return pltpu.VMEM(shape, dtype)


def route(first_tile, owner, local, attributes, camera, depth, cot):
    return call(
        route_kernel,
        [
            ((8, 128), F32), ((8, 128), F32), ((PEERS, 128), I32), ((8, TILES * SLOTS), I32), ((40 * PLANES, 128), F32),
            ((16, SLOTS), F32), ((PEERS, 128), F32),
        ],
        (first_tile, owner, local, attributes, camera, depth, cot),
        [
            vmem(1, TILES * SLOTS, dtype=I32), vmem(TILES, SLOTS, dtype=I32), vmem(ATTR, G_DEV), vmem(1, 6),
            vmem(TILES, SLOTS, dtype=I32), vmem(3, TILES, SLOTS), vmem(ATTR * 8, 128), vmem(40, 128),
            vmem(40 * PLANES, 128), pltpu.SemaphoreType.DMA((7,)),
        ],
        [SMEM] + [HBM] * 6,
        [VMEM] * 4 + [HBM] + [VMEM] * 2,
        60,
    )


def serve(first_tile, asked, rows, *kept):
    outs = [((18 * RANKS, 128), F32)] + [(k.shape, k.dtype) for k in kept]
    return call(serve_kernel, outs, (first_tile, asked, rows, *kept), (), [SMEM] + [VMEM] * (2 + len(kept)))


def composite(got, place, inv, kept, names):
    big = vmem(SLOTS * 8, 128)
    return call(
        composite_kernel,
        [((3, TILES, 256), F32), ((5 * PEERS, 128), F32)],
        (got, place, inv, kept, names),
        [vmem(16, TILES * SLOTS), big, big, big, vmem(16, TILES * SLOTS)],
    )


def collect(back, kept):
    return call(collect_kernel, [((VIEWS * NEAR * 40, 128), F32)], (back, kept))[0]


def pull_back(parts, attributes, image):
    return call(
        pull_kernel,
        [((ATTR, G_DEV), F32), (image.shape, F32)],
        (parts, attributes, image),
        [vmem(ATTR * 8, 128), vmem(ATTR * 4, 128), vmem(40 * VIEWS, 128)],
    )


def exchange(x, axis, groups):
    return lax.all_to_all(x, axis, split_axis=0, concat_axis=0, tiled=True, axis_index_groups=groups)


ALONG = [[8 * z + r for z in range(PLANES)] for r in range(RANKS)]
PLANE = [[8 * z + r for r in range(RANKS)] for z in range(PLANES)]
ACROSS = [[8 * z + 2 * y + c for z in range(PLANES) for c in range(2)] for y in range(NEAR)]
WITHIN = [[8 * z + 2 * y + c for y in range(NEAR)] for z in range(PLANES) for c in range(2)]
VIEWS_WITHIN = [[OWNERS * v + d for v in range(VIEWS) for d in group] for group in WITHIN]


def per_device(attributes, camera, list_owner, list_local, term_depth, image_cot):
    owner = list_owner.reshape(1, -1)
    first_tile = (lax.axis_index("dev") * TILES).astype(I32).reshape(1)
    near, far, inv, place, rows, kept, names = route(
        first_tile, owner, list_local[0], attributes, camera, term_depth[0], image_cot[0]
    )
    rows = exchange(rows.reshape(PLANES, 40, 128), "dev", ALONG).reshape(PLANES * 40, 128)
    far = lax.ppermute(far, "dev", [(d, d ^ 1) for d in range(OWNERS)])
    asked = lax.all_gather(jnp.concatenate([near, far]), "dev", axis_index_groups=WITHIN, tiled=True)
    sent, place, inv, kept, names = serve(first_tile, asked, rows, place, inv, kept, names)
    got = exchange(sent.reshape(RANKS, 1, 2304), "dev", PLANE).reshape(18 * RANKS, 128)
    image, grads = composite(got, place, inv, kept, names)
    back = exchange(grads.reshape(PEERS, 1, 640), "dev", ACROSS).reshape(5 * PEERS, 128)
    mine = collect(back, kept)
    parts = exchange(mine.reshape(VIEWS * NEAR, 40, 128), ("view", "dev"), VIEWS_WITHIN)
    grad, image = pull_back(parts.reshape(VIEWS * NEAR * 40, 128), attributes, image)
    return image[None], grad


def solution(mesh):
    in_specs = (
        P(None, "dev"),
        P("view", None),
        P("view", "dev", None, None),
        P("view", "dev", None),
        P("view", "dev", None),
        P("view", None, "dev", None),
    )
    out_specs = (P("view", None, "dev", None), P(None, "dev"))
    return jax.shard_map(
        per_device, mesh=mesh, in_specs=in_specs, out_specs=out_specs, check_vma=False
    )
```

```python
import jax
import jax.numpy as jnp
from jax import lax
from jax.experimental import pallas as pl
from jax.experimental.pallas import tpu as pltpu
from jax.sharding import PartitionSpec as P

TILE_COLS = 16
TILES = 4
SLOTS = 256
CAP = 16
OWNERS = 128
PEERS = 32
NEAR = 4
PLANES = 16
RANKS = 8
SEGMENTS = 4
G_DEV = 512
ATTR = 59
VIEWS = 4
LOG2E = 1.4426950408889634

SH_C0 = 0.28209479177387814
SH_C1 = 0.4886025119029199
SH_C2 = (
    1.0925484305920792,
    -1.0925484305920792,
    0.31539156525252005,
    -1.0925484305920792,
    0.5462742152960396,
)
SH_C3 = (
    -0.5900435899266435,
    2.890611442640554,
    -0.4570457994644658,
    0.3731763325901154,
    -0.4570457994644658,
    1.445305721320277,
    -0.5900435899266435,
)
BLUR = 1e-05

F32 = jnp.float32
BF16 = jnp.bfloat16
I32 = jnp.int32


def camera_terms(angles, shift):
    cosx, sinx = jnp.cos(angles[0]), jnp.sin(angles[0])
    cosy, siny = jnp.cos(angles[1]), jnp.sin(angles[1])
    cosz, sinz = jnp.cos(angles[2]), jnp.sin(angles[2])
    yx = [
        [cosy, siny * sinx, siny * cosx],
        [None, cosx, -sinx],
        [-siny, cosy * sinx, cosy * cosx],
    ]
    rot = [
        [cosz * yx[0][0]] + [cosz * yx[0][j] - sinz * yx[1][j] for j in (1, 2)],
        [sinz * yx[0][0]] + [sinz * yx[0][j] + cosz * yx[1][j] for j in (1, 2)],
        yx[2],
    ]
    centre = [-(rot[0][j] * shift[0] + rot[1][j] * shift[1] + rot[2][j] * shift[2]) for j in range(3)]
    return rot, shift, centre


def harmonics(dirx, diry, dirz):
    xx, yy, zz = (dirx * dirx, diry * diry, dirz * dirz)
    return [
        -SH_C1 * diry,
        SH_C1 * dirz,
        -SH_C1 * dirx,
        SH_C2[0] * dirx * diry,
        SH_C2[1] * diry * dirz,
        SH_C2[2] * (2.0 * zz - xx - yy),
        SH_C2[3] * dirx * dirz,
        SH_C2[4] * (xx - yy),
        SH_C3[0] * diry * (3.0 * xx - yy),
        SH_C3[1] * dirx * diry * dirz,
        SH_C3[2] * diry * (4.0 * zz - xx - yy),
        SH_C3[3] * dirz * (2.0 * zz - 3.0 * xx - 3.0 * yy),
        SH_C3[4] * dirx * (4.0 * zz - xx - yy),
        SH_C3[5] * dirz * (xx - yy),
        SH_C3[6] * dirx * (xx - 3.0 * yy),
    ]


def project(pos, logscale, quat, sh, cam):
    rot, shift, centre = cam
    cpos = [rot[i][0] * pos[0] + rot[i][1] * pos[1] + rot[i][2] * pos[2] + shift[i] for i in range(3)]
    inverse = 1.0 / cpos[2]
    u, w = cpos[0] * inverse, cpos[1] * inverse
    tmat = [
        [inverse * (rot[0][j] - u * rot[2][j]) for j in range(3)],
        [inverse * (rot[1][j] - w * rot[2][j]) for j in range(3)],
    ]
    scale = [jnp.exp(s) for s in logscale]
    norm = lax.rsqrt(quat[0] * quat[0] + quat[1] * quat[1] + quat[2] * quat[2] + quat[3] * quat[3])
    qw, qa, qb, qc = [q * norm for q in quat]
    rgau = [
        [1 - 2 * (qb * qb + qc * qc), 2 * (qa * qb - qw * qc), 2 * (qa * qc + qw * qb)],
        [2 * (qa * qb + qw * qc), 1 - 2 * (qa * qa + qc * qc), 2 * (qb * qc - qw * qa)],
        [2 * (qa * qc - qw * qb), 2 * (qb * qc + qw * qa), 1 - 2 * (qa * qa + qb * qb)],
    ]
    trs = [
        [(tmat[r][0] * rgau[0][k] + tmat[r][1] * rgau[1][k] + tmat[r][2] * rgau[2][k]) * scale[k] for k in range(3)]
        for r in range(2)
    ]
    sig_a = trs[0][0] * trs[0][0] + trs[0][1] * trs[0][1] + trs[0][2] * trs[0][2] + BLUR
    sig_b = trs[0][0] * trs[1][0] + trs[0][1] * trs[1][1] + trs[0][2] * trs[1][2]
    sig_c = trs[1][0] * trs[1][0] + trs[1][1] * trs[1][1] + trs[1][2] * trs[1][2] + BLUR
    det_inv = 1.0 / (sig_a * sig_c - sig_b * sig_b)
    dirs = [pos[j] - centre[j] for j in range(3)]
    norm_inv = lax.rsqrt(dirs[0] * dirs[0] + dirs[1] * dirs[1] + dirs[2] * dirs[2])
    basis = harmonics(dirs[0] * norm_inv, dirs[1] * norm_inv, dirs[2] * norm_inv)
    colors = []
    for ch in range(3):
        color = 0.5 + SH_C0 * sh[ch]
        for k in range(1, 16):
            color = color + basis[k - 1] * sh[3 * k + ch]
        colors.append(color)
    return [u, w, sig_c * det_inv, -sig_b * det_inv, sig_a * det_inv] + colors


def spread_attributes(attr_ref, wide_ref):
    for j in range(4):
        part = attr_ref[:, 128 * j : 128 * (j + 1)]
        wide_ref[pl.ds(j, ATTR, stride=8), :] = part
        wide_ref[pl.ds(j + 4, ATTR, stride=8), :] = part


def split_attributes(wide_ref):
    attrs = [wide_ref[8 * a : 8 * (a + 1), :] for a in range(ATTR)]
    return attrs[0:3], attrs[3:6], attrs[6:10], attrs[10], attrs[11:]


def dot(a, b, ca, cb):
    return lax.dot_general(a, b, (((ca,), (cb,)), ((), ())), preferred_element_type=F32)


def lane_gather(x, idx):
    return jnp.take_along_axis(x, idx, axis=1, mode="promise_in_bounds")


def split2(x):
    hi = x.astype(BF16)
    return hi, (x - hi.astype(F32)).astype(BF16)


def split3(x):
    hi = x.astype(BF16)
    rest = x - hi.astype(F32)
    mid = rest.astype(BF16)
    return hi, mid, (rest - mid.astype(F32)).astype(BF16)


def route_kernel(
    tile_ref, owner_hbm, local_hbm, attr_hbm, cam_hbm, depth_hbm, cot_hbm,
    near_ref, far_ref, inv_ref, place_ref, rows_ref, kept_ref, names_ref,
    owner_ref, local_ref, attr_ref, cam_ref, depth_ref, cot_ref, wide_ref, tmp_ref, sem,
):
    pairs = [
        (owner_hbm, owner_ref), (local_hbm, local_ref), (attr_hbm, attr_ref), (cam_hbm, cam_ref),
        (depth_hbm, depth_ref), (cot_hbm, cot_ref),
    ]
    copies = [pltpu.make_async_copy(src, dst, sem.at[n]) for n, (src, dst) in enumerate(pairs)]
    for copy in copies:
        copy.start()
    for copy in copies:
        copy.wait()
    spread_attributes(attr_ref, wide_ref)
    pos, logscale, quat, logit, sh = split_attributes(wide_ref)
    cam = [jnp.broadcast_to(cam_ref[:, j : j + 1], (8, 128)) for j in range(6)]
    rows = project(pos, logscale, quat, sh, camera_terms(cam[:3], cam[3:]))
    log_opacity = -LOG2E * jnp.log(1.0 + jnp.exp(-logit))
    rows = rows[:5] + [log_opacity] + rows[5:]
    for c in range(8):
        tmp_ref[pl.ds(c, 4, stride=8), :] = rows[c][0:4]
    tmp_ref[32:36, :] = rows[8][0:4]
    rows = tmp_ref[...]
    for z in range(PLANES):
        rows_ref[36 * z : 36 * (z + 1), :] = rows
    before = (
        lax.broadcasted_iota(I32, (SLOTS, SLOTS), 0) < lax.broadcasted_iota(I32, (SLOTS, SLOTS), 1)
    ).astype(F32).astype(BF16)
    every = jnp.ones((SLOTS, SLOTS), BF16)
    oid = lax.broadcasted_iota(I32, (OWNERS, SLOTS), 0)
    pid = lax.broadcasted_iota(I32, (PEERS, SLOTS), 0)
    lane = lax.broadcasted_iota(I32, (1, SLOTS), 1)
    base = jnp.zeros((OWNERS, SLOTS), F32)
    gid = lax.broadcasted_iota(I32, (2 * RANKS, SLOTS), 0)
    table = jnp.zeros((4 * PEERS, 128), F32)
    request = jnp.zeros((4 * RANKS, 128), F32)
    core = (tile_ref[0] // TILES) & 1
    for t in range(TILES):
        owner = owner_ref[:, SLOTS * t : SLOTS * (t + 1)]
        hot = (oid == owner).astype(F32)
        hot16 = hot.astype(BF16)
        count = dot(hot16, before, 1, 0) + base
        base = base + dot(hot16, every, 1, 0)
        rank = jnp.sum(hot * count, axis=0, keepdims=True).astype(I32)
        local = local_ref[t : t + 1, :]
        local_parts = [local & 255, local >> 8]
        slot = lane + (SLOTS * t + 1)
        group = (owner & 7) * 2 + (owner >> 6)
        lanes = ((owner >> 3) & 7) * CAP + rank
        place_ref[0:1, SLOTS * t : SLOTS * (t + 1)] = group
        place_ref[1:2, SLOTS * t : SLOTS * (t + 1)] = lanes
        hot_group = (gid == ((owner & 1) ^ core) * 8 + (owner & 6) + (owner >> 6)).astype(F32)
        vals = jnp.concatenate([hot_group * p.astype(F32) for p in local_parts], axis=0).astype(BF16)
        request = request + dot(vals, (oid == lanes).astype(F32).astype(BF16), 1, 1)
        peer = (owner >> 3) * 2 + (owner & 1)
        lanes = ((owner >> 1) & 3) * CAP + rank
        hot_peer = (pid == peer).astype(F32)
        parts = local_parts + [slot & 255, slot >> 8]
        vals = jnp.concatenate([hot_peer * p.astype(F32) for p in parts], axis=0).astype(BF16)
        table = table + dot(vals, ((oid & 63) == lanes).astype(F32).astype(BF16), 1, 1)
    place_ref[2:3, :] = jnp.full((1, TILES * SLOTS), tile_ref[0], I32)
    n = PEERS
    near_ref[...] = request[0:8] + 256.0 * request[16:24]
    far_ref[...] = request[8:16] + 256.0 * request[24:32]
    names_ref[...] = table[0:n] + 256.0 * table[n : 2 * n]
    inv_ref[...] = (table[2 * n : 3 * n] + 256.0 * table[3 * n :]).astype(I32)
    for c in range(3):
        kept_ref[4 * c : 4 * c + 4, :] = cot_ref[c]
    kept_ref[12:16, :] = jnp.zeros((4, SLOTS), F32)
    kept_ref[12:13, 0:6] = cam_ref[...]
    for t in range(TILES):
        place_ref[3:4, SLOTS * t : SLOTS * (t + 1)] = depth_ref[t : t + 1, :]


def serve_kernel(tile_ref, asked_ref, rows_ref, *refs):
    kept, (out_ref, *outs) = refs[:4], refs[4:]
    for src, dst in zip(kept, outs):
        dst[...] = src[...]
    dev = tile_ref[0] // TILES
    core, mine = dev & 1, dev & 6
    lid = lax.broadcasted_iota(I32, (G_DEV, 256), 0)
    sub = lax.broadcasted_iota(I32, (8, 128), 0)
    near = lax.broadcasted_iota(I32, (8, 128), 1) >> 4
    for half in range(2):
        start = 288 * half
        table = []
        for j in range(4):
            part = [rows_ref[start + 36 * r + 8 * j : start + 36 * r + 8 * j + 8, :] for r in range(8)]
            part.append(rows_ref[pl.ds(start + 32 + j, 8, stride=36), :])
            table.append(jnp.concatenate(part, axis=0))
        table = [x.astype(F32) for x in split3(jnp.concatenate(table, axis=1))]
        table = jnp.concatenate(table + [jnp.zeros((8, G_DEV), F32)], axis=0).astype(BF16)
        for r in range(0, RANKS, 2):
            ids = [asked_ref[pl.ds(8 * r + 8 * (i ^ core) + mine + half, 1), :] for i in range(2)]
            hot = (lid == jnp.concatenate(ids, axis=1).astype(I32)).astype(F32).astype(BF16)
            got = dot(table, hot, 1, 0)
            got = got[0:72] + got[72:144] + got[144:216]
            for i in range(2):
                part = got[:, 128 * i : 128 * (i + 1)]
                main = part[0:8]
                for n in range(1, 8):
                    main = jnp.where(near == n, part[8 * n : 8 * (n + 1)], main)
                at = 9 * (2 * (r + i) + half)
                out_ref[at : at + 8, :] = main
                last = jnp.sum(jnp.where(near == sub, part[64:72], 0.0), axis=0, keepdims=True)
                out_ref[at + 8 : at + 9, :] = last


def pair_ids(back_ref, n):
    left = lax.broadcasted_iota(I32, (8, 128), 1) < 64
    rows = [jnp.broadcast_to(back_ref[5 * (n + i) + 4 : 5 * (n + i) + 5, :], (8, 128)) for i in range(4)]
    pairs = [jnp.where(left, pltpu.roll(rows[i], 64, 1), rows[i + 1]) for i in (0, 2)]
    return jnp.concatenate(pairs, axis=1)[0:1].astype(I32)


def composite_kernel(
    got_ref, place_ref, inv_ref, kept_ref, names_ref, image_ref, out_ref,
    par_ref, alpha_ref, pull_ref, weight_ref, grad_ref,
):
    groups = 2 * RANKS
    last = got_ref[pl.ds(8, groups, stride=9), :]
    sub = lax.broadcasted_iota(I32, (8, 128), 0)
    for b in range(8):
        group = jnp.broadcast_to(place_ref[0:1, 128 * b : 128 * (b + 1)], (8, 128))
        lanes = jnp.broadcast_to(place_ref[1:2, 128 * b : 128 * (b + 1)], (8, 128))
        got = lane_gather(got_ref[0:8, :], lanes)
        for n in range(1, groups):
            got = jnp.where(group == n, lane_gather(got_ref[9 * n : 9 * n + 8, :], lanes), got)
        par_ref[0:8, 128 * b : 128 * (b + 1)] = got
        low = jnp.where(group == sub, lane_gather(last[0:8], lanes), 0.0)
        high = jnp.where(group == sub + 8, lane_gather(last[8:16], lanes), 0.0)
        par_ref[8:9, 128 * b : 128 * (b + 1)] = jnp.sum(low + high, axis=0, keepdims=True)

    q = lax.broadcasted_iota(I32, (16, 128), 1)
    row16 = lax.broadcasted_iota(I32, (16, 128), 0)
    X = (q & 15).astype(F32) - 7.5
    Y = (q >> 4).astype(F32) - 3.5
    mono = jnp.where(row16 == 0, 1.0, 0.0)
    for n, m in enumerate([X, Y, X * X, X * Y, Y * Y]):
        mono = jnp.where(row16 == n + 1, m, mono)
    mono8 = mono[0:8]
    mono16 = mono.astype(BF16)
    mono_twice = jnp.concatenate([mono16, mono16], axis=1)
    ex, ey = 1.0 / (16.0 * TILE_COLS), 1.0 / (16.0 * (TILES * OWNERS // TILE_COLS))

    zero = jnp.zeros((1, SLOTS), F32)
    zero5 = jnp.zeros((5, SLOTS), F32)
    blank = jnp.zeros((8, 128), F32)
    cots = []
    geometry = []
    for t in range(TILES):
        par = [par_ref[c : c + 1, SLOTS * t : SLOTS * (t + 1)] for c in range(9)]
        u, w, ca, cb, cc, log_op = par[:6]
        tile = place_ref[2:3, 0:SLOTS] + t
        cx = ((tile & (TILE_COLS - 1)) * 16 + 8).astype(F32) * ex - 0.5
        dx0 = cx - u
        A, B, C = -0.5 * LOG2E * ca, -LOG2E * cb, -0.5 * LOG2E * cc
        colors = jnp.concatenate([par[6], par[7], par[8], zero5], axis=0)
        chi, cmid, clo = [c.astype(F32) for c in split3(colors)]
        dy0s = []
        coefs, pulls = [], []
        for h in range(2):
            cy = ((tile >> 4) * 16 + 8 * h + 4).astype(F32) * ey - 0.5
            dy0 = cy - w
            dy0s.append(dy0)
            coef = [
                (A * dx0 + B * dy0) * dx0 + C * dy0 * dy0 + log_op,
                (2.0 * A * dx0 + B * dy0) * ex,
                (B * dx0 + 2.0 * C * dy0) * ey,
                A * (ex * ex),
                B * (ex * ey),
                C * (ey * ey),
                zero,
                zero,
            ]
            coefs += [k.astype(F32) for k in split3(jnp.concatenate(coef, axis=0))]
            g = [kept_ref[4 * c + t : 4 * c + t + 1, 128 * h : 128 * (h + 1)] for c in range(3)]
            ghi, gmid, glo = [x.astype(F32) for x in split3(jnp.concatenate(g + [blank[0:5]], axis=0))]
            cots.append((4 * h + t, ghi, gmid))
            pulls.append([ghi, gmid, glo, ghi, gmid, ghi])
        left = coefs + [chi, chi, chi, cmid, cmid, clo] + [jnp.zeros((32, SLOTS), F32)]
        left = jnp.transpose(jnp.concatenate(left, axis=0)).astype(BF16)
        right = []
        for h in range(2):
            right.append([blank] * (3 * h) + [mono8] * 3 + [blank] * (13 - 3 * h))
            right.append([blank] * 6 + pulls[h] + [blank] * 4)
        right = jnp.concatenate([jnp.concatenate(r, axis=0) for r in right], axis=1).astype(BF16)
        both = dot(left, right, 1, 0)
        for h in range(2):
            at = pl.ds(4 * h + t, SLOTS, stride=8)
            alpha_ref[at, :] = both[:, 256 * h : 256 * h + 128]
            pull_ref[at, :] = both[:, 256 * h + 128 : 256 * h + 256]
        geometry.append((ca, cb, cc, dx0, dy0s, chi, cmid))

    depth = jnp.concatenate(
        [place_ref[3:4, SLOTS * t + 128 * h : SLOTS * t + 128 * (h + 1)] for h in range(2) for t in range(TILES)], axis=0
    )
    segments = SEGMENTS
    length = SLOTS // segments

    ones, zeros = jnp.ones((8, 128), F32), jnp.zeros((8, 128), F32)
    trans, behind = [ones] * segments, [zeros] * segments
    for i in range(length):
        for n in range(segments):
            s = n * length + i
            at = slice(8 * s, 8 * s + 8)
            alpha = jnp.where(s < depth, jnp.exp2(alpha_ref[at, :]), 0.0)
            weight = trans[n] * alpha
            alpha_ref[at, :] = alpha
            weight_ref[at, :] = weight
            trans[n] = trans[n] - weight
            behind[n] = behind[n] + weight * pull_ref[at, :]
    starts, rest = [ones], [zeros]
    for n in range(1, segments):
        starts.append(starts[-1] * trans[n - 1])
        rest.insert(0, behind[segments - n] + trans[segments - n] * rest[0])

    for i in range(length):
        for n in range(segments):
            s = (n + 1) * length - 1 - i
            at = slice(8 * s, 8 * s + 8)
            more = pull_ref[at, :] - rest[n]
            rest[n] = rest[n] + alpha_ref[at, :] * more
            weight = starts[n] * weight_ref[at, :]
            weight_ref[at, :] = weight
            pull_ref[at, :] = weight * more

    cots = {th: (ghi, gmid) for th, ghi, gmid in cots}
    for t in range(TILES):
        ca, cb, cc, dx0, dy0s, chi, cmid = geometry[t]
        color_rows = jnp.concatenate([chi, cmid], axis=0).astype(BF16)
        total = [jnp.zeros((1, SLOTS), F32) for _ in range(6)]
        dcolor = jnp.zeros((3, SLOTS), F32)
        for h in range(2):
            th = 4 * h + t
            dy0 = dy0s[h]
            whi, wlo = split2(weight_ref[pl.ds(th, SLOTS, stride=8), :])
            weights = jnp.concatenate([whi, wlo], axis=1)
            ghi, glo = split2(pull_ref[pl.ds(th, SLOTS, stride=8), :])
            grads = jnp.concatenate([ghi, glo], axis=1)
            seen = dot(color_rows, weights, 1, 0)
            seen = seen[:, :128] + seen[:, 128:]
            seen = seen[0:8] + seen[8:16]
            for c in range(3):
                image_ref[c, t : t + 1, 128 * h : 128 * (h + 1)] = seen[c : c + 1]
            cot = jnp.concatenate(cots[th], axis=0).astype(BF16)
            dcol = dot(jnp.concatenate([cot, cot], axis=1), weights, 1, 1)
            dcolor = dcolor + dcol[0:3] + dcol[8:11]
            mom = dot(mono_twice, grads, 1, 1)
            m0 = mom[0:1]
            mx, my = ex * mom[1:2], ey * mom[2:3]
            total[0] = total[0] + m0
            total[1] = total[1] + dx0 * m0 + mx
            total[2] = total[2] + dy0 * m0 + my
            total[3] = total[3] + dx0 * (dx0 * m0 + 2.0 * mx) + (ex * ex) * mom[3:4]
            total[4] = total[4] + dx0 * (dy0 * m0 + my) + dy0 * mx + (ex * ey) * mom[4:5]
            total[5] = total[5] + dy0 * (dy0 * m0 + 2.0 * my) + (ey * ey) * mom[5:6]
        s0, sx, sy, sxx, sxy, syy = total
        made = [ca * sx + cb * sy, cb * sx + cc * sy, -0.5 * sxx, -sxy, -0.5 * syy, s0, dcolor]
        grad_ref[0:9, SLOTS * t : SLOTS * (t + 1)] = jnp.concatenate(made, axis=0)

    inv = inv_ref[...]

    def pick(tables, idx):
        at = jnp.maximum(idx - 1, 0)
        low, high = at & 127, at >> 7
        got = lane_gather(tables[0], low)
        for j in range(1, 8):
            got = jnp.where(high == j, lane_gather(tables[j], low), got)
        return jnp.where(idx > 0, got, 0.0)

    tables = [grad_ref[0:8, 128 * j : 128 * (j + 1)] for j in range(8)]
    last = [jnp.broadcast_to(grad_ref[8:9, 128 * j : 128 * (j + 1)], (8, 128)) for j in range(8)]
    left = lax.broadcasted_iota(I32, (4, 128), 1) < 64
    for n in range(PEERS):
        got = pick(tables, jnp.broadcast_to(inv[n : n + 1], (8, 128)))
        out_ref[5 * n : 5 * n + 4, :] = jnp.where(left, got[0:4], got[4:8])
    more = [pick(last, inv[n : n + 8]) for n in range(0, PEERS, 8)]
    left = lax.broadcasted_iota(I32, (PEERS, 128), 1) < 64
    out_ref[pl.ds(4, PEERS, stride=5), :] = jnp.where(left, jnp.concatenate(more, axis=0), names_ref[...])


def collect_kernel(back_ref, kept_ref, out_ref):
    lid = lax.broadcasted_iota(I32, (G_DEV, 256), 0)
    sub = lax.broadcasted_iota(I32, (8, 128), 0)
    lane = lax.broadcasted_iota(I32, (8, 128), 1)
    near, left = (lane & 63) >> 4, lane < 64
    acc = jnp.zeros((80, G_DEV), F32)
    for n in range(0, PEERS, 4):
        hot = (lid == pair_ids(back_ref, n)).astype(F32).astype(BF16)
        pairs = []
        for i in range(2):
            at = 5 * (n + 2 * i)
            one = jnp.concatenate([back_ref[at : at + 4, :]] * 2, axis=0)
            two = jnp.concatenate([back_ref[at + 5 : at + 9, :]] * 2, axis=0)
            other = jnp.where(left, pltpu.roll(one, 64, 1), two)
            straight = jnp.where(left, one, pltpu.roll(two, 64, 1))
            main = jnp.where(sub < 4, straight, other)
            last_one = jnp.broadcast_to(back_ref[at + 4 : at + 5, :], (8, 128))
            last_two = jnp.broadcast_to(back_ref[at + 9 : at + 10, :], (8, 128))
            last = jnp.where(left, last_one, pltpu.roll(last_two, 64, 1))
            rows = []
            for m, l in zip(split2(main), split2(last)):
                m, l = m.astype(F32), l.astype(F32)
                rows += [jnp.where(near == r, m, 0.0) for r in range(NEAR)] + [jnp.where(near == sub, l, 0.0)]
            pairs.append(jnp.concatenate(rows, axis=0).astype(BF16))
        acc = acc + dot(jnp.concatenate(pairs, axis=1), hot, 1, 1)
    rows = acc[0:40] + acc[40:80]
    tail = kept_ref[12:16, 0:128]
    for r in range(NEAR):
        part = [rows[8 * r : 8 * r + 8, 128 * j : 128 * (j + 1)] for j in range(4)]
        part += [rows[32 + r : 33 + r, 128 * j : 128 * (j + 1)] for j in range(4)] + [tail]
        part = jnp.concatenate(part, axis=0)
        for v in range(VIEWS):
            out_ref[40 * (NEAR * v + r) : 40 * (NEAR * v + r + 1), :] = part


def pull_kernel(parts_ref, attr_ref, image_in_ref, out_ref, image_ref, wide_ref, res_ref, all_ref):
    image_ref[...] = image_in_ref[...]
    for v in range(VIEWS):
        start = 40 * NEAR * v
        total = parts_ref[start : start + 36, :]
        for r in range(1, NEAR):
            total = total + parts_ref[start + 40 * r : start + 40 * r + 36, :]
        all_ref[40 * v : 40 * v + 36, :] = total
        all_ref[40 * v + 36 : 40 * v + 40, :] = parts_ref[start + 36 : start + 40, :]
    spread_attributes(attr_ref, wide_ref)
    pos, logscale, quat, logit, sh = split_attributes(wide_ref)
    total = None
    opacity_grad = None
    for pair in range(VIEWS // 2):
        starts = (80 * pair, 80 * pair + 40)
        cot = [
            jnp.concatenate([all_ref[pl.ds(s + c, 4, stride=8), :] for s in starts], axis=0) for c in range(8)
        ]
        cot.append(jnp.concatenate([all_ref[s + 32 : s + 36, :] for s in starts], axis=0))
        cam = [
            jnp.concatenate(
                [jnp.broadcast_to(all_ref[s + 36 : s + 37, j : j + 1], (4, 128)) for s in starts], axis=0
            )
            for j in range(6)
        ]
        terms = camera_terms(cam[:3], cam[3:])
        _, pull = jax.vjp(lambda a, b, c, d: project(a, b, c, d, terms), pos, logscale, quat, sh)
        grads = jax.tree.leaves(pull(cot[:5] + cot[6:]))
        total = grads if total is None else [a + b for a, b in zip(total, grads)]
        opacity_grad = cot[5] if opacity_grad is None else opacity_grad + cot[5]
    grads = total[:10] + [opacity_grad / (1.0 + jnp.exp(logit))] + total[10:]
    for a in range(ATTR):
        res_ref[4 * a : 4 * a + 4, :] = grads[a][0:4] + grads[a][4:8]
    for j in range(4):
        out_ref[:, 128 * j : 128 * (j + 1)] = res_ref[pl.ds(j, ATTR, stride=4), :]


VMEM = pl.BlockSpec(memory_space=pltpu.VMEM)
SMEM = pl.BlockSpec(memory_space=pltpu.SMEM)
HBM = pl.BlockSpec(memory_space=pl.ANY)
MIB = 1024 * 1024


def call(kernel, outs, args, scratch=(), in_specs=None, limit=24):
    return pl.pallas_call(
        kernel,
        out_shape=[jax.ShapeDtypeStruct(s, d) for s, d in outs],
        in_specs=in_specs or [VMEM] * len(args),
        out_specs=[VMEM] * len(outs),
        scratch_shapes=list(scratch),
        compiler_params=pltpu.CompilerParams(vmem_limit_bytes=limit * MIB),
    )(*args)


def vmem(*shape, dtype=F32):
    return pltpu.VMEM(shape, dtype)


def route(first_tile, owner, local, attributes, camera, depth, cot):
    return call(
        route_kernel,
        [
            ((8, 128), F32), ((8, 128), F32), ((PEERS, 128), I32), ((8, TILES * SLOTS), I32), ((36 * PLANES, 128), F32),
            ((16, SLOTS), F32), ((PEERS, 128), F32),
        ],
        (first_tile, owner, local, attributes, camera, depth, cot),
        [
            vmem(1, TILES * SLOTS, dtype=I32), vmem(TILES, SLOTS, dtype=I32), vmem(ATTR, G_DEV), vmem(1, 6),
            vmem(TILES, SLOTS, dtype=I32), vmem(3, TILES, SLOTS), vmem(ATTR * 8, 128), vmem(36, 128),
            pltpu.SemaphoreType.DMA((6,)),
        ],
        [SMEM] + [HBM] * 6,
        limit=60,
    )


def serve(first_tile, asked, rows, *kept):
    outs = [((18 * RANKS, 128), F32)] + [(k.shape, k.dtype) for k in kept]
    return call(serve_kernel, outs, (first_tile, asked, rows, *kept), (), [SMEM] + [VMEM] * (2 + len(kept)))


def composite(got, place, inv, kept, names):
    big = vmem(SLOTS * 8, 128)
    return call(
        composite_kernel,
        [((3, TILES, 256), F32), ((5 * PEERS, 128), F32)],
        (got, place, inv, kept, names),
        [vmem(16, TILES * SLOTS), big, big, big, vmem(16, TILES * SLOTS)],
    )


def collect(back, kept):
    return call(collect_kernel, [((VIEWS * NEAR * 40, 128), F32)], (back, kept))[0]


def pull_back(parts, attributes, image):
    return call(
        pull_kernel,
        [((ATTR, G_DEV), F32), (image.shape, F32)],
        (parts, attributes, image),
        [vmem(ATTR * 8, 128), vmem(ATTR * 4, 128), vmem(40 * VIEWS, 128)],
    )


def exchange(x, axis, groups):
    return lax.all_to_all(x, axis, split_axis=0, concat_axis=0, tiled=True, axis_index_groups=groups)


ALONG = [[8 * z + r for z in range(PLANES)] for r in range(RANKS)]
PLANE = [[8 * z + r for r in range(RANKS)] for z in range(PLANES)]
ACROSS = [[8 * z + 2 * y + c for z in range(PLANES) for c in range(2)] for y in range(NEAR)]
WITHIN = [[8 * z + 2 * y + c for y in range(NEAR)] for z in range(PLANES) for c in range(2)]
VIEWS_WITHIN = [[OWNERS * v + d for v in range(VIEWS) for d in group] for group in WITHIN]


def per_device(attributes, camera, list_owner, list_local, term_depth, image_cot):
    owner = list_owner.reshape(1, -1)
    first_tile = (lax.axis_index("dev") * TILES).astype(I32).reshape(1)
    near, far, inv, place, rows, kept, names = route(
        first_tile, owner, list_local[0], attributes, camera, term_depth[0], image_cot[0]
    )
    rows = exchange(rows.reshape(PLANES, 1, 4608), "dev", ALONG).reshape(PLANES * 36, 128)
    far = lax.ppermute(far, "dev", [(d, d ^ 1) for d in range(OWNERS)])
    asked = lax.all_gather(jnp.concatenate([near, far]), "dev", axis_index_groups=WITHIN, tiled=True)
    sent, place, inv, kept, names = serve(first_tile, asked, rows, place, inv, kept, names)
    got = exchange(sent.reshape(RANKS, 1, 2304), "dev", PLANE).reshape(18 * RANKS, 128)
    image, grads = composite(got, place, inv, kept, names)
    back = exchange(grads.reshape(PEERS, 1, 640), "dev", ACROSS).reshape(5 * PEERS, 128)
    mine = collect(back, kept)
    parts = exchange(mine.reshape(VIEWS * NEAR, 40, 128), ("view", "dev"), VIEWS_WITHIN)
    grad, image = pull_back(parts.reshape(VIEWS * NEAR * 40, 128), attributes, image)
    return image[None], grad


def solution(mesh):
    in_specs = (
        P(None, "dev"),
        P("view", None),
        P("view", "dev", None, None),
        P("view", "dev", None),
        P("view", "dev", None),
        P("view", None, "dev", None),
    )
    out_specs = (P("view", None, "dev", None), P(None, "dev"))
    return jax.shard_map(
        per_device, mesh=mesh, in_specs=in_specs, out_specs=out_specs, check_vma=False
    )
```

```python
import jax
import jax.numpy as jnp
from jax import lax
from jax.experimental import pallas as pl
from jax.experimental.pallas import tpu as pltpu
from jax.sharding import PartitionSpec as P

TILE_COLS = 16
TILES = 4
SLOTS = 256
CAP = 16
OWNERS = 128
PEERS = 32
NEAR = 4
PLANES = 16
RANKS = 8
SEGMENTS = 4
G_DEV = 512
ATTR = 59
VIEWS = 4
LOG2E = 1.4426950408889634

SH_C0 = 0.28209479177387814
SH_C1 = 0.4886025119029199
SH_C2 = (
    1.0925484305920792,
    -1.0925484305920792,
    0.31539156525252005,
    -1.0925484305920792,
    0.5462742152960396,
)
SH_C3 = (
    -0.5900435899266435,
    2.890611442640554,
    -0.4570457994644658,
    0.3731763325901154,
    -0.4570457994644658,
    1.445305721320277,
    -0.5900435899266435,
)
BLUR = 1e-05

F32 = jnp.float32
BF16 = jnp.bfloat16
I32 = jnp.int32


def camera_terms(angles, shift):
    cosx, sinx = jnp.cos(angles[0]), jnp.sin(angles[0])
    cosy, siny = jnp.cos(angles[1]), jnp.sin(angles[1])
    cosz, sinz = jnp.cos(angles[2]), jnp.sin(angles[2])
    yx = [
        [cosy, siny * sinx, siny * cosx],
        [None, cosx, -sinx],
        [-siny, cosy * sinx, cosy * cosx],
    ]
    rot = [
        [cosz * yx[0][0]] + [cosz * yx[0][j] - sinz * yx[1][j] for j in (1, 2)],
        [sinz * yx[0][0]] + [sinz * yx[0][j] + cosz * yx[1][j] for j in (1, 2)],
        yx[2],
    ]
    centre = [-(rot[0][j] * shift[0] + rot[1][j] * shift[1] + rot[2][j] * shift[2]) for j in range(3)]
    return rot, shift, centre


def harmonics(dirx, diry, dirz):
    xx, yy, zz = (dirx * dirx, diry * diry, dirz * dirz)
    return [
        -SH_C1 * diry,
        SH_C1 * dirz,
        -SH_C1 * dirx,
        SH_C2[0] * dirx * diry,
        SH_C2[1] * diry * dirz,
        SH_C2[2] * (2.0 * zz - xx - yy),
        SH_C2[3] * dirx * dirz,
        SH_C2[4] * (xx - yy),
        SH_C3[0] * diry * (3.0 * xx - yy),
        SH_C3[1] * dirx * diry * dirz,
        SH_C3[2] * diry * (4.0 * zz - xx - yy),
        SH_C3[3] * dirz * (2.0 * zz - 3.0 * xx - 3.0 * yy),
        SH_C3[4] * dirx * (4.0 * zz - xx - yy),
        SH_C3[5] * dirz * (xx - yy),
        SH_C3[6] * dirx * (xx - 3.0 * yy),
    ]


def project(pos, logscale, quat, sh, cam):
    rot, shift, centre = cam
    cpos = [rot[i][0] * pos[0] + rot[i][1] * pos[1] + rot[i][2] * pos[2] + shift[i] for i in range(3)]
    inverse = 1.0 / cpos[2]
    u, w = cpos[0] * inverse, cpos[1] * inverse
    tmat = [
        [inverse * (rot[0][j] - u * rot[2][j]) for j in range(3)],
        [inverse * (rot[1][j] - w * rot[2][j]) for j in range(3)],
    ]
    scale = [jnp.exp(s) for s in logscale]
    norm = lax.rsqrt(quat[0] * quat[0] + quat[1] * quat[1] + quat[2] * quat[2] + quat[3] * quat[3])
    qw, qa, qb, qc = [q * norm for q in quat]
    rgau = [
        [1 - 2 * (qb * qb + qc * qc), 2 * (qa * qb - qw * qc), 2 * (qa * qc + qw * qb)],
        [2 * (qa * qb + qw * qc), 1 - 2 * (qa * qa + qc * qc), 2 * (qb * qc - qw * qa)],
        [2 * (qa * qc - qw * qb), 2 * (qb * qc + qw * qa), 1 - 2 * (qa * qa + qb * qb)],
    ]
    trs = [
        [(tmat[r][0] * rgau[0][k] + tmat[r][1] * rgau[1][k] + tmat[r][2] * rgau[2][k]) * scale[k] for k in range(3)]
        for r in range(2)
    ]
    sig_a = trs[0][0] * trs[0][0] + trs[0][1] * trs[0][1] + trs[0][2] * trs[0][2] + BLUR
    sig_b = trs[0][0] * trs[1][0] + trs[0][1] * trs[1][1] + trs[0][2] * trs[1][2]
    sig_c = trs[1][0] * trs[1][0] + trs[1][1] * trs[1][1] + trs[1][2] * trs[1][2] + BLUR
    det_inv = 1.0 / (sig_a * sig_c - sig_b * sig_b)
    dirs = [pos[j] - centre[j] for j in range(3)]
    norm_inv = lax.rsqrt(dirs[0] * dirs[0] + dirs[1] * dirs[1] + dirs[2] * dirs[2])
    basis = harmonics(dirs[0] * norm_inv, dirs[1] * norm_inv, dirs[2] * norm_inv)
    colors = []
    for ch in range(3):
        color = 0.5 + SH_C0 * sh[ch]
        for k in range(1, 16):
            color = color + basis[k - 1] * sh[3 * k + ch]
        colors.append(color)
    return [u, w, sig_c * det_inv, -sig_b * det_inv, sig_a * det_inv] + colors


def spread_attributes(attr_ref, wide_ref):
    for j in range(4):
        part = attr_ref[:, 128 * j : 128 * (j + 1)]
        wide_ref[pl.ds(j, ATTR, stride=8), :] = part
        wide_ref[pl.ds(j + 4, ATTR, stride=8), :] = part


def split_attributes(wide_ref):
    attrs = [wide_ref[8 * a : 8 * (a + 1), :] for a in range(ATTR)]
    return attrs[0:3], attrs[3:6], attrs[6:10], attrs[10], attrs[11:]


def dot(a, b, ca, cb):
    return lax.dot_general(a, b, (((ca,), (cb,)), ((), ())), preferred_element_type=F32)


def lane_gather(x, idx):
    return jnp.take_along_axis(x, idx, axis=1, mode="promise_in_bounds")


def split2(x):
    hi = x.astype(BF16)
    return hi, (x - hi.astype(F32)).astype(BF16)


def split3(x):
    hi = x.astype(BF16)
    rest = x - hi.astype(F32)
    mid = rest.astype(BF16)
    return hi, mid, (rest - mid.astype(F32)).astype(BF16)


def route_kernel(
    tile_ref, owner_hbm, local_hbm, attr_hbm, cam_hbm, depth_hbm, cot_hbm,
    near_ref, far_ref, inv_ref, place_ref, rows_hbm, kept_ref, names_ref,
    owner_ref, local_ref, attr_ref, cam_ref, depth_ref, cot_ref, wide_ref, tmp_ref, rows_ref, sem,
):
    pairs = [
        (owner_hbm, owner_ref), (local_hbm, local_ref), (attr_hbm, attr_ref), (cam_hbm, cam_ref),
        (depth_hbm, depth_ref), (cot_hbm, cot_ref),
    ]
    copies = [pltpu.make_async_copy(src, dst, sem.at[n]) for n, (src, dst) in enumerate(pairs)]
    for copy in copies:
        copy.start()
    copies[2].wait()
    copies[3].wait()
    spread_attributes(attr_ref, wide_ref)
    pos, logscale, quat, logit, sh = split_attributes(wide_ref)
    cam = [jnp.broadcast_to(cam_ref[:, j : j + 1], (8, 128)) for j in range(6)]
    rows = project(pos, logscale, quat, sh, camera_terms(cam[:3], cam[3:]))
    log_opacity = -LOG2E * jnp.log(1.0 + jnp.exp(-logit))
    rows = rows[:5] + [log_opacity] + rows[5:]
    for c in range(8):
        tmp_ref[pl.ds(c, 4, stride=8), :] = rows[c][0:4]
    tmp_ref[32:36, :] = rows[8][0:4]
    rows = tmp_ref[...]
    for z in range(PLANES):
        rows_ref[36 * z : 36 * (z + 1), :] = rows
    rows_copy = pltpu.make_async_copy(rows_ref, rows_hbm, sem.at[6])
    rows_copy.start()
    for n in (0, 1, 4, 5):
        copies[n].wait()
    before = (
        lax.broadcasted_iota(I32, (SLOTS, SLOTS), 0) < lax.broadcasted_iota(I32, (SLOTS, SLOTS), 1)
    ).astype(F32).astype(BF16)
    every = jnp.ones((SLOTS, SLOTS), BF16)
    oid = lax.broadcasted_iota(I32, (OWNERS, SLOTS), 0)
    pid = lax.broadcasted_iota(I32, (PEERS, SLOTS), 0)
    lane = lax.broadcasted_iota(I32, (1, SLOTS), 1)
    base = jnp.zeros((OWNERS, SLOTS), F32)
    gid = lax.broadcasted_iota(I32, (2 * RANKS, SLOTS), 0)
    table = jnp.zeros((4 * PEERS, 128), F32)
    request = jnp.zeros((4 * RANKS, 128), F32)
    core = (tile_ref[0] // TILES) & 1
    for t in range(TILES):
        owner = owner_ref[:, SLOTS * t : SLOTS * (t + 1)]
        hot = (oid == owner).astype(F32)
        hot16 = hot.astype(BF16)
        count = dot(hot16, before, 1, 0) + base
        base = base + dot(hot16, every, 1, 0)
        rank = jnp.sum(hot * count, axis=0, keepdims=True).astype(I32)
        local = local_ref[t : t + 1, :]
        local_parts = [local & 255, local >> 8]
        slot = lane + (SLOTS * t + 1)
        group = (owner & 7) * 2 + (owner >> 6)
        lanes = ((owner >> 3) & 7) * CAP + rank
        place_ref[0:1, SLOTS * t : SLOTS * (t + 1)] = group
        place_ref[1:2, SLOTS * t : SLOTS * (t + 1)] = lanes
        hot_group = (gid == ((owner & 1) ^ core) * 8 + (owner & 6) + (owner >> 6)).astype(F32)
        vals = jnp.concatenate([hot_group * p.astype(F32) for p in local_parts], axis=0).astype(BF16)
        request = request + dot(vals, (oid == lanes).astype(F32).astype(BF16), 1, 1)
        peer = (owner >> 3) * 2 + (owner & 1)
        lanes = ((owner >> 1) & 3) * CAP + rank
        hot_peer = (pid == peer).astype(F32)
        parts = local_parts + [slot & 255, slot >> 8]
        vals = jnp.concatenate([hot_peer * p.astype(F32) for p in parts], axis=0).astype(BF16)
        table = table + dot(vals, ((oid & 63) == lanes).astype(F32).astype(BF16), 1, 1)
    place_ref[2:3, :] = jnp.full((1, TILES * SLOTS), tile_ref[0], I32)
    n = PEERS
    near_ref[...] = request[0:8] + 256.0 * request[16:24]
    far_ref[...] = request[8:16] + 256.0 * request[24:32]
    names_ref[...] = table[0:n] + 256.0 * table[n : 2 * n]
    inv_ref[...] = (table[2 * n : 3 * n] + 256.0 * table[3 * n :]).astype(I32)
    for c in range(3):
        kept_ref[4 * c : 4 * c + 4, :] = cot_ref[c]
    kept_ref[12:16, :] = jnp.zeros((4, SLOTS), F32)
    kept_ref[12:13, 0:6] = cam_ref[...]
    for t in range(TILES):
        place_ref[3:4, SLOTS * t : SLOTS * (t + 1)] = depth_ref[t : t + 1, :]
    rows_copy.wait()


def serve_kernel(tile_ref, rows_ref, *refs):
    asks, (out_ref, asked_ref) = refs[:NEAR], refs[NEAR:]
    for k in range(NEAR):
        asked_ref[16 * k : 16 * (k + 1), :] = asks[k][...]
    dev = tile_ref[0] // TILES
    core, mine = dev & 1, dev & 6
    lid = lax.broadcasted_iota(I32, (G_DEV, 256), 0)
    sub = lax.broadcasted_iota(I32, (8, 128), 0)
    near = lax.broadcasted_iota(I32, (8, 128), 1) >> 4
    for half in range(2):
        start = 288 * half
        table = []
        for j in range(4):
            part = [rows_ref[start + 36 * r + 8 * j : start + 36 * r + 8 * j + 8, :] for r in range(8)]
            part.append(rows_ref[pl.ds(start + 32 + j, 8, stride=36), :])
            table.append(jnp.concatenate(part, axis=0))
        table = [x.astype(F32) for x in split3(jnp.concatenate(table, axis=1))]
        table = jnp.concatenate(table + [jnp.zeros((8, G_DEV), F32)], axis=0).astype(BF16)
        for r in range(0, RANKS, 2):
            start_row = 16 * (((mine - r) >> 1) & (NEAR - 1)) + mine + half
            ids = [asked_ref[pl.ds(start_row + 8 * (i ^ core), 1), :] for i in range(2)]
            hot = (lid == jnp.concatenate(ids, axis=1).astype(I32)).astype(F32).astype(BF16)
            got = dot(table, hot, 1, 0)
            got = got[0:72] + got[72:144] + got[144:216]
            for i in range(2):
                part = got[:, 128 * i : 128 * (i + 1)]
                main = part[0:8]
                for n in range(1, 8):
                    main = jnp.where(near == n, part[8 * n : 8 * (n + 1)], main)
                at = 9 * (2 * (r + i) + half)
                out_ref[at : at + 8, :] = main
                last = jnp.sum(jnp.where(near == sub, part[64:72], 0.0), axis=0, keepdims=True)
                out_ref[at + 8 : at + 9, :] = last


def pair_ids(back_ref, n):
    left = lax.broadcasted_iota(I32, (8, 128), 1) < 64
    rows = [jnp.broadcast_to(back_ref[5 * (n + i) + 4 : 5 * (n + i) + 5, :], (8, 128)) for i in range(4)]
    pairs = [jnp.where(left, pltpu.roll(rows[i], 64, 1), rows[i + 1]) for i in (0, 2)]
    return jnp.concatenate(pairs, axis=1)[0:1].astype(I32)


def composite_kernel(
    got_ref, place_ref, inv_ref, kept_ref, names_ref, image_ref, out_ref,
    par_ref, alpha_ref, pull_ref, weight_ref, grad_ref,
):
    groups = 2 * RANKS
    last = got_ref[pl.ds(8, groups, stride=9), :]
    sub = lax.broadcasted_iota(I32, (8, 128), 0)
    for b in range(8):
        group = jnp.broadcast_to(place_ref[0:1, 128 * b : 128 * (b + 1)], (8, 128))
        lanes = jnp.broadcast_to(place_ref[1:2, 128 * b : 128 * (b + 1)], (8, 128))
        got = lane_gather(got_ref[0:8, :], lanes)
        for n in range(1, groups):
            got = jnp.where(group == n, lane_gather(got_ref[9 * n : 9 * n + 8, :], lanes), got)
        par_ref[0:8, 128 * b : 128 * (b + 1)] = got
        low = jnp.where(group == sub, lane_gather(last[0:8], lanes), 0.0)
        high = jnp.where(group == sub + 8, lane_gather(last[8:16], lanes), 0.0)
        par_ref[8:9, 128 * b : 128 * (b + 1)] = jnp.sum(low + high, axis=0, keepdims=True)

    q = lax.broadcasted_iota(I32, (16, 128), 1)
    row16 = lax.broadcasted_iota(I32, (16, 128), 0)
    X = (q & 15).astype(F32) - 7.5
    Y = (q >> 4).astype(F32) - 3.5
    mono = jnp.where(row16 == 0, 1.0, 0.0)
    for n, m in enumerate([X, Y, X * X, X * Y, Y * Y]):
        mono = jnp.where(row16 == n + 1, m, mono)
    mono8 = mono[0:8]
    mono16 = mono.astype(BF16)
    mono_twice = jnp.concatenate([mono16, mono16], axis=1)
    ex, ey = 1.0 / (16.0 * TILE_COLS), 1.0 / (16.0 * (TILES * OWNERS // TILE_COLS))

    zero = jnp.zeros((1, SLOTS), F32)
    zero5 = jnp.zeros((5, SLOTS), F32)
    blank = jnp.zeros((8, 128), F32)
    cots = []
    geometry = []
    for t in range(TILES):
        par = [par_ref[c : c + 1, SLOTS * t : SLOTS * (t + 1)] for c in range(9)]
        u, w, ca, cb, cc, log_op = par[:6]
        tile = place_ref[2:3, 0:SLOTS] + t
        cx = ((tile & (TILE_COLS - 1)) * 16 + 8).astype(F32) * ex - 0.5
        dx0 = cx - u
        A, B, C = -0.5 * LOG2E * ca, -LOG2E * cb, -0.5 * LOG2E * cc
        colors = jnp.concatenate([par[6], par[7], par[8], zero5], axis=0)
        chi, cmid, clo = [c.astype(F32) for c in split3(colors)]
        dy0s = []
        coefs, pulls = [], []
        for h in range(2):
            cy = ((tile >> 4) * 16 + 8 * h + 4).astype(F32) * ey - 0.5
            dy0 = cy - w
            dy0s.append(dy0)
            coef = [
                (A * dx0 + B * dy0) * dx0 + C * dy0 * dy0 + log_op,
                (2.0 * A * dx0 + B * dy0) * ex,
                (B * dx0 + 2.0 * C * dy0) * ey,
                A * (ex * ex),
                B * (ex * ey),
                C * (ey * ey),
                zero,
                zero,
            ]
            coefs += [k.astype(F32) for k in split3(jnp.concatenate(coef, axis=0))]
            g = [kept_ref[4 * c + t : 4 * c + t + 1, 128 * h : 128 * (h + 1)] for c in range(3)]
            ghi, gmid, glo = [x.astype(F32) for x in split3(jnp.concatenate(g + [blank[0:5]], axis=0))]
            cots.append((4 * h + t, ghi, gmid))
            pulls.append([ghi, gmid, glo, ghi, gmid, ghi])
        left = coefs + [chi, chi, chi, cmid, cmid, clo] + [jnp.zeros((32, SLOTS), F32)]
        left = jnp.transpose(jnp.concatenate(left, axis=0)).astype(BF16)
        right = []
        for h in range(2):
            right.append([blank] * (3 * h) + [mono8] * 3 + [blank] * (13 - 3 * h))
            right.append([blank] * 6 + pulls[h] + [blank] * 4)
        right = jnp.concatenate([jnp.concatenate(r, axis=0) for r in right], axis=1).astype(BF16)
        both = dot(left, right, 1, 0)
        for h in range(2):
            at = pl.ds(4 * h + t, SLOTS, stride=8)
            alpha_ref[at, :] = both[:, 256 * h : 256 * h + 128]
            pull_ref[at, :] = both[:, 256 * h + 128 : 256 * h + 256]
        geometry.append((ca, cb, cc, dx0, dy0s, chi, cmid))

    depth = jnp.concatenate(
        [place_ref[3:4, SLOTS * t + 128 * h : SLOTS * t + 128 * (h + 1)] for h in range(2) for t in range(TILES)], axis=0
    )
    segments = SEGMENTS
    length = SLOTS // segments

    ones, zeros = jnp.ones((8, 128), F32), jnp.zeros((8, 128), F32)
    trans, behind = [ones] * segments, [zeros] * segments
    for i in range(length):
        for n in range(segments):
            s = n * length + i
            at = slice(8 * s, 8 * s + 8)
            alpha = jnp.where(s < depth, jnp.exp2(alpha_ref[at, :]), 0.0)
            weight = trans[n] * alpha
            alpha_ref[at, :] = alpha
            weight_ref[at, :] = weight
            trans[n] = trans[n] - weight
            behind[n] = behind[n] + weight * pull_ref[at, :]
    starts, rest = [ones], [zeros]
    for n in range(1, segments):
        starts.append(starts[-1] * trans[n - 1])
        rest.insert(0, behind[segments - n] + trans[segments - n] * rest[0])

    for i in range(length):
        for n in range(segments):
            s = (n + 1) * length - 1 - i
            at = slice(8 * s, 8 * s + 8)
            more = pull_ref[at, :] - rest[n]
            rest[n] = rest[n] + alpha_ref[at, :] * more
            weight = starts[n] * weight_ref[at, :]
            weight_ref[at, :] = weight
            pull_ref[at, :] = weight * more

    cots = {th: (ghi, gmid) for th, ghi, gmid in cots}
    for t in range(TILES):
        ca, cb, cc, dx0, dy0s, chi, cmid = geometry[t]
        color_rows = jnp.concatenate([chi, cmid], axis=0).astype(BF16)
        total = [jnp.zeros((1, SLOTS), F32) for _ in range(6)]
        dcolor = jnp.zeros((3, SLOTS), F32)
        for h in range(2):
            th = 4 * h + t
            dy0 = dy0s[h]
            whi, wlo = split2(weight_ref[pl.ds(th, SLOTS, stride=8), :])
            weights = jnp.concatenate([whi, wlo], axis=1)
            ghi, glo = split2(pull_ref[pl.ds(th, SLOTS, stride=8), :])
            grads = jnp.concatenate([ghi, glo], axis=1)
            seen = dot(color_rows, weights, 1, 0)
            seen = seen[:, :128] + seen[:, 128:]
            seen = seen[0:8] + seen[8:16]
            for c in range(3):
                image_ref[c, t : t + 1, 128 * h : 128 * (h + 1)] = seen[c : c + 1]
            cot = jnp.concatenate(cots[th], axis=0).astype(BF16)
            dcol = dot(jnp.concatenate([cot, cot], axis=1), weights, 1, 1)
            dcolor = dcolor + dcol[0:3] + dcol[8:11]
            mom = dot(mono_twice, grads, 1, 1)
            m0 = mom[0:1]
            mx, my = ex * mom[1:2], ey * mom[2:3]
            total[0] = total[0] + m0
            total[1] = total[1] + dx0 * m0 + mx
            total[2] = total[2] + dy0 * m0 + my
            total[3] = total[3] + dx0 * (dx0 * m0 + 2.0 * mx) + (ex * ex) * mom[3:4]
            total[4] = total[4] + dx0 * (dy0 * m0 + my) + dy0 * mx + (ex * ey) * mom[4:5]
            total[5] = total[5] + dy0 * (dy0 * m0 + 2.0 * my) + (ey * ey) * mom[5:6]
        s0, sx, sy, sxx, sxy, syy = total
        made = [ca * sx + cb * sy, cb * sx + cc * sy, -0.5 * sxx, -sxy, -0.5 * syy, s0, dcolor]
        grad_ref[0:9, SLOTS * t : SLOTS * (t + 1)] = jnp.concatenate(made, axis=0)

    inv = inv_ref[...]

    def pick(tables, idx):
        at = jnp.maximum(idx - 1, 0)
        low, high = at & 127, at >> 7
        got = lane_gather(tables[0], low)
        for j in range(1, 8):
            got = jnp.where(high == j, lane_gather(tables[j], low), got)
        return jnp.where(idx > 0, got, 0.0)

    tables = [grad_ref[0:8, 128 * j : 128 * (j + 1)] for j in range(8)]
    last = [jnp.broadcast_to(grad_ref[8:9, 128 * j : 128 * (j + 1)], (8, 128)) for j in range(8)]
    left = lax.broadcasted_iota(I32, (4, 128), 1) < 64
    for n in range(PEERS):
        got = pick(tables, jnp.broadcast_to(inv[n : n + 1], (8, 128)))
        out_ref[5 * n : 5 * n + 4, :] = jnp.where(left, got[0:4], got[4:8])
    more = [pick(last, inv[n : n + 8]) for n in range(0, PEERS, 8)]
    left = lax.broadcasted_iota(I32, (PEERS, 128), 1) < 64
    out_ref[pl.ds(4, PEERS, stride=5), :] = jnp.where(left, jnp.concatenate(more, axis=0), names_ref[...])


def collect_kernel(back_ref, kept_ref, out_ref):
    lid = lax.broadcasted_iota(I32, (G_DEV, 256), 0)
    sub = lax.broadcasted_iota(I32, (8, 128), 0)
    lane = lax.broadcasted_iota(I32, (8, 128), 1)
    near, left = (lane & 63) >> 4, lane < 64
    acc = jnp.zeros((80, G_DEV), F32)
    for n in range(0, PEERS, 4):
        hot = (lid == pair_ids(back_ref, n)).astype(F32).astype(BF16)
        pairs = []
        for i in range(2):
            at = 5 * (n + 2 * i)
            one = jnp.concatenate([back_ref[at : at + 4, :]] * 2, axis=0)
            two = jnp.concatenate([back_ref[at + 5 : at + 9, :]] * 2, axis=0)
            other = jnp.where(left, pltpu.roll(one, 64, 1), two)
            straight = jnp.where(left, one, pltpu.roll(two, 64, 1))
            main = jnp.where(sub < 4, straight, other)
            last_one = jnp.broadcast_to(back_ref[at + 4 : at + 5, :], (8, 128))
            last_two = jnp.broadcast_to(back_ref[at + 9 : at + 10, :], (8, 128))
            last = jnp.where(left, last_one, pltpu.roll(last_two, 64, 1))
            rows = []
            for m, l in zip(split2(main), split2(last)):
                m, l = m.astype(F32), l.astype(F32)
                rows += [jnp.where(near == r, m, 0.0) for r in range(NEAR)] + [jnp.where(near == sub, l, 0.0)]
            pairs.append(jnp.concatenate(rows, axis=0).astype(BF16))
        acc = acc + dot(jnp.concatenate(pairs, axis=1), hot, 1, 1)
    rows = acc[0:40] + acc[40:80]
    tail = kept_ref[12:16, 0:128]
    for r in range(NEAR):
        part = [rows[8 * r : 8 * r + 8, 128 * j : 128 * (j + 1)] for j in range(4)]
        part += [rows[32 + r : 33 + r, 128 * j : 128 * (j + 1)] for j in range(4)] + [tail]
        part = jnp.concatenate(part, axis=0)
        for v in range(VIEWS):
            out_ref[40 * (NEAR * v + r) : 40 * (NEAR * v + r + 1), :] = part


def pull_kernel(parts_ref, attr_ref, image_in_ref, out_ref, image_ref, wide_ref, res_ref, all_ref):
    image_ref[...] = image_in_ref[...]
    for v in range(VIEWS):
        start = 40 * NEAR * v
        total = parts_ref[start : start + 36, :]
        for r in range(1, NEAR):
            total = total + parts_ref[start + 40 * r : start + 40 * r + 36, :]
        all_ref[40 * v : 40 * v + 36, :] = total
        all_ref[40 * v + 36 : 40 * v + 40, :] = parts_ref[start + 36 : start + 40, :]
    spread_attributes(attr_ref, wide_ref)
    pos, logscale, quat, logit, sh = split_attributes(wide_ref)
    total = None
    opacity_grad = None
    for pair in range(VIEWS // 2):
        starts = (80 * pair, 80 * pair + 40)
        cot = [
            jnp.concatenate([all_ref[pl.ds(s + c, 4, stride=8), :] for s in starts], axis=0) for c in range(8)
        ]
        cot.append(jnp.concatenate([all_ref[s + 32 : s + 36, :] for s in starts], axis=0))
        cam = [
            jnp.concatenate(
                [jnp.broadcast_to(all_ref[s + 36 : s + 37, j : j + 1], (4, 128)) for s in starts], axis=0
            )
            for j in range(6)
        ]
        terms = camera_terms(cam[:3], cam[3:])
        _, pull = jax.vjp(lambda a, b, c, d: project(a, b, c, d, terms), pos, logscale, quat, sh)
        grads = jax.tree.leaves(pull(cot[:5] + cot[6:]))
        total = grads if total is None else [a + b for a, b in zip(total, grads)]
        opacity_grad = cot[5] if opacity_grad is None else opacity_grad + cot[5]
    grads = total[:10] + [opacity_grad / (1.0 + jnp.exp(logit))] + total[10:]
    for a in range(ATTR):
        res_ref[4 * a : 4 * a + 4, :] = grads[a][0:4] + grads[a][4:8]
    for j in range(4):
        out_ref[:, 128 * j : 128 * (j + 1)] = res_ref[pl.ds(j, ATTR, stride=4), :]


VMEM = pl.BlockSpec(memory_space=pltpu.VMEM)
SMEM = pl.BlockSpec(memory_space=pltpu.SMEM)
HBM = pl.BlockSpec(memory_space=pl.ANY)
MIB = 1024 * 1024


def call(kernel, outs, args, scratch=(), in_specs=None, out_specs=None, limit=24):
    return pl.pallas_call(
        kernel,
        out_shape=[jax.ShapeDtypeStruct(s, d) for s, d in outs],
        in_specs=in_specs or [VMEM] * len(args),
        out_specs=out_specs or [VMEM] * len(outs),
        scratch_shapes=list(scratch),
        compiler_params=pltpu.CompilerParams(vmem_limit_bytes=limit * MIB),
    )(*args)


def in_hbm(x):
    return pltpu.with_memory_space_constraint(x, pltpu.HBM)


def vmem(*shape, dtype=F32):
    return pltpu.VMEM(shape, dtype)


def route(first_tile, owner, local, attributes, camera, depth, cot):
    return call(
        route_kernel,
        [
            ((8, 128), F32), ((8, 128), F32), ((PEERS, 128), I32), ((8, TILES * SLOTS), I32), ((36 * PLANES, 128), F32),
            ((16, SLOTS), F32), ((PEERS, 128), F32),
        ],
        (first_tile, *[in_hbm(x) for x in (owner, local, attributes, camera, depth, cot)]),
        [
            vmem(1, TILES * SLOTS, dtype=I32), vmem(TILES, SLOTS, dtype=I32), vmem(ATTR, G_DEV), vmem(1, 6),
            vmem(TILES, SLOTS, dtype=I32), vmem(3, TILES, SLOTS), vmem(ATTR * 8, 128), vmem(36, 128),
            vmem(36 * PLANES, 128), pltpu.SemaphoreType.DMA((7,)),
        ],
        [SMEM] + [HBM] * 6,
        [VMEM] * 4 + [HBM] + [VMEM] * 2,
    )


def serve(first_tile, rows, asks):
    return call(
        serve_kernel, [((18 * RANKS, 128), F32)], (first_tile, rows, *asks), [vmem(16 * NEAR, 128)], [SMEM] + [VMEM] * 5
    )[0]


def composite(got, place, inv, kept, names):
    big = vmem(SLOTS * 8, 128)
    return call(
        composite_kernel,
        [((3, TILES, 256), F32), ((5 * PEERS, 128), F32)],
        (got, place, inv, kept, names),
        [vmem(16, TILES * SLOTS), big, big, big, vmem(16, TILES * SLOTS)],
    )


def collect(back, kept):
    return call(collect_kernel, [((VIEWS * NEAR * 40, 128), F32)], (back, kept))[0]


def pull_back(parts, attributes, image):
    return call(
        pull_kernel,
        [((ATTR, G_DEV), F32), (image.shape, F32)],
        (parts, attributes, image),
        [vmem(ATTR * 8, 128), vmem(ATTR * 4, 128), vmem(40 * VIEWS, 128)],
    )


def exchange(x, axis, groups):
    return lax.all_to_all(x, axis, split_axis=0, concat_axis=0, tiled=True, axis_index_groups=groups)


ALONG = [[8 * z + r for z in range(PLANES)] for r in range(RANKS)]
PLANE = [[8 * z + r for r in range(RANKS)] for z in range(PLANES)]
ACROSS = [[8 * z + 2 * y + c for z in range(PLANES) for c in range(2)] for y in range(NEAR)]
WITHIN = [[8 * z + 2 * y + c for y in range(NEAR)] for z in range(PLANES) for c in range(2)]
VIEWS_WITHIN = [[OWNERS * v + d for v in range(VIEWS) for d in group] for group in WITHIN]


def per_device(attributes, camera, list_owner, list_local, term_depth, image_cot):
    owner = list_owner.reshape(1, -1)
    first_tile = (lax.axis_index("dev") * TILES).astype(I32).reshape(1)
    near, far, inv, place, rows, kept, names = route(
        first_tile, owner, list_local[0], attributes, camera, term_depth[0], image_cot[0]
    )
    rows = exchange(rows.reshape(PLANES, 1, 4608), "dev", ALONG).reshape(PLANES * 36, 128)
    far = lax.ppermute(far, "dev", [(d, d ^ 1) for d in range(OWNERS)])
    asks = [jnp.concatenate([near, far])]
    for k in range(1, NEAR):
        asks.append(lax.ppermute(asks[0], "dev", [(d, d // 8 * 8 + (d + 2 * k) % 8) for d in range(OWNERS)]))
    sent = serve(first_tile, rows, asks)
    got = exchange(sent.reshape(RANKS, 1, 2304), "dev", PLANE).reshape(18 * RANKS, 128)
    image, grads = composite(got, place, inv, kept, names)
    back = exchange(grads.reshape(PEERS, 1, 640), "dev", ACROSS).reshape(5 * PEERS, 128)
    mine = collect(back, kept)
    parts = exchange(mine.reshape(VIEWS * NEAR, 40, 128), ("view", "dev"), VIEWS_WITHIN)
    grad, image = pull_back(parts.reshape(VIEWS * NEAR * 40, 128), attributes, image)
    return image[None], grad


def solution(mesh):
    in_specs = (
        P(None, "dev"),
        P("view", None),
        P("view", "dev", None, None),
        P("view", "dev", None),
        P("view", "dev", None),
        P("view", None, "dev", None),
    )
    out_specs = (P("view", None, "dev", None), P(None, "dev"))
    return jax.shard_map(
        per_device, mesh=mesh, in_specs=in_specs, out_specs=out_specs, check_vma=False
    )
```

```python
import jax
import jax.numpy as jnp
from jax import lax
from jax.experimental import pallas as pl
from jax.experimental.pallas import tpu as pltpu
from jax.sharding import PartitionSpec as P

TILE_COLS = 16
TILES = 4
SLOTS = 256
CAP = 16
OWNERS = 128
PEERS = 32
NEAR = 4
PLANES = 16
RANKS = 8
SEGMENTS = 4
G_DEV = 512
ATTR = 59
VIEWS = 4
LOG2E = 1.4426950408889634

SH_C0 = 0.28209479177387814
SH_C1 = 0.4886025119029199
SH_C2 = (
    1.0925484305920792,
    -1.0925484305920792,
    0.31539156525252005,
    -1.0925484305920792,
    0.5462742152960396,
)
SH_C3 = (
    -0.5900435899266435,
    2.890611442640554,
    -0.4570457994644658,
    0.3731763325901154,
    -0.4570457994644658,
    1.445305721320277,
    -0.5900435899266435,
)
BLUR = 1e-05

F32 = jnp.float32
BF16 = jnp.bfloat16
I32 = jnp.int32


def camera_terms(angles, shift):
    cosx, sinx = jnp.cos(angles[0]), jnp.sin(angles[0])
    cosy, siny = jnp.cos(angles[1]), jnp.sin(angles[1])
    cosz, sinz = jnp.cos(angles[2]), jnp.sin(angles[2])
    yx = [
        [cosy, siny * sinx, siny * cosx],
        [None, cosx, -sinx],
        [-siny, cosy * sinx, cosy * cosx],
    ]
    rot = [
        [cosz * yx[0][0]] + [cosz * yx[0][j] - sinz * yx[1][j] for j in (1, 2)],
        [sinz * yx[0][0]] + [sinz * yx[0][j] + cosz * yx[1][j] for j in (1, 2)],
        yx[2],
    ]
    centre = [-(rot[0][j] * shift[0] + rot[1][j] * shift[1] + rot[2][j] * shift[2]) for j in range(3)]
    return rot, shift, centre


def harmonics(dirx, diry, dirz):
    xx, yy, zz = (dirx * dirx, diry * diry, dirz * dirz)
    return [
        -SH_C1 * diry,
        SH_C1 * dirz,
        -SH_C1 * dirx,
        SH_C2[0] * dirx * diry,
        SH_C2[1] * diry * dirz,
        SH_C2[2] * (2.0 * zz - xx - yy),
        SH_C2[3] * dirx * dirz,
        SH_C2[4] * (xx - yy),
        SH_C3[0] * diry * (3.0 * xx - yy),
        SH_C3[1] * dirx * diry * dirz,
        SH_C3[2] * diry * (4.0 * zz - xx - yy),
        SH_C3[3] * dirz * (2.0 * zz - 3.0 * xx - 3.0 * yy),
        SH_C3[4] * dirx * (4.0 * zz - xx - yy),
        SH_C3[5] * dirz * (xx - yy),
        SH_C3[6] * dirx * (xx - 3.0 * yy),
    ]


def project(pos, logscale, quat, sh, cam):
    rot, shift, centre = cam
    cpos = [rot[i][0] * pos[0] + rot[i][1] * pos[1] + rot[i][2] * pos[2] + shift[i] for i in range(3)]
    inverse = 1.0 / cpos[2]
    u, w = cpos[0] * inverse, cpos[1] * inverse
    tmat = [
        [inverse * (rot[0][j] - u * rot[2][j]) for j in range(3)],
        [inverse * (rot[1][j] - w * rot[2][j]) for j in range(3)],
    ]
    scale = [jnp.exp(s) for s in logscale]
    norm = lax.rsqrt(quat[0] * quat[0] + quat[1] * quat[1] + quat[2] * quat[2] + quat[3] * quat[3])
    qw, qa, qb, qc = [q * norm for q in quat]
    rgau = [
        [1 - 2 * (qb * qb + qc * qc), 2 * (qa * qb - qw * qc), 2 * (qa * qc + qw * qb)],
        [2 * (qa * qb + qw * qc), 1 - 2 * (qa * qa + qc * qc), 2 * (qb * qc - qw * qa)],
        [2 * (qa * qc - qw * qb), 2 * (qb * qc + qw * qa), 1 - 2 * (qa * qa + qb * qb)],
    ]
    trs = [
        [(tmat[r][0] * rgau[0][k] + tmat[r][1] * rgau[1][k] + tmat[r][2] * rgau[2][k]) * scale[k] for k in range(3)]
        for r in range(2)
    ]
    sig_a = trs[0][0] * trs[0][0] + trs[0][1] * trs[0][1] + trs[0][2] * trs[0][2] + BLUR
    sig_b = trs[0][0] * trs[1][0] + trs[0][1] * trs[1][1] + trs[0][2] * trs[1][2]
    sig_c = trs[1][0] * trs[1][0] + trs[1][1] * trs[1][1] + trs[1][2] * trs[1][2] + BLUR
    det_inv = 1.0 / (sig_a * sig_c - sig_b * sig_b)
    dirs = [pos[j] - centre[j] for j in range(3)]
    norm_inv = lax.rsqrt(dirs[0] * dirs[0] + dirs[1] * dirs[1] + dirs[2] * dirs[2])
    basis = harmonics(dirs[0] * norm_inv, dirs[1] * norm_inv, dirs[2] * norm_inv)
    colors = []
    for ch in range(3):
        color = 0.5 + SH_C0 * sh[ch]
        for k in range(1, 16):
            color = color + basis[k - 1] * sh[3 * k + ch]
        colors.append(color)
    return [u, w, sig_c * det_inv, -sig_b * det_inv, sig_a * det_inv] + colors


def spread_attributes(attr_ref, wide_ref):
    for j in range(4):
        part = attr_ref[:, 128 * j : 128 * (j + 1)]
        wide_ref[pl.ds(j, ATTR, stride=8), :] = part
        wide_ref[pl.ds(j + 4, ATTR, stride=8), :] = part


def split_attributes(wide_ref):
    attrs = [wide_ref[8 * a : 8 * (a + 1), :] for a in range(ATTR)]
    return attrs[0:3], attrs[3:6], attrs[6:10], attrs[10], attrs[11:]


def dot(a, b, ca, cb):
    return lax.dot_general(a, b, (((ca,), (cb,)), ((), ())), preferred_element_type=F32)


def lane_gather(x, idx):
    return jnp.take_along_axis(x, idx, axis=1, mode="promise_in_bounds")


def split2(x):
    hi = x.astype(BF16)
    return hi, (x - hi.astype(F32)).astype(BF16)


def split3(x):
    hi = x.astype(BF16)
    rest = x - hi.astype(F32)
    mid = rest.astype(BF16)
    return hi, mid, (rest - mid.astype(F32)).astype(BF16)


def route_kernel(
    tile_ref, owner_hbm, local_hbm, attr_hbm, cam_hbm, depth_hbm, cot_hbm,
    asked_ref, inv_ref, place_ref, rows_hbm, kept_ref, names_ref,
    owner_ref, local_ref, attr_ref, cam_ref, depth_ref, cot_ref, wide_ref, tmp_ref, rows_ref, sem,
):
    pairs = [
        (owner_hbm, owner_ref), (local_hbm, local_ref), (attr_hbm, attr_ref), (cam_hbm, cam_ref),
        (depth_hbm, depth_ref), (cot_hbm, cot_ref),
    ]
    copies = [pltpu.make_async_copy(src, dst, sem.at[n]) for n, (src, dst) in enumerate(pairs)]
    for copy in copies:
        copy.start()
    copies[2].wait()
    copies[3].wait()
    spread_attributes(attr_ref, wide_ref)
    pos, logscale, quat, logit, sh = split_attributes(wide_ref)
    cam = [jnp.broadcast_to(cam_ref[:, j : j + 1], (8, 128)) for j in range(6)]
    rows = project(pos, logscale, quat, sh, camera_terms(cam[:3], cam[3:]))
    log_opacity = -LOG2E * jnp.log(1.0 + jnp.exp(-logit))
    rows = rows[:5] + [log_opacity] + rows[5:]
    for c in range(8):
        tmp_ref[pl.ds(c, 4, stride=8), :] = rows[c][0:4]
    tmp_ref[32:36, :] = rows[8][0:4]
    rows = tmp_ref[...]
    for z in range(PLANES):
        rows_ref[36 * z : 36 * (z + 1), :] = rows
    rows_copy = pltpu.make_async_copy(rows_ref, rows_hbm, sem.at[6])
    rows_copy.start()
    for n in (0, 1, 4, 5):
        copies[n].wait()
    before = (
        lax.broadcasted_iota(I32, (SLOTS, SLOTS), 0) < lax.broadcasted_iota(I32, (SLOTS, SLOTS), 1)
    ).astype(F32).astype(BF16)
    every = jnp.ones((SLOTS, SLOTS), BF16)
    oid = lax.broadcasted_iota(I32, (OWNERS, SLOTS), 0)
    pid = lax.broadcasted_iota(I32, (PEERS, SLOTS), 0)
    lane = lax.broadcasted_iota(I32, (1, SLOTS), 1)
    base = jnp.zeros((OWNERS, SLOTS), F32)
    gid = lax.broadcasted_iota(I32, (2 * RANKS, SLOTS), 0)
    table = jnp.zeros((4 * PEERS, 128), F32)
    request = jnp.zeros((4 * RANKS, 128), F32)
    for t in range(TILES):
        owner = owner_ref[:, SLOTS * t : SLOTS * (t + 1)]
        hot = (oid == owner).astype(F32)
        hot16 = hot.astype(BF16)
        count = dot(hot16, before, 1, 0) + base
        base = base + dot(hot16, every, 1, 0)
        rank = jnp.sum(hot * count, axis=0, keepdims=True).astype(I32)
        local = local_ref[t : t + 1, :]
        local_parts = [local & 255, local >> 8]
        slot = lane + (SLOTS * t + 1)
        group = (owner & 7) * 2 + (owner >> 6)
        lanes = ((owner >> 3) & 7) * CAP + rank
        place_ref[0:1, SLOTS * t : SLOTS * (t + 1)] = group
        place_ref[1:2, SLOTS * t : SLOTS * (t + 1)] = lanes
        hot_group = (gid == group).astype(F32)
        vals = jnp.concatenate([hot_group * p.astype(F32) for p in local_parts], axis=0).astype(BF16)
        request = request + dot(vals, (oid == lanes).astype(F32).astype(BF16), 1, 1)
        peer = (owner >> 3) * 2 + (owner & 1)
        lanes = ((owner >> 1) & 3) * CAP + rank
        hot_peer = (pid == peer).astype(F32)
        parts = local_parts + [slot & 255, slot >> 8]
        vals = jnp.concatenate([hot_peer * p.astype(F32) for p in parts], axis=0).astype(BF16)
        table = table + dot(vals, ((oid & 63) == lanes).astype(F32).astype(BF16), 1, 1)
    place_ref[2:3, :] = jnp.full((1, TILES * SLOTS), tile_ref[0], I32)
    n = PEERS
    asked_ref[...] = request[0 : 2 * RANKS] + 256.0 * request[2 * RANKS :]
    names_ref[...] = table[0:n] + 256.0 * table[n : 2 * n]
    inv_ref[...] = (table[2 * n : 3 * n] + 256.0 * table[3 * n :]).astype(I32)
    for c in range(3):
        kept_ref[4 * c : 4 * c + 4, :] = cot_ref[c]
    kept_ref[12:16, :] = jnp.zeros((4, SLOTS), F32)
    kept_ref[12:13, 0:6] = cam_ref[...]
    for t in range(TILES):
        place_ref[3:4, SLOTS * t : SLOTS * (t + 1)] = depth_ref[t : t + 1, :]
    rows_copy.wait()


def serve_kernel(tile_ref, asked_ref, rows_ref, out_ref):
    mine = 2 * ((tile_ref[0] // TILES) & (RANKS - 1))
    lid = lax.broadcasted_iota(I32, (G_DEV, 256), 0)
    sub = lax.broadcasted_iota(I32, (8, 128), 0)
    near = lax.broadcasted_iota(I32, (8, 128), 1) >> 4
    for half in range(2):
        start = 288 * half
        table = []
        for j in range(4):
            part = [rows_ref[start + 36 * r + 8 * j : start + 36 * r + 8 * j + 8, :] for r in range(8)]
            part.append(rows_ref[pl.ds(start + 32 + j, 8, stride=36), :])
            table.append(jnp.concatenate(part, axis=0))
        table = [x.astype(F32) for x in split3(jnp.concatenate(table, axis=1))]
        table = jnp.concatenate(table + [jnp.zeros((8, G_DEV), F32)], axis=0).astype(BF16)
        for r in range(0, RANKS, 2):
            ids = [asked_ref[pl.ds(16 * (r + i) + mine + half, 1), :] for i in range(2)]
            hot = (lid == jnp.concatenate(ids, axis=1).astype(I32)).astype(F32).astype(BF16)
            got = dot(table, hot, 1, 0)
            got = got[0:72] + got[72:144] + got[144:216]
            for i in range(2):
                part = got[:, 128 * i : 128 * (i + 1)]
                main = part[0:8]
                for n in range(1, 8):
                    main = jnp.where(near == n, part[8 * n : 8 * (n + 1)], main)
                at = 9 * (2 * (r + i) + half)
                out_ref[at : at + 8, :] = main
                last = jnp.sum(jnp.where(near == sub, part[64:72], 0.0), axis=0, keepdims=True)
                out_ref[at + 8 : at + 9, :] = last


def pair_ids(back_ref, n):
    left = lax.broadcasted_iota(I32, (8, 128), 1) < 64
    rows = [jnp.broadcast_to(back_ref[5 * (n + i) + 4 : 5 * (n + i) + 5, :], (8, 128)) for i in range(4)]
    pairs = [jnp.where(left, pltpu.roll(rows[i], 64, 1), rows[i + 1]) for i in (0, 2)]
    return jnp.concatenate(pairs, axis=1)[0:1].astype(I32)


def composite_kernel(
    got_ref, place_ref, inv_ref, kept_ref, names_ref, image_ref, out_ref,
    par_ref, alpha_ref, pull_ref, weight_ref, grad_ref,
):
    groups = 2 * RANKS
    last = got_ref[pl.ds(8, groups, stride=9), :]
    sub = lax.broadcasted_iota(I32, (8, 128), 0)
    for b in range(8):
        group = jnp.broadcast_to(place_ref[0:1, 128 * b : 128 * (b + 1)], (8, 128))
        lanes = jnp.broadcast_to(place_ref[1:2, 128 * b : 128 * (b + 1)], (8, 128))
        got = lane_gather(got_ref[0:8, :], lanes)
        for n in range(1, groups):
            got = jnp.where(group == n, lane_gather(got_ref[9 * n : 9 * n + 8, :], lanes), got)
        par_ref[0:8, 128 * b : 128 * (b + 1)] = got
        low = jnp.where(group == sub, lane_gather(last[0:8], lanes), 0.0)
        high = jnp.where(group == sub + 8, lane_gather(last[8:16], lanes), 0.0)
        par_ref[8:9, 128 * b : 128 * (b + 1)] = jnp.sum(low + high, axis=0, keepdims=True)

    q = lax.broadcasted_iota(I32, (16, 128), 1)
    row16 = lax.broadcasted_iota(I32, (16, 128), 0)
    X = (q & 15).astype(F32) - 7.5
    Y = (q >> 4).astype(F32) - 3.5
    mono = jnp.where(row16 == 0, 1.0, 0.0)
    for n, m in enumerate([X, Y, X * X, X * Y, Y * Y]):
        mono = jnp.where(row16 == n + 1, m, mono)
    mono8 = mono[0:8]
    mono16 = mono.astype(BF16)
    mono_twice = jnp.concatenate([mono16, mono16], axis=1)
    ex, ey = 1.0 / (16.0 * TILE_COLS), 1.0 / (16.0 * (TILES * OWNERS // TILE_COLS))

    zero = jnp.zeros((1, SLOTS), F32)
    zero5 = jnp.zeros((5, SLOTS), F32)
    blank = jnp.zeros((8, 128), F32)
    cots = []
    geometry = []
    for t in range(TILES):
        par = [par_ref[c : c + 1, SLOTS * t : SLOTS * (t + 1)] for c in range(9)]
        u, w, ca, cb, cc, log_op = par[:6]
        tile = place_ref[2:3, 0:SLOTS] + t
        cx = ((tile & (TILE_COLS - 1)) * 16 + 8).astype(F32) * ex - 0.5
        dx0 = cx - u
        A, B, C = -0.5 * LOG2E * ca, -LOG2E * cb, -0.5 * LOG2E * cc
        colors = jnp.concatenate([par[6], par[7], par[8], zero5], axis=0)
        chi, cmid, clo = [c.astype(F32) for c in split3(colors)]
        dy0s = []
        coefs, pulls = [], []
        for h in range(2):
            cy = ((tile >> 4) * 16 + 8 * h + 4).astype(F32) * ey - 0.5
            dy0 = cy - w
            dy0s.append(dy0)
            coef = [
                (A * dx0 + B * dy0) * dx0 + C * dy0 * dy0 + log_op,
                (2.0 * A * dx0 + B * dy0) * ex,
                (B * dx0 + 2.0 * C * dy0) * ey,
                A * (ex * ex),
                B * (ex * ey),
                C * (ey * ey),
                zero,
                zero,
            ]
            coefs += [k.astype(F32) for k in split3(jnp.concatenate(coef, axis=0))]
            g = [kept_ref[4 * c + t : 4 * c + t + 1, 128 * h : 128 * (h + 1)] for c in range(3)]
            ghi, gmid, glo = [x.astype(F32) for x in split3(jnp.concatenate(g + [blank[0:5]], axis=0))]
            cots.append((4 * h + t, ghi, gmid))
            pulls.append([ghi, gmid, glo, ghi, gmid, ghi])
        left = coefs + [chi, chi, chi, cmid, cmid, clo] + [jnp.zeros((32, SLOTS), F32)]
        left = jnp.transpose(jnp.concatenate(left, axis=0)).astype(BF16)
        right = []
        for h in range(2):
            right.append([blank] * (3 * h) + [mono8] * 3 + [blank] * (13 - 3 * h))
            right.append([blank] * 6 + pulls[h] + [blank] * 4)
        right = jnp.concatenate([jnp.concatenate(r, axis=0) for r in right], axis=1).astype(BF16)
        both = dot(left, right, 1, 0)
        for h in range(2):
            at = pl.ds(4 * h + t, SLOTS, stride=8)
            alpha_ref[at, :] = both[:, 256 * h : 256 * h + 128]
            pull_ref[at, :] = both[:, 256 * h + 128 : 256 * h + 256]
        geometry.append((ca, cb, cc, dx0, dy0s, chi, cmid))

    depth = jnp.concatenate(
        [place_ref[3:4, SLOTS * t + 128 * h : SLOTS * t + 128 * (h + 1)] for h in range(2) for t in range(TILES)], axis=0
    )
    segments = SEGMENTS
    length = SLOTS // segments

    ones, zeros = jnp.ones((8, 128), F32), jnp.zeros((8, 128), F32)
    trans, behind = [ones] * segments, [zeros] * segments
    for i in range(length):
        for n in range(segments):
            s = n * length + i
            at = slice(8 * s, 8 * s + 8)
            alpha = jnp.where(s < depth, jnp.exp2(alpha_ref[at, :]), 0.0)
            weight = trans[n] * alpha
            alpha_ref[at, :] = alpha
            weight_ref[at, :] = weight
            trans[n] = trans[n] - weight
            behind[n] = behind[n] + weight * pull_ref[at, :]
    starts, rest = [ones], [zeros]
    for n in range(1, segments):
        starts.append(starts[-1] * trans[n - 1])
        rest.insert(0, behind[segments - n] + trans[segments - n] * rest[0])

    for i in range(length):
        for n in range(segments):
            s = (n + 1) * length - 1 - i
            at = slice(8 * s, 8 * s + 8)
            more = pull_ref[at, :] - rest[n]
            rest[n] = rest[n] + alpha_ref[at, :] * more
            weight = starts[n] * weight_ref[at, :]
            weight_ref[at, :] = weight
            pull_ref[at, :] = weight * more

    cots = {th: (ghi, gmid) for th, ghi, gmid in cots}
    for t in range(TILES):
        ca, cb, cc, dx0, dy0s, chi, cmid = geometry[t]
        color_rows = jnp.concatenate([chi, cmid], axis=0).astype(BF16)
        total = [jnp.zeros((1, SLOTS), F32) for _ in range(6)]
        dcolor = jnp.zeros((3, SLOTS), F32)
        for h in range(2):
            th = 4 * h + t
            dy0 = dy0s[h]
            whi, wlo = split2(weight_ref[pl.ds(th, SLOTS, stride=8), :])
            weights = jnp.concatenate([whi, wlo], axis=1)
            ghi, glo = split2(pull_ref[pl.ds(th, SLOTS, stride=8), :])
            grads = jnp.concatenate([ghi, glo], axis=1)
            seen = dot(color_rows, weights, 1, 0)
            seen = seen[:, :128] + seen[:, 128:]
            seen = seen[0:8] + seen[8:16]
            for c in range(3):
                image_ref[c, t : t + 1, 128 * h : 128 * (h + 1)] = seen[c : c + 1]
            cot = jnp.concatenate(cots[th], axis=0).astype(BF16)
            dcol = dot(jnp.concatenate([cot, cot], axis=1), weights, 1, 1)
            dcolor = dcolor + dcol[0:3] + dcol[8:11]
            mom = dot(mono_twice, grads, 1, 1)
            m0 = mom[0:1]
            mx, my = ex * mom[1:2], ey * mom[2:3]
            total[0] = total[0] + m0
            total[1] = total[1] + dx0 * m0 + mx
            total[2] = total[2] + dy0 * m0 + my
            total[3] = total[3] + dx0 * (dx0 * m0 + 2.0 * mx) + (ex * ex) * mom[3:4]
            total[4] = total[4] + dx0 * (dy0 * m0 + my) + dy0 * mx + (ex * ey) * mom[4:5]
            total[5] = total[5] + dy0 * (dy0 * m0 + 2.0 * my) + (ey * ey) * mom[5:6]
        s0, sx, sy, sxx, sxy, syy = total
        made = [ca * sx + cb * sy, cb * sx + cc * sy, -0.5 * sxx, -sxy, -0.5 * syy, s0, dcolor]
        grad_ref[0:9, SLOTS * t : SLOTS * (t + 1)] = jnp.concatenate(made, axis=0)

    inv = inv_ref[...]

    def pick(tables, idx):
        at = jnp.maximum(idx - 1, 0)
        low, high = at & 127, at >> 7
        got = lane_gather(tables[0], low)
        for j in range(1, 8):
            got = jnp.where(high == j, lane_gather(tables[j], low), got)
        return jnp.where(idx > 0, got, 0.0)

    tables = [grad_ref[0:8, 128 * j : 128 * (j + 1)] for j in range(8)]
    last = [jnp.broadcast_to(grad_ref[8:9, 128 * j : 128 * (j + 1)], (8, 128)) for j in range(8)]
    left = lax.broadcasted_iota(I32, (4, 128), 1) < 64
    for n in range(PEERS):
        got = pick(tables, jnp.broadcast_to(inv[n : n + 1], (8, 128)))
        out_ref[5 * n : 5 * n + 4, :] = jnp.where(left, got[0:4], got[4:8])
    more = [pick(last, inv[n : n + 8]) for n in range(0, PEERS, 8)]
    left = lax.broadcasted_iota(I32, (PEERS, 128), 1) < 64
    out_ref[pl.ds(4, PEERS, stride=5), :] = jnp.where(left, jnp.concatenate(more, axis=0), names_ref[...])


def collect_kernel(back_ref, kept_ref, out_ref):
    lid = lax.broadcasted_iota(I32, (G_DEV, 256), 0)
    sub = lax.broadcasted_iota(I32, (8, 128), 0)
    lane = lax.broadcasted_iota(I32, (8, 128), 1)
    near, left = (lane & 63) >> 4, lane < 64
    acc = jnp.zeros((80, G_DEV), F32)
    for n in range(0, PEERS, 4):
        hot = (lid == pair_ids(back_ref, n)).astype(F32).astype(BF16)
        pairs = []
        for i in range(2):
            at = 5 * (n + 2 * i)
            one = jnp.concatenate([back_ref[at : at + 4, :]] * 2, axis=0)
            two = jnp.concatenate([back_ref[at + 5 : at + 9, :]] * 2, axis=0)
            other = jnp.where(left, pltpu.roll(one, 64, 1), two)
            straight = jnp.where(left, one, pltpu.roll(two, 64, 1))
            main = jnp.where(sub < 4, straight, other)
            last_one = jnp.broadcast_to(back_ref[at + 4 : at + 5, :], (8, 128))
            last_two = jnp.broadcast_to(back_ref[at + 9 : at + 10, :], (8, 128))
            last = jnp.where(left, last_one, pltpu.roll(last_two, 64, 1))
            rows = []
            for m, l in zip(split2(main), split2(last)):
                m, l = m.astype(F32), l.astype(F32)
                rows += [jnp.where(near == r, m, 0.0) for r in range(NEAR)] + [jnp.where(near == sub, l, 0.0)]
            pairs.append(jnp.concatenate(rows, axis=0).astype(BF16))
        acc = acc + dot(jnp.concatenate(pairs, axis=1), hot, 1, 1)
    rows = acc[0:40] + acc[40:80]
    tail = kept_ref[12:16, 0:128]
    for r in range(NEAR):
        part = [rows[8 * r : 8 * r + 8, 128 * j : 128 * (j + 1)] for j in range(4)]
        part += [rows[32 + r : 33 + r, 128 * j : 128 * (j + 1)] for j in range(4)] + [tail]
        part = jnp.concatenate(part, axis=0)
        for v in range(VIEWS):
            out_ref[40 * (NEAR * v + r) : 40 * (NEAR * v + r + 1), :] = part


def pull_kernel(parts_ref, attr_ref, image_in_ref, out_ref, image_ref, wide_ref, res_ref, all_ref):
    image_ref[...] = image_in_ref[...]
    for v in range(VIEWS):
        start = 40 * NEAR * v
        total = parts_ref[start : start + 36, :]
        for r in range(1, NEAR):
            total = total + parts_ref[start + 40 * r : start + 40 * r + 36, :]
        all_ref[40 * v : 40 * v + 36, :] = total
        all_ref[40 * v + 36 : 40 * v + 40, :] = parts_ref[start + 36 : start + 40, :]
    spread_attributes(attr_ref, wide_ref)
    pos, logscale, quat, logit, sh = split_attributes(wide_ref)
    total = None
    opacity_grad = None
    for pair in range(VIEWS // 2):
        starts = (80 * pair, 80 * pair + 40)
        cot = [
            jnp.concatenate([all_ref[pl.ds(s + c, 4, stride=8), :] for s in starts], axis=0) for c in range(8)
        ]
        cot.append(jnp.concatenate([all_ref[s + 32 : s + 36, :] for s in starts], axis=0))
        cam = [
            jnp.concatenate(
                [jnp.broadcast_to(all_ref[s + 36 : s + 37, j : j + 1], (4, 128)) for s in starts], axis=0
            )
            for j in range(6)
        ]
        terms = camera_terms(cam[:3], cam[3:])
        _, pull = jax.vjp(lambda a, b, c, d: project(a, b, c, d, terms), pos, logscale, quat, sh)
        grads = jax.tree.leaves(pull(cot[:5] + cot[6:]))
        total = grads if total is None else [a + b for a, b in zip(total, grads)]
        opacity_grad = cot[5] if opacity_grad is None else opacity_grad + cot[5]
    grads = total[:10] + [opacity_grad / (1.0 + jnp.exp(logit))] + total[10:]
    for a in range(ATTR):
        res_ref[4 * a : 4 * a + 4, :] = grads[a][0:4] + grads[a][4:8]
    for j in range(4):
        out_ref[:, 128 * j : 128 * (j + 1)] = res_ref[pl.ds(j, ATTR, stride=4), :]


VMEM = pl.BlockSpec(memory_space=pltpu.VMEM)
SMEM = pl.BlockSpec(memory_space=pltpu.SMEM)
HBM = pl.BlockSpec(memory_space=pl.ANY)
MIB = 1024 * 1024


def call(kernel, outs, args, scratch=(), in_specs=None, out_specs=None, limit=24):
    return pl.pallas_call(
        kernel,
        out_shape=[jax.ShapeDtypeStruct(s, d) for s, d in outs],
        in_specs=in_specs or [VMEM] * len(args),
        out_specs=out_specs or [VMEM] * len(outs),
        scratch_shapes=list(scratch),
        compiler_params=pltpu.CompilerParams(vmem_limit_bytes=limit * MIB),
    )(*args)


def in_hbm(x):
    return pltpu.with_memory_space_constraint(x, pltpu.HBM)


def vmem(*shape, dtype=F32):
    return pltpu.VMEM(shape, dtype)


def route(first_tile, owner, local, attributes, camera, depth, cot):
    return call(
        route_kernel,
        [
            ((2 * RANKS, 128), F32), ((PEERS, 128), I32), ((8, TILES * SLOTS), I32), ((36 * PLANES, 128), F32),
            ((16, SLOTS), F32), ((PEERS, 128), F32),
        ],
        (first_tile, *[in_hbm(x) for x in (owner, local, attributes, camera, depth, cot)]),
        [
            vmem(1, TILES * SLOTS, dtype=I32), vmem(TILES, SLOTS, dtype=I32), vmem(ATTR, G_DEV), vmem(1, 6),
            vmem(TILES, SLOTS, dtype=I32), vmem(3, TILES, SLOTS), vmem(ATTR * 8, 128), vmem(36, 128),
            vmem(36 * PLANES, 128), pltpu.SemaphoreType.DMA((7,)),
        ],
        [SMEM] + [HBM] * 6,
        [VMEM] * 3 + [HBM] + [VMEM] * 2,
    )


def serve(first_tile, asked, rows):
    return call(
        serve_kernel, [((18 * RANKS, 128), F32)], (first_tile, asked, rows), (), [SMEM] + [VMEM] * 2
    )[0]


def composite(got, place, inv, kept, names):
    big = vmem(SLOTS * 8, 128)
    return call(
        composite_kernel,
        [((3, TILES, 256), F32), ((5 * PEERS, 128), F32)],
        (got, place, inv, kept, names),
        [vmem(16, TILES * SLOTS), big, big, big, vmem(16, TILES * SLOTS)],
    )


def collect(back, kept):
    return call(collect_kernel, [((VIEWS * NEAR * 40, 128), F32)], (back, kept))[0]


def pull_back(parts, attributes, image):
    return call(
        pull_kernel,
        [((ATTR, G_DEV), F32), (image.shape, F32)],
        (parts, attributes, image),
        [vmem(ATTR * 8, 128), vmem(ATTR * 4, 128), vmem(40 * VIEWS, 128)],
    )


def exchange(x, axis, groups):
    return lax.all_to_all(x, axis, split_axis=0, concat_axis=0, tiled=True, axis_index_groups=groups)


ALONG = [[8 * z + r for z in range(PLANES)] for r in range(RANKS)]
PLANE = [[8 * z + r for r in range(RANKS)] for z in range(PLANES)]
ACROSS = [[8 * z + 2 * y + c for z in range(PLANES) for c in range(2)] for y in range(NEAR)]
WITHIN = [[8 * z + 2 * y + c for y in range(NEAR)] for z in range(PLANES) for c in range(2)]
VIEWS_WITHIN = [[OWNERS * v + d for v in range(VIEWS) for d in group] for group in WITHIN]


def per_device(attributes, camera, list_owner, list_local, term_depth, image_cot):
    owner = list_owner.reshape(1, -1)
    first_tile = (lax.axis_index("dev") * TILES).astype(I32).reshape(1)
    asked, inv, place, rows, kept, names = route(
        first_tile, owner, list_local[0], attributes, camera, term_depth[0], image_cot[0]
    )
    rows = exchange(rows.reshape(PLANES, 1, 4608), "dev", ALONG).reshape(PLANES * 36, 128)
    asked = lax.all_gather(asked, "dev", axis_index_groups=PLANE, tiled=True)
    sent = serve(first_tile, asked, rows)
    got = exchange(sent.reshape(RANKS, 1, 2304), "dev", PLANE).reshape(18 * RANKS, 128)
    image, grads = composite(got, place, inv, kept, names)
    back = exchange(grads.reshape(PEERS, 1, 640), "dev", ACROSS).reshape(5 * PEERS, 128)
    mine = collect(back, kept)
    parts = exchange(mine.reshape(VIEWS * NEAR, 40, 128), ("view", "dev"), VIEWS_WITHIN)
    grad, image = pull_back(parts.reshape(VIEWS * NEAR * 40, 128), attributes, image)
    return image[None], grad


def solution(mesh):
    in_specs = (
        P(None, "dev"),
        P("view", None),
        P("view", "dev", None, None),
        P("view", "dev", None),
        P("view", "dev", None),
        P("view", None, "dev", None),
    )
    out_specs = (P("view", None, "dev", None), P(None, "dev"))
    return jax.shard_map(
        per_device, mesh=mesh, in_specs=in_specs, out_specs=out_specs, check_vma=False
    )
```

```python
import jax
import jax.numpy as jnp
from jax import lax
from jax.experimental import pallas as pl
from jax.experimental.pallas import tpu as pltpu
from jax.sharding import PartitionSpec as P

TILE_COLS = 16
TILES = 4
SLOTS = 256
CAP = 16
OWNERS = 128
PEERS = 32
NEAR = 4
PLANES = 16
RANKS = 8
SEGMENTS = 8
RING = (0, 2, 4, 6, 7, 5, 3, 1)
G_DEV = 512
ATTR = 59
VIEWS = 4
LOG2E = 1.4426950408889634

SH_C0 = 0.28209479177387814
SH_C1 = 0.4886025119029199
SH_C2 = (
    1.0925484305920792,
    -1.0925484305920792,
    0.31539156525252005,
    -1.0925484305920792,
    0.5462742152960396,
)
SH_C3 = (
    -0.5900435899266435,
    2.890611442640554,
    -0.4570457994644658,
    0.3731763325901154,
    -0.4570457994644658,
    1.445305721320277,
    -0.5900435899266435,
)
BLUR = 1e-05

F32 = jnp.float32
BF16 = jnp.bfloat16
I32 = jnp.int32


def camera_terms(angles, shift):
    cosx, sinx = jnp.cos(angles[0]), jnp.sin(angles[0])
    cosy, siny = jnp.cos(angles[1]), jnp.sin(angles[1])
    cosz, sinz = jnp.cos(angles[2]), jnp.sin(angles[2])
    yx = [
        [cosy, siny * sinx, siny * cosx],
        [None, cosx, -sinx],
        [-siny, cosy * sinx, cosy * cosx],
    ]
    rot = [
        [cosz * yx[0][0]] + [cosz * yx[0][j] - sinz * yx[1][j] for j in (1, 2)],
        [sinz * yx[0][0]] + [sinz * yx[0][j] + cosz * yx[1][j] for j in (1, 2)],
        yx[2],
    ]
    centre = [-(rot[0][j] * shift[0] + rot[1][j] * shift[1] + rot[2][j] * shift[2]) for j in range(3)]
    return rot, shift, centre


def harmonics(dirx, diry, dirz):
    xx, yy, zz = (dirx * dirx, diry * diry, dirz * dirz)
    return [
        -SH_C1 * diry,
        SH_C1 * dirz,
        -SH_C1 * dirx,
        SH_C2[0] * dirx * diry,
        SH_C2[1] * diry * dirz,
        SH_C2[2] * (2.0 * zz - xx - yy),
        SH_C2[3] * dirx * dirz,
        SH_C2[4] * (xx - yy),
        SH_C3[0] * diry * (3.0 * xx - yy),
        SH_C3[1] * dirx * diry * dirz,
        SH_C3[2] * diry * (4.0 * zz - xx - yy),
        SH_C3[3] * dirz * (2.0 * zz - 3.0 * xx - 3.0 * yy),
        SH_C3[4] * dirx * (4.0 * zz - xx - yy),
        SH_C3[5] * dirz * (xx - yy),
        SH_C3[6] * dirx * (xx - 3.0 * yy),
    ]


def project(pos, logscale, quat, sh, cam):
    rot, shift, centre = cam
    cpos = [rot[i][0] * pos[0] + rot[i][1] * pos[1] + rot[i][2] * pos[2] + shift[i] for i in range(3)]
    inverse = 1.0 / cpos[2]
    u, w = cpos[0] * inverse, cpos[1] * inverse
    tmat = [
        [inverse * (rot[0][j] - u * rot[2][j]) for j in range(3)],
        [inverse * (rot[1][j] - w * rot[2][j]) for j in range(3)],
    ]
    scale = [jnp.exp(s) for s in logscale]
    norm = lax.rsqrt(quat[0] * quat[0] + quat[1] * quat[1] + quat[2] * quat[2] + quat[3] * quat[3])
    qw, qa, qb, qc = [q * norm for q in quat]
    rgau = [
        [1 - 2 * (qb * qb + qc * qc), 2 * (qa * qb - qw * qc), 2 * (qa * qc + qw * qb)],
        [2 * (qa * qb + qw * qc), 1 - 2 * (qa * qa + qc * qc), 2 * (qb * qc - qw * qa)],
        [2 * (qa * qc - qw * qb), 2 * (qb * qc + qw * qa), 1 - 2 * (qa * qa + qb * qb)],
    ]
    trs = [
        [(tmat[r][0] * rgau[0][k] + tmat[r][1] * rgau[1][k] + tmat[r][2] * rgau[2][k]) * scale[k] for k in range(3)]
        for r in range(2)
    ]
    sig_a = trs[0][0] * trs[0][0] + trs[0][1] * trs[0][1] + trs[0][2] * trs[0][2] + BLUR
    sig_b = trs[0][0] * trs[1][0] + trs[0][1] * trs[1][1] + trs[0][2] * trs[1][2]
    sig_c = trs[1][0] * trs[1][0] + trs[1][1] * trs[1][1] + trs[1][2] * trs[1][2] + BLUR
    det_inv = 1.0 / (sig_a * sig_c - sig_b * sig_b)
    dirs = [pos[j] - centre[j] for j in range(3)]
    norm_inv = lax.rsqrt(dirs[0] * dirs[0] + dirs[1] * dirs[1] + dirs[2] * dirs[2])
    basis = harmonics(dirs[0] * norm_inv, dirs[1] * norm_inv, dirs[2] * norm_inv)
    colors = []
    for ch in range(3):
        color = 0.5 + SH_C0 * sh[ch]
        for k in range(1, 16):
            color = color + basis[k - 1] * sh[3 * k + ch]
        colors.append(color)
    return [u, w, sig_c * det_inv, -sig_b * det_inv, sig_a * det_inv] + colors


def spread_attributes(attr_ref, wide_ref):
    for j in range(4):
        part = attr_ref[:, 128 * j : 128 * (j + 1)]
        wide_ref[pl.ds(j, ATTR, stride=8), :] = part
        wide_ref[pl.ds(j + 4, ATTR, stride=8), :] = part


def split_attributes(wide_ref):
    attrs = [wide_ref[8 * a : 8 * (a + 1), :] for a in range(ATTR)]
    return attrs[0:3], attrs[3:6], attrs[6:10], attrs[10], attrs[11:]


def dot(a, b, ca, cb):
    return lax.dot_general(a, b, (((ca,), (cb,)), ((), ())), preferred_element_type=F32)


def lane_gather(x, idx):
    return jnp.take_along_axis(x, idx, axis=1, mode="promise_in_bounds")


def split2(x):
    hi = x.astype(BF16)
    return hi, (x - hi.astype(F32)).astype(BF16)


def split3(x):
    hi = x.astype(BF16)
    rest = x - hi.astype(F32)
    mid = rest.astype(BF16)
    return hi, mid, (rest - mid.astype(F32)).astype(BF16)


def route_kernel(
    tile_ref, owner_hbm, local_hbm, attr_hbm, cam_hbm, depth_hbm, cot_hbm,
    asked_ref, inv_ref, place_ref, rows_hbm, kept_ref, names_ref,
    owner_ref, local_ref, attr_ref, cam_ref, depth_ref, cot_ref, wide_ref, tmp_ref, rows_ref, sem,
):
    pairs = [
        (owner_hbm, owner_ref), (local_hbm, local_ref), (attr_hbm, attr_ref), (cam_hbm, cam_ref),
        (depth_hbm, depth_ref), (cot_hbm, cot_ref),
    ]
    copies = [pltpu.make_async_copy(src, dst, sem.at[n]) for n, (src, dst) in enumerate(pairs)]
    for copy in copies:
        copy.start()
    copies[2].wait()
    copies[3].wait()
    spread_attributes(attr_ref, wide_ref)
    pos, logscale, quat, logit, sh = split_attributes(wide_ref)
    cam = [jnp.broadcast_to(cam_ref[:, j : j + 1], (8, 128)) for j in range(6)]
    rows = project(pos, logscale, quat, sh, camera_terms(cam[:3], cam[3:]))
    log_opacity = -LOG2E * jnp.log(1.0 + jnp.exp(-logit))
    rows = rows[:5] + [log_opacity] + rows[5:]
    for c in range(8):
        tmp_ref[pl.ds(c, 4, stride=8), :] = rows[c][0:4]
    tmp_ref[32:36, :] = rows[8][0:4]
    rows = tmp_ref[...]
    for z in range(PLANES):
        rows_ref[36 * z : 36 * (z + 1), :] = rows
    rows_copy = pltpu.make_async_copy(rows_ref, rows_hbm, sem.at[6])
    rows_copy.start()
    for n in (0, 1, 4, 5):
        copies[n].wait()
    before = (
        lax.broadcasted_iota(I32, (SLOTS, SLOTS), 0) < lax.broadcasted_iota(I32, (SLOTS, SLOTS), 1)
    ).astype(F32).astype(BF16)
    every = jnp.ones((SLOTS, SLOTS), BF16)
    oid = lax.broadcasted_iota(I32, (OWNERS, SLOTS), 0)
    pid = lax.broadcasted_iota(I32, (PEERS, SLOTS), 0)
    lane = lax.broadcasted_iota(I32, (1, SLOTS), 1)
    base = jnp.zeros((OWNERS, SLOTS), F32)
    gid = lax.broadcasted_iota(I32, (2 * RANKS, SLOTS), 0)
    table = jnp.zeros((4 * PEERS, 128), F32)
    request = jnp.zeros((4 * RANKS, 128), F32)
    for t in range(TILES):
        owner = owner_ref[:, SLOTS * t : SLOTS * (t + 1)]
        hot = (oid == owner).astype(F32)
        hot16 = hot.astype(BF16)
        count = dot(hot16, before, 1, 0) + base
        base = base + dot(hot16, every, 1, 0)
        rank = jnp.sum(hot * count, axis=0, keepdims=True).astype(I32)
        local = local_ref[t : t + 1, :]
        local_parts = [local & 255, local >> 8]
        slot = lane + (SLOTS * t + 1)
        group = (owner & 7) * 2 + (owner >> 6)
        lanes = ((owner >> 3) & 7) * CAP + rank
        place_ref[0:1, SLOTS * t : SLOTS * (t + 1)] = group
        place_ref[1:2, SLOTS * t : SLOTS * (t + 1)] = lanes
        hot_group = (gid == group).astype(F32)
        vals = jnp.concatenate([hot_group * p.astype(F32) for p in local_parts], axis=0).astype(BF16)
        request = request + dot(vals, (oid == lanes).astype(F32).astype(BF16), 1, 1)
        peer = (owner >> 3) * 2 + (owner & 1)
        lanes = ((owner >> 1) & 3) * CAP + rank
        hot_peer = (pid == peer).astype(F32)
        parts = local_parts + [slot & 255, slot >> 8]
        vals = jnp.concatenate([hot_peer * p.astype(F32) for p in parts], axis=0).astype(BF16)
        table = table + dot(vals, ((oid & 63) == lanes).astype(F32).astype(BF16), 1, 1)
    place_ref[2:3, :] = jnp.full((1, TILES * SLOTS), tile_ref[0], I32)
    n = PEERS
    asked_ref[...] = request[0 : 2 * RANKS] + 256.0 * request[2 * RANKS :]
    names_ref[...] = table[0:n] + 256.0 * table[n : 2 * n]
    inv_ref[...] = (table[2 * n : 3 * n] + 256.0 * table[3 * n :]).astype(I32)
    for c in range(3):
        kept_ref[4 * c : 4 * c + 4, :] = cot_ref[c]
    kept_ref[12:16, :] = jnp.zeros((4, SLOTS), F32)
    kept_ref[12:13, 0:6] = cam_ref[...]
    for t in range(TILES):
        place_ref[3:4, SLOTS * t : SLOTS * (t + 1)] = depth_ref[t : t + 1, :]
    rows_copy.wait()


def serve_kernel(tile_ref, asked_ref, rows_ref, out_ref):
    mine = 2 * ((tile_ref[0] // TILES) & (RANKS - 1))
    lid = lax.broadcasted_iota(I32, (G_DEV, 256), 0).astype(jnp.int16)
    sub = lax.broadcasted_iota(I32, (8, 128), 0)
    near = lax.broadcasted_iota(I32, (8, 128), 1) >> 4
    for half in range(2):
        start = 288 * half
        table = []
        for j in range(4):
            part = [rows_ref[start + 36 * r + 8 * j : start + 36 * r + 8 * j + 8, :] for r in range(8)]
            part.append(rows_ref[pl.ds(start + 32 + j, 8, stride=36), :])
            table.append(jnp.concatenate(part, axis=0))
        table = [x.astype(F32) for x in split3(jnp.concatenate(table, axis=1))]
        table = jnp.concatenate(table + [jnp.zeros((8, G_DEV), F32)], axis=0).astype(BF16)
        for r in range(0, RANKS, 2):
            ids = [asked_ref[pl.ds(16 * RING.index(r + i) + mine + half, 1), :] for i in range(2)]
            hot = one_hot(lid, jnp.concatenate(ids, axis=1).astype(I32))
            got = dot(table, hot, 1, 0)
            got = got[0:72] + got[72:144] + got[144:216]
            for i in range(2):
                part = got[:, 128 * i : 128 * (i + 1)]
                main = part[0:8]
                for n in range(1, 8):
                    main = jnp.where(near == n, part[8 * n : 8 * (n + 1)], main)
                at = 9 * (2 * (r + i) + half)
                out_ref[at : at + 8, :] = main
                last = jnp.sum(jnp.where(near == sub, part[64:72], 0.0), axis=0, keepdims=True)
                out_ref[at + 8 : at + 9, :] = last


def one_hot(lid, ids):
    ids = jnp.broadcast_to(ids, (16, 256)).astype(jnp.int16)
    same = lid == jnp.concatenate([ids] * (G_DEV // 16), axis=0)
    return jnp.where(same, jnp.ones(lid.shape, BF16), jnp.zeros(lid.shape, BF16))


def pair_ids(back_ref, n):
    left = lax.broadcasted_iota(I32, (8, 128), 1) < 64
    rows = [jnp.broadcast_to(back_ref[5 * (n + i) + 4 : 5 * (n + i) + 5, :], (8, 128)) for i in range(4)]
    pairs = [jnp.where(left, pltpu.roll(rows[i], 64, 1), rows[i + 1]) for i in (0, 2)]
    return jnp.concatenate(pairs, axis=1)[0:1].astype(I32)


def composite_kernel(
    got_ref, place_ref, inv_ref, kept_ref, names_ref, image_ref, out_ref,
    par_ref, alpha_ref, pull_ref, weight_ref, grad_ref,
):
    groups = 2 * RANKS
    last = got_ref[pl.ds(8, groups, stride=9), :]
    sub = lax.broadcasted_iota(I32, (8, 128), 0)
    for b in range(8):
        group = jnp.broadcast_to(place_ref[0:1, 128 * b : 128 * (b + 1)], (8, 128))
        lanes = jnp.broadcast_to(place_ref[1:2, 128 * b : 128 * (b + 1)], (8, 128))
        got = lane_gather(got_ref[0:8, :], lanes)
        for n in range(1, groups):
            got = jnp.where(group == n, lane_gather(got_ref[9 * n : 9 * n + 8, :], lanes), got)
        par_ref[0:8, 128 * b : 128 * (b + 1)] = got
        low = jnp.where(group == sub, lane_gather(last[0:8], lanes), 0.0)
        high = jnp.where(group == sub + 8, lane_gather(last[8:16], lanes), 0.0)
        par_ref[8:9, 128 * b : 128 * (b + 1)] = jnp.sum(low + high, axis=0, keepdims=True)

    q = lax.broadcasted_iota(I32, (16, 128), 1)
    row16 = lax.broadcasted_iota(I32, (16, 128), 0)
    X = (q & 15).astype(F32) - 7.5
    Y = (q >> 4).astype(F32) - 3.5
    mono = jnp.where(row16 == 0, 1.0, 0.0)
    for n, m in enumerate([X, Y, X * X, X * Y, Y * Y]):
        mono = jnp.where(row16 == n + 1, m, mono)
    mono8 = mono[0:8]
    mono16 = mono.astype(BF16)
    mono_twice = jnp.concatenate([mono16, mono16], axis=1)
    ex, ey = 1.0 / (16.0 * TILE_COLS), 1.0 / (16.0 * (TILES * OWNERS // TILE_COLS))

    zero = jnp.zeros((1, SLOTS), F32)
    zero5 = jnp.zeros((5, SLOTS), F32)
    blank = jnp.zeros((8, 128), F32)
    cots = []
    geometry = []
    for t in range(TILES):
        par = [par_ref[c : c + 1, SLOTS * t : SLOTS * (t + 1)] for c in range(9)]
        u, w, ca, cb, cc, log_op = par[:6]
        tile = place_ref[2:3, 0:SLOTS] + t
        cx = ((tile & (TILE_COLS - 1)) * 16 + 8).astype(F32) * ex - 0.5
        dx0 = cx - u
        A, B, C = -0.5 * LOG2E * ca, -LOG2E * cb, -0.5 * LOG2E * cc
        colors = jnp.concatenate([par[6], par[7], par[8], zero5], axis=0)
        chi, cmid, clo = [c.astype(F32) for c in split3(colors)]
        dy0s = []
        coefs, pulls = [], []
        for h in range(2):
            cy = ((tile >> 4) * 16 + 8 * h + 4).astype(F32) * ey - 0.5
            dy0 = cy - w
            dy0s.append(dy0)
            coef = [
                (A * dx0 + B * dy0) * dx0 + C * dy0 * dy0 + log_op,
                (2.0 * A * dx0 + B * dy0) * ex,
                (B * dx0 + 2.0 * C * dy0) * ey,
                A * (ex * ex),
                B * (ex * ey),
                C * (ey * ey),
                zero,
                zero,
            ]
            coefs += [k.astype(F32) for k in split3(jnp.concatenate(coef, axis=0))]
            g = [kept_ref[4 * c + t : 4 * c + t + 1, 128 * h : 128 * (h + 1)] for c in range(3)]
            ghi, gmid, glo = [x.astype(F32) for x in split3(jnp.concatenate(g + [blank[0:5]], axis=0))]
            cots.append((4 * h + t, ghi, gmid))
            pulls.append([ghi, gmid, glo, ghi, gmid, ghi])
        left = coefs + [chi, chi, chi, cmid, cmid, clo] + [jnp.zeros((32, SLOTS), F32)]
        left = jnp.transpose(jnp.concatenate(left, axis=0)).astype(BF16)
        right = []
        for h in range(2):
            right.append([blank] * (3 * h) + [mono8] * 3 + [blank] * (13 - 3 * h))
            right.append([blank] * 6 + pulls[h] + [blank] * 4)
        right = jnp.concatenate([jnp.concatenate(r, axis=0) for r in right], axis=1).astype(BF16)
        both = dot(left, right, 1, 0)
        for h in range(2):
            at = pl.ds(4 * h + t, SLOTS, stride=8)
            alpha_ref[at, :] = both[:, 256 * h : 256 * h + 128]
            pull_ref[at, :] = both[:, 256 * h + 128 : 256 * h + 256]
        geometry.append((ca, cb, cc, dx0, dy0s, chi, cmid))

    depth = jnp.concatenate(
        [place_ref[3:4, SLOTS * t + 128 * h : SLOTS * t + 128 * (h + 1)] for h in range(2) for t in range(TILES)], axis=0
    )
    segments = SEGMENTS
    length = SLOTS // segments

    ones, zeros = jnp.ones((8, 128), F32), jnp.zeros((8, 128), F32)
    trans, behind = [ones] * segments, [zeros] * segments
    for i in range(length):
        for n in range(segments):
            s = n * length + i
            at = slice(8 * s, 8 * s + 8)
            alpha = jnp.where(s < depth, jnp.exp2(alpha_ref[at, :]), 0.0)
            weight = trans[n] * alpha
            alpha_ref[at, :] = alpha
            weight_ref[at, :] = weight
            trans[n] = trans[n] - weight
            behind[n] = behind[n] + weight * pull_ref[at, :]
    starts, rest = [ones], [zeros]
    for n in range(1, segments):
        starts.append(starts[-1] * trans[n - 1])
        rest.insert(0, behind[segments - n] + trans[segments - n] * rest[0])

    for i in range(length):
        for n in range(segments):
            s = (n + 1) * length - 1 - i
            at = slice(8 * s, 8 * s + 8)
            more = pull_ref[at, :] - rest[n]
            rest[n] = rest[n] + alpha_ref[at, :] * more
            weight = starts[n] * weight_ref[at, :]
            weight_ref[at, :] = weight
            pull_ref[at, :] = weight * more

    cots = {th: (ghi, gmid) for th, ghi, gmid in cots}
    for t in range(TILES):
        ca, cb, cc, dx0, dy0s, chi, cmid = geometry[t]
        color_rows = jnp.concatenate([chi, cmid], axis=0).astype(BF16)
        total = [jnp.zeros((1, SLOTS), F32) for _ in range(6)]
        dcolor = jnp.zeros((3, SLOTS), F32)
        for h in range(2):
            th = 4 * h + t
            dy0 = dy0s[h]
            whi, wlo = split2(weight_ref[pl.ds(th, SLOTS, stride=8), :])
            weights = jnp.concatenate([whi, wlo], axis=1)
            ghi, glo = split2(pull_ref[pl.ds(th, SLOTS, stride=8), :])
            grads = jnp.concatenate([ghi, glo], axis=1)
            seen = dot(color_rows, weights, 1, 0)
            seen = seen[:, :128] + seen[:, 128:]
            seen = seen[0:8] + seen[8:16]
            for c in range(3):
                image_ref[c, t : t + 1, 128 * h : 128 * (h + 1)] = seen[c : c + 1]
            cot = jnp.concatenate(cots[th], axis=0).astype(BF16)
            dcol = dot(jnp.concatenate([cot, cot], axis=1), weights, 1, 1)
            dcolor = dcolor + dcol[0:3] + dcol[8:11]
            mom = dot(mono_twice, grads, 1, 1)
            m0 = mom[0:1]
            mx, my = ex * mom[1:2], ey * mom[2:3]
            total[0] = total[0] + m0
            total[1] = total[1] + dx0 * m0 + mx
            total[2] = total[2] + dy0 * m0 + my
            total[3] = total[3] + dx0 * (dx0 * m0 + 2.0 * mx) + (ex * ex) * mom[3:4]
            total[4] = total[4] + dx0 * (dy0 * m0 + my) + dy0 * mx + (ex * ey) * mom[4:5]
            total[5] = total[5] + dy0 * (dy0 * m0 + 2.0 * my) + (ey * ey) * mom[5:6]
        s0, sx, sy, sxx, sxy, syy = total
        made = [ca * sx + cb * sy, cb * sx + cc * sy, -0.5 * sxx, -sxy, -0.5 * syy, s0, dcolor]
        grad_ref[0:9, SLOTS * t : SLOTS * (t + 1)] = jnp.concatenate(made, axis=0)

    inv = inv_ref[...]

    def pick(tables, idx):
        at = jnp.maximum(idx - 1, 0)
        low, high = at & 127, at >> 7
        got = lane_gather(tables[0], low)
        for j in range(1, 8):
            got = jnp.where(high == j, lane_gather(tables[j], low), got)
        return jnp.where(idx > 0, got, 0.0)

    tables = [grad_ref[0:8, 128 * j : 128 * (j + 1)] for j in range(8)]
    last = [jnp.broadcast_to(grad_ref[8:9, 128 * j : 128 * (j + 1)], (8, 128)) for j in range(8)]
    left = lax.broadcasted_iota(I32, (4, 128), 1) < 64
    for n in range(PEERS):
        got = pick(tables, jnp.broadcast_to(inv[n : n + 1], (8, 128)))
        out_ref[5 * n : 5 * n + 4, :] = jnp.where(left, got[0:4], got[4:8])
    more = [pick(last, inv[n : n + 8]) for n in range(0, PEERS, 8)]
    left = lax.broadcasted_iota(I32, (PEERS, 128), 1) < 64
    out_ref[pl.ds(4, PEERS, stride=5), :] = jnp.where(left, jnp.concatenate(more, axis=0), names_ref[...])


def collect_kernel(back_ref, kept_ref, out_ref):
    lid = lax.broadcasted_iota(I32, (G_DEV, 256), 0).astype(jnp.int16)
    sub = lax.broadcasted_iota(I32, (8, 128), 0)
    lane = lax.broadcasted_iota(I32, (8, 128), 1)
    near, left = (lane & 63) >> 4, lane < 64
    acc = jnp.zeros((80, G_DEV), F32)
    for n in range(0, PEERS, 4):
        hot = one_hot(lid, pair_ids(back_ref, n))
        pairs = []
        for i in range(2):
            at = 5 * (n + 2 * i)
            one = jnp.concatenate([back_ref[at : at + 4, :]] * 2, axis=0)
            two = jnp.concatenate([back_ref[at + 5 : at + 9, :]] * 2, axis=0)
            other = jnp.where(left, pltpu.roll(one, 64, 1), two)
            straight = jnp.where(left, one, pltpu.roll(two, 64, 1))
            main = jnp.where(sub < 4, straight, other)
            last_one = jnp.broadcast_to(back_ref[at + 4 : at + 5, :], (8, 128))
            last_two = jnp.broadcast_to(back_ref[at + 9 : at + 10, :], (8, 128))
            last = jnp.where(left, last_one, pltpu.roll(last_two, 64, 1))
            rows = []
            for m, l in zip(split2(main), split2(last)):
                m, l = m.astype(F32), l.astype(F32)
                rows += [jnp.where(near == r, m, 0.0) for r in range(NEAR)] + [jnp.where(near == sub, l, 0.0)]
            pairs.append(jnp.concatenate(rows, axis=0).astype(BF16))
        acc = acc + dot(jnp.concatenate(pairs, axis=1), hot, 1, 1)
    rows = acc[0:40] + acc[40:80]
    tail = kept_ref[12:16, 0:128]
    for r in range(NEAR):
        part = [rows[8 * r : 8 * r + 8, 128 * j : 128 * (j + 1)] for j in range(4)]
        part += [rows[32 + r : 33 + r, 128 * j : 128 * (j + 1)] for j in range(4)] + [tail]
        part = jnp.concatenate(part, axis=0)
        for v in range(VIEWS):
            out_ref[40 * (NEAR * v + r) : 40 * (NEAR * v + r + 1), :] = part


def pull_kernel(parts_ref, attr_ref, image_in_ref, out_ref, image_ref, wide_ref, res_ref, all_ref):
    image_ref[...] = image_in_ref[...]
    for v in range(VIEWS):
        start = 40 * NEAR * v
        total = parts_ref[start : start + 36, :]
        for r in range(1, NEAR):
            total = total + parts_ref[start + 40 * r : start + 40 * r + 36, :]
        all_ref[40 * v : 40 * v + 36, :] = total
        all_ref[40 * v + 36 : 40 * v + 40, :] = parts_ref[start + 36 : start + 40, :]
    spread_attributes(attr_ref, wide_ref)
    pos, logscale, quat, logit, sh = split_attributes(wide_ref)
    total = None
    opacity_grad = None
    for pair in range(VIEWS // 2):
        starts = (80 * pair, 80 * pair + 40)
        cot = [
            jnp.concatenate([all_ref[pl.ds(s + c, 4, stride=8), :] for s in starts], axis=0) for c in range(8)
        ]
        cot.append(jnp.concatenate([all_ref[s + 32 : s + 36, :] for s in starts], axis=0))
        cam = [
            jnp.concatenate(
                [jnp.broadcast_to(all_ref[s + 36 : s + 37, j : j + 1], (4, 128)) for s in starts], axis=0
            )
            for j in range(6)
        ]
        terms = camera_terms(cam[:3], cam[3:])
        _, pull = jax.vjp(lambda a, b, c, d: project(a, b, c, d, terms), pos, logscale, quat, sh)
        grads = jax.tree.leaves(pull(cot[:5] + cot[6:]))
        total = grads if total is None else [a + b for a, b in zip(total, grads)]
        opacity_grad = cot[5] if opacity_grad is None else opacity_grad + cot[5]
    grads = total[:10] + [opacity_grad / (1.0 + jnp.exp(logit))] + total[10:]
    for a in range(ATTR):
        res_ref[4 * a : 4 * a + 4, :] = grads[a][0:4] + grads[a][4:8]
    for j in range(4):
        out_ref[:, 128 * j : 128 * (j + 1)] = res_ref[pl.ds(j, ATTR, stride=4), :]


VMEM = pl.BlockSpec(memory_space=pltpu.VMEM)
SMEM = pl.BlockSpec(memory_space=pltpu.SMEM)
HBM = pl.BlockSpec(memory_space=pl.ANY)
MIB = 1024 * 1024


def call(kernel, outs, args, scratch=(), in_specs=None, out_specs=None, limit=24):
    return pl.pallas_call(
        kernel,
        out_shape=[jax.ShapeDtypeStruct(s, d) for s, d in outs],
        in_specs=in_specs or [VMEM] * len(args),
        out_specs=out_specs or [VMEM] * len(outs),
        scratch_shapes=list(scratch),
        compiler_params=pltpu.CompilerParams(vmem_limit_bytes=limit * MIB),
    )(*args)


def in_hbm(x):
    return pltpu.with_memory_space_constraint(x, pltpu.HBM)


def vmem(*shape, dtype=F32):
    return pltpu.VMEM(shape, dtype)


def route(first_tile, owner, local, attributes, camera, depth, cot):
    return call(
        route_kernel,
        [
            ((2 * RANKS, 128), F32), ((PEERS, 128), I32), ((8, TILES * SLOTS), I32), ((36 * PLANES, 128), F32),
            ((16, SLOTS), F32), ((PEERS, 128), F32),
        ],
        (first_tile, *[in_hbm(x) for x in (owner, local, attributes, camera, depth, cot)]),
        [
            vmem(1, TILES * SLOTS, dtype=I32), vmem(TILES, SLOTS, dtype=I32), vmem(ATTR, G_DEV), vmem(1, 6),
            vmem(TILES, SLOTS, dtype=I32), vmem(3, TILES, SLOTS), vmem(ATTR * 8, 128), vmem(36, 128),
            vmem(36 * PLANES, 128), pltpu.SemaphoreType.DMA((7,)),
        ],
        [SMEM] + [HBM] * 6,
        [VMEM] * 3 + [HBM] + [VMEM] * 2,
    )


def serve(first_tile, asked, rows):
    return call(
        serve_kernel, [((18 * RANKS, 128), F32)], (first_tile, asked, rows), (), [SMEM] + [VMEM] * 2
    )[0]


def composite(got, place, inv, kept, names):
    big = vmem(SLOTS * 8, 128)
    return call(
        composite_kernel,
        [((3, TILES, 256), F32), ((5 * PEERS, 128), F32)],
        (got, place, inv, kept, names),
        [vmem(16, TILES * SLOTS), big, big, big, vmem(16, TILES * SLOTS)],
    )


def collect(back, kept):
    return call(collect_kernel, [((VIEWS * NEAR * 40, 128), F32)], (back, kept))[0]


def pull_back(parts, attributes, image):
    return call(
        pull_kernel,
        [((ATTR, G_DEV), F32), (image.shape, F32)],
        (parts, attributes, image),
        [vmem(ATTR * 8, 128), vmem(ATTR * 4, 128), vmem(40 * VIEWS, 128)],
    )


def exchange(x, axis, groups):
    return lax.all_to_all(x, axis, split_axis=0, concat_axis=0, tiled=True, axis_index_groups=groups)


ALONG = [[8 * z + r for z in range(PLANES)] for r in range(RANKS)]
PLANE = [[8 * z + r for r in range(RANKS)] for z in range(PLANES)]
AROUND = [[8 * z + r for r in RING] for z in range(PLANES)]
ACROSS = [[8 * z + 2 * y + c for z in range(PLANES) for c in range(2)] for y in range(NEAR)]
WITHIN = [[8 * z + 2 * y + c for y in range(NEAR)] for z in range(PLANES) for c in range(2)]
VIEWS_WITHIN = [[OWNERS * v + d for v in range(VIEWS) for d in group] for group in WITHIN]


def per_device(attributes, camera, list_owner, list_local, term_depth, image_cot):
    owner = list_owner.reshape(1, -1)
    first_tile = (lax.axis_index("dev") * TILES).astype(I32).reshape(1)
    asked, inv, place, rows, kept, names = route(
        first_tile, owner, list_local[0], attributes, camera, term_depth[0], image_cot[0]
    )
    rows = exchange(rows.reshape(PLANES, 1, 4608), "dev", ALONG).reshape(PLANES * 36, 128)
    asked = lax.all_gather(asked, "dev", axis_index_groups=AROUND, tiled=True)
    sent = serve(first_tile, asked, rows)
    got = exchange(sent.reshape(RANKS, 1, 2304), "dev", PLANE).reshape(18 * RANKS, 128)
    image, grads = composite(got, place, inv, kept, names)
    back = exchange(grads.reshape(PEERS, 1, 640), "dev", ACROSS).reshape(5 * PEERS, 128)
    mine = collect(back, kept)
    parts = exchange(mine.reshape(VIEWS * NEAR, 40, 128), ("view", "dev"), VIEWS_WITHIN)
    grad, image = pull_back(parts.reshape(VIEWS * NEAR * 40, 128), attributes, image)
    return image[None], grad


def solution(mesh):
    in_specs = (
        P(None, "dev"),
        P("view", None),
        P("view", "dev", None, None),
        P("view", "dev", None),
        P("view", "dev", None),
        P("view", None, "dev", None),
    )
    out_specs = (P("view", None, "dev", None), P(None, "dev"))
    return jax.shard_map(
        per_device, mesh=mesh, in_specs=in_specs, out_specs=out_specs, check_vma=False
    )
```

```python
import jax
import jax.numpy as jnp
from jax import lax
from jax.experimental import pallas as pl
from jax.experimental.pallas import tpu as pltpu
from jax.sharding import PartitionSpec as P

TILE_COLS = 16
TILES = 4
SLOTS = 256
CAP = 16
OWNERS = 128
PEERS = 32
NEAR = 4
PLANES = 16
RANKS = 8
SEGMENTS = 8
G_DEV = 512
ATTR = 59
VIEWS = 4
LOG2E = 1.4426950408889634

SH_C0 = 0.28209479177387814
SH_C1 = 0.4886025119029199
SH_C2 = (
    1.0925484305920792,
    -1.0925484305920792,
    0.31539156525252005,
    -1.0925484305920792,
    0.5462742152960396,
)
SH_C3 = (
    -0.5900435899266435,
    2.890611442640554,
    -0.4570457994644658,
    0.3731763325901154,
    -0.4570457994644658,
    1.445305721320277,
    -0.5900435899266435,
)
BLUR = 1e-05

F32 = jnp.float32
BF16 = jnp.bfloat16
I32 = jnp.int32


def camera_terms(angles, shift):
    cosx, sinx = jnp.cos(angles[0]), jnp.sin(angles[0])
    cosy, siny = jnp.cos(angles[1]), jnp.sin(angles[1])
    cosz, sinz = jnp.cos(angles[2]), jnp.sin(angles[2])
    yx = [
        [cosy, siny * sinx, siny * cosx],
        [None, cosx, -sinx],
        [-siny, cosy * sinx, cosy * cosx],
    ]
    rot = [
        [cosz * yx[0][0]] + [cosz * yx[0][j] - sinz * yx[1][j] for j in (1, 2)],
        [sinz * yx[0][0]] + [sinz * yx[0][j] + cosz * yx[1][j] for j in (1, 2)],
        yx[2],
    ]
    centre = [-(rot[0][j] * shift[0] + rot[1][j] * shift[1] + rot[2][j] * shift[2]) for j in range(3)]
    return rot, shift, centre


def harmonics(dirx, diry, dirz):
    xx, yy, zz = (dirx * dirx, diry * diry, dirz * dirz)
    return [
        -SH_C1 * diry,
        SH_C1 * dirz,
        -SH_C1 * dirx,
        SH_C2[0] * dirx * diry,
        SH_C2[1] * diry * dirz,
        SH_C2[2] * (2.0 * zz - xx - yy),
        SH_C2[3] * dirx * dirz,
        SH_C2[4] * (xx - yy),
        SH_C3[0] * diry * (3.0 * xx - yy),
        SH_C3[1] * dirx * diry * dirz,
        SH_C3[2] * diry * (4.0 * zz - xx - yy),
        SH_C3[3] * dirz * (2.0 * zz - 3.0 * xx - 3.0 * yy),
        SH_C3[4] * dirx * (4.0 * zz - xx - yy),
        SH_C3[5] * dirz * (xx - yy),
        SH_C3[6] * dirx * (xx - 3.0 * yy),
    ]


def project(pos, logscale, quat, sh, cam):
    rot, shift, centre = cam
    cpos = [rot[i][0] * pos[0] + rot[i][1] * pos[1] + rot[i][2] * pos[2] + shift[i] for i in range(3)]
    inverse = 1.0 / cpos[2]
    u, w = cpos[0] * inverse, cpos[1] * inverse
    tmat = [
        [inverse * (rot[0][j] - u * rot[2][j]) for j in range(3)],
        [inverse * (rot[1][j] - w * rot[2][j]) for j in range(3)],
    ]
    scale = [jnp.exp(s) for s in logscale]
    norm = lax.rsqrt(quat[0] * quat[0] + quat[1] * quat[1] + quat[2] * quat[2] + quat[3] * quat[3])
    qw, qa, qb, qc = [q * norm for q in quat]
    rgau = [
        [1 - 2 * (qb * qb + qc * qc), 2 * (qa * qb - qw * qc), 2 * (qa * qc + qw * qb)],
        [2 * (qa * qb + qw * qc), 1 - 2 * (qa * qa + qc * qc), 2 * (qb * qc - qw * qa)],
        [2 * (qa * qc - qw * qb), 2 * (qb * qc + qw * qa), 1 - 2 * (qa * qa + qb * qb)],
    ]
    trs = [
        [(tmat[r][0] * rgau[0][k] + tmat[r][1] * rgau[1][k] + tmat[r][2] * rgau[2][k]) * scale[k] for k in range(3)]
        for r in range(2)
    ]
    sig_a = trs[0][0] * trs[0][0] + trs[0][1] * trs[0][1] + trs[0][2] * trs[0][2] + BLUR
    sig_b = trs[0][0] * trs[1][0] + trs[0][1] * trs[1][1] + trs[0][2] * trs[1][2]
    sig_c = trs[1][0] * trs[1][0] + trs[1][1] * trs[1][1] + trs[1][2] * trs[1][2] + BLUR
    det_inv = 1.0 / (sig_a * sig_c - sig_b * sig_b)
    dirs = [pos[j] - centre[j] for j in range(3)]
    norm_inv = lax.rsqrt(dirs[0] * dirs[0] + dirs[1] * dirs[1] + dirs[2] * dirs[2])
    basis = harmonics(dirs[0] * norm_inv, dirs[1] * norm_inv, dirs[2] * norm_inv)
    colors = []
    for ch in range(3):
        color = 0.5 + SH_C0 * sh[ch]
        for k in range(1, 16):
            color = color + basis[k - 1] * sh[3 * k + ch]
        colors.append(color)
    return [u, w, sig_c * det_inv, -sig_b * det_inv, sig_a * det_inv] + colors


def spread_attributes(attr_ref, wide_ref):
    for j in range(4):
        part = attr_ref[:, 128 * j : 128 * (j + 1)]
        wide_ref[pl.ds(j, ATTR, stride=8), :] = part
        wide_ref[pl.ds(j + 4, ATTR, stride=8), :] = part


def split_attributes(wide_ref):
    attrs = [wide_ref[8 * a : 8 * (a + 1), :] for a in range(ATTR)]
    return attrs[0:3], attrs[3:6], attrs[6:10], attrs[10], attrs[11:]


def dot(a, b, ca, cb):
    return lax.dot_general(a, b, (((ca,), (cb,)), ((), ())), preferred_element_type=F32)


def lane_gather(x, idx):
    return jnp.take_along_axis(x, idx, axis=1, mode="promise_in_bounds")


def split2(x):
    hi = x.astype(BF16)
    return hi, (x - hi.astype(F32)).astype(BF16)


def split3(x):
    hi = x.astype(BF16)
    rest = x - hi.astype(F32)
    mid = rest.astype(BF16)
    return hi, mid, (rest - mid.astype(F32)).astype(BF16)


def route_kernel(
    tile_ref, owner_hbm, local_hbm, attr_hbm, cam_hbm, depth_hbm, cot_hbm,
    asked_ref, inv_ref, place_ref, rows_hbm, kept_ref, names_ref,
    owner_ref, local_ref, attr_ref, cam_ref, depth_ref, cot_ref, wide_ref, tmp_ref, rows_ref, sem,
):
    pairs = [
        (owner_hbm, owner_ref), (local_hbm, local_ref), (attr_hbm, attr_ref), (cam_hbm, cam_ref),
        (depth_hbm, depth_ref), (cot_hbm, cot_ref),
    ]
    copies = [pltpu.make_async_copy(src, dst, sem.at[n]) for n, (src, dst) in enumerate(pairs)]
    for copy in copies:
        copy.start()
    copies[2].wait()
    copies[3].wait()
    spread_attributes(attr_ref, wide_ref)
    pos, logscale, quat, logit, sh = split_attributes(wide_ref)
    cam = [jnp.broadcast_to(cam_ref[:, j : j + 1], (8, 128)) for j in range(6)]
    rows = project(pos, logscale, quat, sh, camera_terms(cam[:3], cam[3:]))
    log_opacity = -LOG2E * jnp.log(1.0 + jnp.exp(-logit))
    rows = rows[:5] + [log_opacity] + rows[5:]
    for c in range(8):
        tmp_ref[pl.ds(c, 4, stride=8), :] = rows[c][0:4]
    tmp_ref[32:36, :] = rows[8][0:4]
    rows = tmp_ref[...]
    for z in range(PLANES):
        rows_ref[36 * z : 36 * (z + 1), :] = rows
    rows_copy = pltpu.make_async_copy(rows_ref, rows_hbm, sem.at[6])
    rows_copy.start()
    for n in (0, 1, 4, 5):
        copies[n].wait()
    before = (
        lax.broadcasted_iota(I32, (SLOTS, SLOTS), 0) < lax.broadcasted_iota(I32, (SLOTS, SLOTS), 1)
    ).astype(F32).astype(BF16)
    every = jnp.ones((SLOTS, SLOTS), BF16)
    oid = lax.broadcasted_iota(I32, (OWNERS, SLOTS), 0)
    pid = lax.broadcasted_iota(I32, (PEERS, SLOTS), 0)
    lane = lax.broadcasted_iota(I32, (1, SLOTS), 1)
    base = jnp.zeros((OWNERS, SLOTS), F32)
    gid = lax.broadcasted_iota(I32, (2 * RANKS, SLOTS), 0)
    table = jnp.zeros((4 * PEERS, 128), F32)
    request = jnp.zeros((4 * RANKS, 128), F32)
    for t in range(TILES):
        owner = owner_ref[:, SLOTS * t : SLOTS * (t + 1)]
        hot = (oid == owner).astype(F32)
        hot16 = hot.astype(BF16)
        count = dot(hot16, before, 1, 0) + base
        base = base + dot(hot16, every, 1, 0)
        rank = jnp.sum(hot * count, axis=0, keepdims=True).astype(I32)
        local = local_ref[t : t + 1, :]
        local_parts = [local & 255, local >> 8]
        slot = lane + (SLOTS * t + 1)
        group = (owner & 7) * 2 + (owner >> 6)
        lanes = ((owner >> 3) & 7) * CAP + rank
        place_ref[0:1, SLOTS * t : SLOTS * (t + 1)] = group
        place_ref[1:2, SLOTS * t : SLOTS * (t + 1)] = lanes
        hot_group = (gid == group).astype(F32)
        vals = jnp.concatenate([hot_group * p.astype(F32) for p in local_parts], axis=0).astype(BF16)
        request = request + dot(vals, (oid == lanes).astype(F32).astype(BF16), 1, 1)
        peer = (owner >> 3) * 2 + (owner & 1)
        lanes = ((owner >> 1) & 3) * CAP + rank
        hot_peer = (pid == peer).astype(F32)
        parts = local_parts + [slot & 255, slot >> 8]
        vals = jnp.concatenate([hot_peer * p.astype(F32) for p in parts], axis=0).astype(BF16)
        table = table + dot(vals, ((oid & 63) == lanes).astype(F32).astype(BF16), 1, 1)
    place_ref[2:3, :] = jnp.full((1, TILES * SLOTS), tile_ref[0], I32)
    n = PEERS
    asked_ref[...] = request[0 : 2 * RANKS] + 256.0 * request[2 * RANKS :]
    names_ref[...] = table[0:n] + 256.0 * table[n : 2 * n]
    inv_ref[...] = (table[2 * n : 3 * n] + 256.0 * table[3 * n :]).astype(I32)
    for c in range(3):
        kept_ref[4 * c : 4 * c + 4, :] = cot_ref[c]
    kept_ref[12:16, :] = jnp.zeros((4, SLOTS), F32)
    kept_ref[12:13, 0:6] = cam_ref[...]
    for t in range(TILES):
        place_ref[3:4, SLOTS * t : SLOTS * (t + 1)] = depth_ref[t : t + 1, :]
    rows_copy.wait()


def serve_kernel(tile_ref, asked_ref, rows_ref, out_ref):
    mine = 2 * ((tile_ref[0] // TILES) & (RANKS - 1))
    lid = lax.broadcasted_iota(I32, (G_DEV, 256), 0).astype(jnp.int16)
    sub = lax.broadcasted_iota(I32, (8, 128), 0)
    near = lax.broadcasted_iota(I32, (8, 128), 1) >> 4
    for half in range(2):
        start = 288 * half
        table = []
        for j in range(4):
            part = [rows_ref[start + 36 * r + 8 * j : start + 36 * r + 8 * j + 8, :] for r in range(8)]
            part.append(rows_ref[pl.ds(start + 32 + j, 8, stride=36), :])
            table.append(jnp.concatenate(part, axis=0))
        table = [x.astype(F32) for x in split3(jnp.concatenate(table, axis=1))]
        table = jnp.concatenate(table + [jnp.zeros((8, G_DEV), F32)], axis=0).astype(BF16)
        for r in range(0, RANKS, 2):
            ids = [asked_ref[pl.ds(16 * (r + i) + mine + half, 1), :] for i in range(2)]
            hot = one_hot(lid, jnp.concatenate(ids, axis=1).astype(I32))
            got = dot(table, hot, 1, 0)
            got = got[0:72] + got[72:144] + got[144:216]
            for i in range(2):
                part = got[:, 128 * i : 128 * (i + 1)]
                main = part[0:8]
                for n in range(1, 8):
                    main = jnp.where(near == n, part[8 * n : 8 * (n + 1)], main)
                at = 9 * (2 * (r + i) + half)
                out_ref[at : at + 8, :] = main
                last = jnp.sum(jnp.where(near == sub, part[64:72], 0.0), axis=0, keepdims=True)
                out_ref[at + 8 : at + 9, :] = last


def one_hot(lid, ids):
    ids = jnp.broadcast_to(ids, (16, 256)).astype(jnp.int16)
    same = lid == jnp.concatenate([ids] * (G_DEV // 16), axis=0)
    return jnp.where(same, jnp.ones(lid.shape, BF16), jnp.zeros(lid.shape, BF16))


def pair_ids(back_ref, n):
    left = lax.broadcasted_iota(I32, (8, 128), 1) < 64
    rows = [jnp.broadcast_to(back_ref[5 * (n + i) + 4 : 5 * (n + i) + 5, :], (8, 128)) for i in range(4)]
    pairs = [jnp.where(left, pltpu.roll(rows[i], 64, 1), rows[i + 1]) for i in (0, 2)]
    return jnp.concatenate(pairs, axis=1)[0:1].astype(I32)


def composite_kernel(
    got_ref, place_ref, inv_ref, kept_ref, names_ref, image_ref, out_ref,
    par_ref, alpha_ref, pull_ref, weight_ref, grad_ref,
):
    groups = 2 * RANKS
    last = got_ref[pl.ds(8, groups, stride=9), :]
    sub = lax.broadcasted_iota(I32, (8, 128), 0)
    for b in range(8):
        group = jnp.broadcast_to(place_ref[0:1, 128 * b : 128 * (b + 1)], (8, 128))
        lanes = jnp.broadcast_to(place_ref[1:2, 128 * b : 128 * (b + 1)], (8, 128))
        got = lane_gather(got_ref[0:8, :], lanes)
        for n in range(1, groups):
            got = jnp.where(group == n, lane_gather(got_ref[9 * n : 9 * n + 8, :], lanes), got)
        par_ref[0:8, 128 * b : 128 * (b + 1)] = got
        low = jnp.where(group == sub, lane_gather(last[0:8], lanes), 0.0)
        high = jnp.where(group == sub + 8, lane_gather(last[8:16], lanes), 0.0)
        par_ref[8:9, 128 * b : 128 * (b + 1)] = jnp.sum(low + high, axis=0, keepdims=True)

    q = lax.broadcasted_iota(I32, (16, 128), 1)
    row16 = lax.broadcasted_iota(I32, (16, 128), 0)
    X = (q & 15).astype(F32) - 7.5
    Y = (q >> 4).astype(F32) - 3.5
    mono = jnp.where(row16 == 0, 1.0, 0.0)
    for n, m in enumerate([X, Y, X * X, X * Y, Y * Y]):
        mono = jnp.where(row16 == n + 1, m, mono)
    mono8 = mono[0:8]
    mono16 = mono.astype(BF16)
    mono_twice = jnp.concatenate([mono16, mono16], axis=1)
    ex, ey = 1.0 / (16.0 * TILE_COLS), 1.0 / (16.0 * (TILES * OWNERS // TILE_COLS))

    zero = jnp.zeros((1, SLOTS), F32)
    zero5 = jnp.zeros((5, SLOTS), F32)
    blank = jnp.zeros((8, 128), F32)
    cots = []
    geometry = []
    for t in range(TILES):
        par = [par_ref[c : c + 1, SLOTS * t : SLOTS * (t + 1)] for c in range(9)]
        u, w, ca, cb, cc, log_op = par[:6]
        tile = place_ref[2:3, 0:SLOTS] + t
        cx = ((tile & (TILE_COLS - 1)) * 16 + 8).astype(F32) * ex - 0.5
        dx0 = cx - u
        A, B, C = -0.5 * LOG2E * ca, -LOG2E * cb, -0.5 * LOG2E * cc
        colors = jnp.concatenate([par[6], par[7], par[8], zero5], axis=0)
        chi, cmid, clo = [c.astype(F32) for c in split3(colors)]
        dy0s = []
        coefs, pulls = [], []
        for h in range(2):
            cy = ((tile >> 4) * 16 + 8 * h + 4).astype(F32) * ey - 0.5
            dy0 = cy - w
            dy0s.append(dy0)
            coef = [
                (A * dx0 + B * dy0) * dx0 + C * dy0 * dy0 + log_op,
                (2.0 * A * dx0 + B * dy0) * ex,
                (B * dx0 + 2.0 * C * dy0) * ey,
                A * (ex * ex),
                B * (ex * ey),
                C * (ey * ey),
                zero,
                zero,
            ]
            coefs += [k.astype(F32) for k in split3(jnp.concatenate(coef, axis=0))]
            g = [kept_ref[4 * c + t : 4 * c + t + 1, 128 * h : 128 * (h + 1)] for c in range(3)]
            ghi, gmid, glo = [x.astype(F32) for x in split3(jnp.concatenate(g + [blank[0:5]], axis=0))]
            cots.append((4 * h + t, ghi, gmid))
            pulls.append([ghi, gmid, glo, ghi, gmid, ghi])
        left = coefs + [chi, chi, chi, cmid, cmid, clo] + [jnp.zeros((32, SLOTS), F32)]
        left = jnp.transpose(jnp.concatenate(left, axis=0)).astype(BF16)
        right = []
        for h in range(2):
            right.append([blank] * (3 * h) + [mono8] * 3 + [blank] * (13 - 3 * h))
            right.append([blank] * 6 + pulls[h] + [blank] * 4)
        right = jnp.concatenate([jnp.concatenate(r, axis=0) for r in right], axis=1).astype(BF16)
        both = dot(left, right, 1, 0)
        for h in range(2):
            at = pl.ds(4 * h + t, SLOTS, stride=8)
            alpha_ref[at, :] = both[:, 256 * h : 256 * h + 128]
            pull_ref[at, :] = both[:, 256 * h + 128 : 256 * h + 256]
        geometry.append((ca, cb, cc, dx0, dy0s, chi, cmid))

    depth = jnp.concatenate(
        [place_ref[3:4, SLOTS * t + 128 * h : SLOTS * t + 128 * (h + 1)] for h in range(2) for t in range(TILES)], axis=0
    )
    segments = SEGMENTS
    length = SLOTS // segments

    ones, zeros = jnp.ones((8, 128), F32), jnp.zeros((8, 128), F32)
    trans, behind = [ones] * segments, [zeros] * segments
    for i in range(length):
        for n in range(segments):
            s = n * length + i
            at = slice(8 * s, 8 * s + 8)
            alpha = jnp.where(s < depth, jnp.exp2(alpha_ref[at, :]), 0.0)
            weight = trans[n] * alpha
            alpha_ref[at, :] = alpha
            weight_ref[at, :] = weight
            trans[n] = trans[n] - weight
            behind[n] = behind[n] + weight * pull_ref[at, :]
    starts, rest = [ones], [zeros]
    for n in range(1, segments):
        starts.append(starts[-1] * trans[n - 1])
        rest.insert(0, behind[segments - n] + trans[segments - n] * rest[0])

    for i in range(length):
        for n in range(segments):
            s = (n + 1) * length - 1 - i
            at = slice(8 * s, 8 * s + 8)
            more = pull_ref[at, :] - rest[n]
            rest[n] = rest[n] + alpha_ref[at, :] * more
            weight = starts[n] * weight_ref[at, :]
            weight_ref[at, :] = weight
            pull_ref[at, :] = weight * more

    cots = {th: (ghi, gmid) for th, ghi, gmid in cots}
    for t in range(TILES):
        ca, cb, cc, dx0, dy0s, chi, cmid = geometry[t]
        color_rows = jnp.concatenate([chi, cmid], axis=0).astype(BF16)
        total = [jnp.zeros((1, SLOTS), F32) for _ in range(6)]
        dcolor = jnp.zeros((3, SLOTS), F32)
        for h in range(2):
            th = 4 * h + t
            dy0 = dy0s[h]
            whi, wlo = split2(weight_ref[pl.ds(th, SLOTS, stride=8), :])
            weights = jnp.concatenate([whi, wlo], axis=1)
            ghi, glo = split2(pull_ref[pl.ds(th, SLOTS, stride=8), :])
            grads = jnp.concatenate([ghi, glo], axis=1)
            seen = dot(color_rows, weights, 1, 0)
            seen = seen[:, :128] + seen[:, 128:]
            seen = seen[0:8] + seen[8:16]
            for c in range(3):
                image_ref[c, t : t + 1, 128 * h : 128 * (h + 1)] = seen[c : c + 1]
            cot = jnp.concatenate(cots[th], axis=0).astype(BF16)
            dcol = dot(jnp.concatenate([cot, cot], axis=1), weights, 1, 1)
            dcolor = dcolor + dcol[0:3] + dcol[8:11]
            mom = dot(mono_twice, grads, 1, 1)
            m0 = mom[0:1]
            mx, my = ex * mom[1:2], ey * mom[2:3]
            total[0] = total[0] + m0
            total[1] = total[1] + dx0 * m0 + mx
            total[2] = total[2] + dy0 * m0 + my
            total[3] = total[3] + dx0 * (dx0 * m0 + 2.0 * mx) + (ex * ex) * mom[3:4]
            total[4] = total[4] + dx0 * (dy0 * m0 + my) + dy0 * mx + (ex * ey) * mom[4:5]
            total[5] = total[5] + dy0 * (dy0 * m0 + 2.0 * my) + (ey * ey) * mom[5:6]
        s0, sx, sy, sxx, sxy, syy = total
        made = [ca * sx + cb * sy, cb * sx + cc * sy, -0.5 * sxx, -sxy, -0.5 * syy, s0, dcolor]
        grad_ref[0:9, SLOTS * t : SLOTS * (t + 1)] = jnp.concatenate(made, axis=0)

    inv = inv_ref[...]

    def pick(tables, idx):
        at = jnp.maximum(idx - 1, 0)
        low, high = at & 127, at >> 7
        got = lane_gather(tables[0], low)
        for j in range(1, 8):
            got = jnp.where(high == j, lane_gather(tables[j], low), got)
        return jnp.where(idx > 0, got, 0.0)

    tables = [grad_ref[0:8, 128 * j : 128 * (j + 1)] for j in range(8)]
    last = [jnp.broadcast_to(grad_ref[8:9, 128 * j : 128 * (j + 1)], (8, 128)) for j in range(8)]
    left = lax.broadcasted_iota(I32, (4, 128), 1) < 64
    for n in range(PEERS):
        got = pick(tables, jnp.broadcast_to(inv[n : n + 1], (8, 128)))
        out_ref[5 * n : 5 * n + 4, :] = jnp.where(left, got[0:4], got[4:8])
    more = [pick(last, inv[n : n + 8]) for n in range(0, PEERS, 8)]
    left = lax.broadcasted_iota(I32, (PEERS, 128), 1) < 64
    out_ref[pl.ds(4, PEERS, stride=5), :] = jnp.where(left, jnp.concatenate(more, axis=0), names_ref[...])


def collect_kernel(back_ref, kept_ref, out_ref):
    lid = lax.broadcasted_iota(I32, (G_DEV, 256), 0).astype(jnp.int16)
    sub = lax.broadcasted_iota(I32, (8, 128), 0)
    lane = lax.broadcasted_iota(I32, (8, 128), 1)
    near, left = (lane & 63) >> 4, lane < 64
    acc = jnp.zeros((80, G_DEV), F32)
    for n in range(0, PEERS, 4):
        hot = one_hot(lid, pair_ids(back_ref, n))
        pairs = []
        for i in range(2):
            at = 5 * (n + 2 * i)
            one = jnp.concatenate([back_ref[at : at + 4, :]] * 2, axis=0)
            two = jnp.concatenate([back_ref[at + 5 : at + 9, :]] * 2, axis=0)
            other = jnp.where(left, pltpu.roll(one, 64, 1), two)
            straight = jnp.where(left, one, pltpu.roll(two, 64, 1))
            main = jnp.where(sub < 4, straight, other)
            last_one = jnp.broadcast_to(back_ref[at + 4 : at + 5, :], (8, 128))
            last_two = jnp.broadcast_to(back_ref[at + 9 : at + 10, :], (8, 128))
            last = jnp.where(left, last_one, pltpu.roll(last_two, 64, 1))
            rows = []
            for m, l in zip(split2(main), split2(last)):
                m, l = m.astype(F32), l.astype(F32)
                rows += [jnp.where(near == r, m, 0.0) for r in range(NEAR)] + [jnp.where(near == sub, l, 0.0)]
            pairs.append(jnp.concatenate(rows, axis=0).astype(BF16))
        acc = acc + dot(jnp.concatenate(pairs, axis=1), hot, 1, 1)
    rows = acc[0:40] + acc[40:80]
    tail = kept_ref[12:16, 0:128]
    for r in range(NEAR):
        part = [rows[8 * r : 8 * r + 8, 128 * j : 128 * (j + 1)] for j in range(4)]
        part += [rows[32 + r : 33 + r, 128 * j : 128 * (j + 1)] for j in range(4)] + [tail]
        part = jnp.concatenate(part, axis=0)
        for v in range(VIEWS):
            out_ref[40 * (NEAR * v + r) : 40 * (NEAR * v + r + 1), :] = part


def pull_kernel(parts_ref, attr_ref, image_in_ref, out_ref, image_ref, wide_ref, res_ref, all_ref):
    image_ref[...] = image_in_ref[...]
    for v in range(VIEWS):
        start = 40 * NEAR * v
        total = parts_ref[start : start + 36, :]
        for r in range(1, NEAR):
            total = total + parts_ref[start + 40 * r : start + 40 * r + 36, :]
        all_ref[40 * v : 40 * v + 36, :] = total
        all_ref[40 * v + 36 : 40 * v + 40, :] = parts_ref[start + 36 : start + 40, :]
    spread_attributes(attr_ref, wide_ref)
    pos, logscale, quat, logit, sh = split_attributes(wide_ref)
    total = None
    opacity_grad = None
    for pair in range(VIEWS // 2):
        starts = (80 * pair, 80 * pair + 40)
        cot = [
            jnp.concatenate([all_ref[pl.ds(s + c, 4, stride=8), :] for s in starts], axis=0) for c in range(8)
        ]
        cot.append(jnp.concatenate([all_ref[s + 32 : s + 36, :] for s in starts], axis=0))
        cam = [
            jnp.concatenate(
                [jnp.broadcast_to(all_ref[s + 36 : s + 37, j : j + 1], (4, 128)) for s in starts], axis=0
            )
            for j in range(6)
        ]
        terms = camera_terms(cam[:3], cam[3:])
        _, pull = jax.vjp(lambda a, b, c, d: project(a, b, c, d, terms), pos, logscale, quat, sh)
        grads = jax.tree.leaves(pull(cot[:5] + cot[6:]))
        total = grads if total is None else [a + b for a, b in zip(total, grads)]
        opacity_grad = cot[5] if opacity_grad is None else opacity_grad + cot[5]
    grads = total[:10] + [opacity_grad / (1.0 + jnp.exp(logit))] + total[10:]
    for a in range(ATTR):
        res_ref[4 * a : 4 * a + 4, :] = grads[a][0:4] + grads[a][4:8]
    for j in range(4):
        out_ref[:, 128 * j : 128 * (j + 1)] = res_ref[pl.ds(j, ATTR, stride=4), :]


VMEM = pl.BlockSpec(memory_space=pltpu.VMEM)
SMEM = pl.BlockSpec(memory_space=pltpu.SMEM)
HBM = pl.BlockSpec(memory_space=pl.ANY)
MIB = 1024 * 1024


def call(kernel, outs, args, scratch=(), in_specs=None, out_specs=None, limit=24):
    return pl.pallas_call(
        kernel,
        out_shape=[jax.ShapeDtypeStruct(s, d) for s, d in outs],
        in_specs=in_specs or [VMEM] * len(args),
        out_specs=out_specs or [VMEM] * len(outs),
        scratch_shapes=list(scratch),
        compiler_params=pltpu.CompilerParams(vmem_limit_bytes=limit * MIB),
    )(*args)


def in_hbm(x):
    return pltpu.with_memory_space_constraint(x, pltpu.HBM)


def vmem(*shape, dtype=F32):
    return pltpu.VMEM(shape, dtype)


def route(first_tile, owner, local, attributes, camera, depth, cot):
    return call(
        route_kernel,
        [
            ((2 * RANKS, 128), F32), ((PEERS, 128), I32), ((8, TILES * SLOTS), I32), ((36 * PLANES, 128), F32),
            ((16, SLOTS), F32), ((PEERS, 128), F32),
        ],
        (first_tile, *[in_hbm(x) for x in (owner, local, attributes, camera, depth, cot)]),
        [
            vmem(1, TILES * SLOTS, dtype=I32), vmem(TILES, SLOTS, dtype=I32), vmem(ATTR, G_DEV), vmem(1, 6),
            vmem(TILES, SLOTS, dtype=I32), vmem(3, TILES, SLOTS), vmem(ATTR * 8, 128), vmem(36, 128),
            vmem(36 * PLANES, 128), pltpu.SemaphoreType.DMA((7,)),
        ],
        [SMEM] + [HBM] * 6,
        [VMEM] * 3 + [HBM] + [VMEM] * 2,
    )


def serve(first_tile, asked, rows):
    return call(
        serve_kernel, [((18 * RANKS, 128), F32)], (first_tile, asked, rows), (), [SMEM] + [VMEM] * 2
    )[0]


def composite(got, place, inv, kept, names):
    big = vmem(SLOTS * 8, 128)
    return call(
        composite_kernel,
        [((3, TILES, 256), F32), ((5 * PEERS, 128), F32)],
        (got, place, inv, kept, names),
        [vmem(16, TILES * SLOTS), big, big, big, vmem(16, TILES * SLOTS)],
    )


def collect(back, kept):
    return call(collect_kernel, [((VIEWS * NEAR * 40, 128), F32)], (back, kept))[0]


def pull_back(parts, attributes, image):
    return call(
        pull_kernel,
        [((ATTR, G_DEV), F32), (image.shape, F32)],
        (parts, attributes, image),
        [vmem(ATTR * 8, 128), vmem(ATTR * 4, 128), vmem(40 * VIEWS, 128)],
    )


def exchange(x, axis, groups):
    return lax.all_to_all(x, axis, split_axis=0, concat_axis=0, tiled=True, axis_index_groups=groups)


ALONG = [[8 * z + r for z in range(PLANES)] for r in range(RANKS)]
PLANE = [[8 * z + r for r in range(RANKS)] for z in range(PLANES)]
ACROSS = [[8 * z + 2 * y + c for z in range(PLANES) for c in range(2)] for y in range(NEAR)]
WITHIN = [[8 * z + 2 * y + c for y in range(NEAR)] for z in range(PLANES) for c in range(2)]
VIEWS_WITHIN = [[OWNERS * v + d for v in range(VIEWS) for d in group] for group in WITHIN]


def per_device(attributes, camera, list_owner, list_local, term_depth, image_cot):
    owner = list_owner.reshape(1, -1)
    first_tile = (lax.axis_index("dev") * TILES).astype(I32).reshape(1)
    asked, inv, place, rows, kept, names = route(
        first_tile, owner, list_local[0], attributes, camera, term_depth[0], image_cot[0]
    )
    rows = exchange(rows.reshape(PLANES, 1, 4608), "dev", ALONG).reshape(PLANES * 36, 128)
    asked = lax.all_gather(asked, "dev", axis_index_groups=PLANE, tiled=True)
    sent = serve(first_tile, asked, rows)
    got = exchange(sent.reshape(RANKS, 1, 2304), "dev", PLANE).reshape(18 * RANKS, 128)
    image, grads = composite(got, place, inv, kept, names)
    back = exchange(grads.reshape(PEERS, 1, 640), "dev", ACROSS).reshape(5 * PEERS, 128)
    mine = collect(back, kept)
    parts = exchange(mine.reshape(VIEWS * NEAR, 40, 128), ("view", "dev"), VIEWS_WITHIN)
    grad, image = pull_back(parts.reshape(VIEWS * NEAR * 40, 128), attributes, image)
    return image[None], grad


def solution(mesh):
    in_specs = (
        P(None, "dev"),
        P("view", None),
        P("view", "dev", None, None),
        P("view", "dev", None),
        P("view", "dev", None),
        P("view", None, "dev", None),
    )
    out_specs = (P("view", None, "dev", None), P(None, "dev"))
    return jax.shard_map(
        per_device, mesh=mesh, in_specs=in_specs, out_specs=out_specs, check_vma=False
    )
```

```python
import jax
import jax.numpy as jnp
from jax import lax
from jax.experimental import pallas as pl
from jax.experimental.pallas import tpu as pltpu
from jax.sharding import PartitionSpec as P

TILE_COLS = 16
TILES = 4
SLOTS = 256
CAP = 16
OWNERS = 128
PEERS = 32
NEAR = 4
PLANES = 16
RANKS = 8
SEGMENTS = 8
G_DEV = 512
ATTR = 59
VIEWS = 4
LOG2E = 1.4426950408889634

SH_C0 = 0.28209479177387814
SH_C1 = 0.4886025119029199
SH_C2 = (
    1.0925484305920792,
    -1.0925484305920792,
    0.31539156525252005,
    -1.0925484305920792,
    0.5462742152960396,
)
SH_C3 = (
    -0.5900435899266435,
    2.890611442640554,
    -0.4570457994644658,
    0.3731763325901154,
    -0.4570457994644658,
    1.445305721320277,
    -0.5900435899266435,
)
BLUR = 1e-05

F32 = jnp.float32
BF16 = jnp.bfloat16
I32 = jnp.int32


def camera_terms(angles, shift):
    cosx, sinx = jnp.cos(angles[0]), jnp.sin(angles[0])
    cosy, siny = jnp.cos(angles[1]), jnp.sin(angles[1])
    cosz, sinz = jnp.cos(angles[2]), jnp.sin(angles[2])
    yx = [
        [cosy, siny * sinx, siny * cosx],
        [None, cosx, -sinx],
        [-siny, cosy * sinx, cosy * cosx],
    ]
    rot = [
        [cosz * yx[0][0]] + [cosz * yx[0][j] - sinz * yx[1][j] for j in (1, 2)],
        [sinz * yx[0][0]] + [sinz * yx[0][j] + cosz * yx[1][j] for j in (1, 2)],
        yx[2],
    ]
    centre = [-(rot[0][j] * shift[0] + rot[1][j] * shift[1] + rot[2][j] * shift[2]) for j in range(3)]
    return rot, shift, centre


def harmonics(dirx, diry, dirz):
    xx, yy, zz = (dirx * dirx, diry * diry, dirz * dirz)
    return [
        -SH_C1 * diry,
        SH_C1 * dirz,
        -SH_C1 * dirx,
        SH_C2[0] * dirx * diry,
        SH_C2[1] * diry * dirz,
        SH_C2[2] * (2.0 * zz - xx - yy),
        SH_C2[3] * dirx * dirz,
        SH_C2[4] * (xx - yy),
        SH_C3[0] * diry * (3.0 * xx - yy),
        SH_C3[1] * dirx * diry * dirz,
        SH_C3[2] * diry * (4.0 * zz - xx - yy),
        SH_C3[3] * dirz * (2.0 * zz - 3.0 * xx - 3.0 * yy),
        SH_C3[4] * dirx * (4.0 * zz - xx - yy),
        SH_C3[5] * dirz * (xx - yy),
        SH_C3[6] * dirx * (xx - 3.0 * yy),
    ]


def project(pos, logscale, quat, sh, cam):
    rot, shift, centre = cam
    cpos = [rot[i][0] * pos[0] + rot[i][1] * pos[1] + rot[i][2] * pos[2] + shift[i] for i in range(3)]
    inverse = 1.0 / cpos[2]
    u, w = cpos[0] * inverse, cpos[1] * inverse
    tmat = [
        [inverse * (rot[0][j] - u * rot[2][j]) for j in range(3)],
        [inverse * (rot[1][j] - w * rot[2][j]) for j in range(3)],
    ]
    scale = [jnp.exp(s) for s in logscale]
    norm = lax.rsqrt(quat[0] * quat[0] + quat[1] * quat[1] + quat[2] * quat[2] + quat[3] * quat[3])
    qw, qa, qb, qc = [q * norm for q in quat]
    rgau = [
        [1 - 2 * (qb * qb + qc * qc), 2 * (qa * qb - qw * qc), 2 * (qa * qc + qw * qb)],
        [2 * (qa * qb + qw * qc), 1 - 2 * (qa * qa + qc * qc), 2 * (qb * qc - qw * qa)],
        [2 * (qa * qc - qw * qb), 2 * (qb * qc + qw * qa), 1 - 2 * (qa * qa + qb * qb)],
    ]
    trs = [
        [(tmat[r][0] * rgau[0][k] + tmat[r][1] * rgau[1][k] + tmat[r][2] * rgau[2][k]) * scale[k] for k in range(3)]
        for r in range(2)
    ]
    sig_a = trs[0][0] * trs[0][0] + trs[0][1] * trs[0][1] + trs[0][2] * trs[0][2] + BLUR
    sig_b = trs[0][0] * trs[1][0] + trs[0][1] * trs[1][1] + trs[0][2] * trs[1][2]
    sig_c = trs[1][0] * trs[1][0] + trs[1][1] * trs[1][1] + trs[1][2] * trs[1][2] + BLUR
    det_inv = 1.0 / (sig_a * sig_c - sig_b * sig_b)
    dirs = [pos[j] - centre[j] for j in range(3)]
    norm_inv = lax.rsqrt(dirs[0] * dirs[0] + dirs[1] * dirs[1] + dirs[2] * dirs[2])
    basis = harmonics(dirs[0] * norm_inv, dirs[1] * norm_inv, dirs[2] * norm_inv)
    colors = []
    for ch in range(3):
        color = 0.5 + SH_C0 * sh[ch]
        for k in range(1, 16):
            color = color + basis[k - 1] * sh[3 * k + ch]
        colors.append(color)
    return [u, w, sig_c * det_inv, -sig_b * det_inv, sig_a * det_inv] + colors


def spread_attributes(attr_ref, wide_ref):
    for j in range(4):
        part = attr_ref[:, 128 * j : 128 * (j + 1)]
        wide_ref[pl.ds(j, ATTR, stride=8), :] = part
        wide_ref[pl.ds(j + 4, ATTR, stride=8), :] = part


def split_attributes(wide_ref):
    attrs = [wide_ref[8 * a : 8 * (a + 1), :] for a in range(ATTR)]
    return attrs[0:3], attrs[3:6], attrs[6:10], attrs[10], attrs[11:]


def dot(a, b, ca, cb):
    return lax.dot_general(a, b, (((ca,), (cb,)), ((), ())), preferred_element_type=F32)


def lane_gather(x, idx):
    return jnp.take_along_axis(x, idx, axis=1, mode="promise_in_bounds")


def split2(x):
    hi = x.astype(BF16)
    return hi, (x - hi.astype(F32)).astype(BF16)


def split3(x):
    hi = x.astype(BF16)
    rest = x - hi.astype(F32)
    mid = rest.astype(BF16)
    return hi, mid, (rest - mid.astype(F32)).astype(BF16)


def route_kernel(
    tile_ref, owner_hbm, local_hbm, attr_hbm, cam_hbm, depth_hbm, cot_hbm,
    asked_ref, inv_ref, place_ref, rows_hbm, kept_ref, names_ref, wide_ref,
    owner_ref, local_ref, attr_ref, cam_ref, depth_ref, cot_ref, tmp_ref, rows_ref, sem,
):
    pairs = [
        (owner_hbm, owner_ref), (local_hbm, local_ref), (attr_hbm, attr_ref), (cam_hbm, cam_ref),
        (depth_hbm, depth_ref), (cot_hbm, cot_ref),
    ]
    copies = [pltpu.make_async_copy(src, dst, sem.at[n]) for n, (src, dst) in enumerate(pairs)]
    for copy in copies:
        copy.start()
    copies[2].wait()
    copies[3].wait()
    spread_attributes(attr_ref, wide_ref)
    pos, logscale, quat, logit, sh = split_attributes(wide_ref)
    cam = [jnp.broadcast_to(cam_ref[:, j : j + 1], (8, 128)) for j in range(6)]
    rows = project(pos, logscale, quat, sh, camera_terms(cam[:3], cam[3:]))
    log_opacity = -LOG2E * jnp.log(1.0 + jnp.exp(-logit))
    rows = rows[:5] + [log_opacity] + rows[5:]
    for c in range(8):
        tmp_ref[pl.ds(c, 4, stride=8), :] = rows[c][0:4]
    tmp_ref[32:36, :] = rows[8][0:4]
    rows = tmp_ref[...]
    for z in range(PLANES):
        rows_ref[36 * z : 36 * (z + 1), :] = rows
    rows_copy = pltpu.make_async_copy(rows_ref, rows_hbm, sem.at[6])
    rows_copy.start()
    for n in (0, 1, 4, 5):
        copies[n].wait()
    before = (
        lax.broadcasted_iota(I32, (SLOTS, SLOTS), 0) < lax.broadcasted_iota(I32, (SLOTS, SLOTS), 1)
    ).astype(F32).astype(BF16)
    every = jnp.ones((SLOTS, SLOTS), BF16)
    oid = lax.broadcasted_iota(I32, (OWNERS, SLOTS), 0)
    pid = lax.broadcasted_iota(I32, (PEERS, SLOTS), 0)
    lane = lax.broadcasted_iota(I32, (1, SLOTS), 1)
    base = jnp.zeros((OWNERS, SLOTS), F32)
    gid = lax.broadcasted_iota(I32, (2 * RANKS, SLOTS), 0)
    table = jnp.zeros((4 * PEERS, 128), F32)
    request = jnp.zeros((4 * RANKS, 128), F32)
    for t in range(TILES):
        owner = owner_ref[:, SLOTS * t : SLOTS * (t + 1)]
        hot = (oid == owner).astype(F32)
        hot16 = hot.astype(BF16)
        count = dot(hot16, before, 1, 0) + base
        base = base + dot(hot16, every, 1, 0)
        rank = jnp.sum(hot * count, axis=0, keepdims=True).astype(I32)
        local = local_ref[t : t + 1, :]
        local_parts = [local & 255, local >> 8]
        slot = lane + (SLOTS * t + 1)
        group = (owner & 7) * 2 + (owner >> 6)
        lanes = ((owner >> 3) & 7) * CAP + rank
        place_ref[0:1, SLOTS * t : SLOTS * (t + 1)] = group
        place_ref[1:2, SLOTS * t : SLOTS * (t + 1)] = lanes
        hot_group = (gid == group).astype(F32)
        vals = jnp.concatenate([hot_group * p.astype(F32) for p in local_parts], axis=0).astype(BF16)
        request = request + dot(vals, (oid == lanes).astype(F32).astype(BF16), 1, 1)
        peer = (owner >> 3) * 2 + (owner & 1)
        lanes = ((owner >> 1) & 3) * CAP + rank
        hot_peer = (pid == peer).astype(F32)
        parts = local_parts + [slot & 255, slot >> 8]
        vals = jnp.concatenate([hot_peer * p.astype(F32) for p in parts], axis=0).astype(BF16)
        table = table + dot(vals, ((oid & 63) == lanes).astype(F32).astype(BF16), 1, 1)
    place_ref[2:3, :] = jnp.full((1, TILES * SLOTS), tile_ref[0], I32)
    n = PEERS
    asked_ref[...] = request[0 : 2 * RANKS] + 256.0 * request[2 * RANKS :]
    names_ref[...] = table[0:n] + 256.0 * table[n : 2 * n]
    inv_ref[...] = (table[2 * n : 3 * n] + 256.0 * table[3 * n :]).astype(I32)
    for c in range(3):
        kept_ref[4 * c : 4 * c + 4, :] = cot_ref[c]
    kept_ref[12:16, :] = jnp.zeros((4, SLOTS), F32)
    kept_ref[12:13, 0:6] = cam_ref[...]
    for t in range(TILES):
        place_ref[3:4, SLOTS * t : SLOTS * (t + 1)] = depth_ref[t : t + 1, :]
    rows_copy.wait()


def serve_kernel(tile_ref, asked_ref, rows_ref, out_ref):
    mine = 2 * ((tile_ref[0] // TILES) & (RANKS - 1))
    lid = lax.broadcasted_iota(I32, (G_DEV, 256), 0).astype(jnp.int16)
    sub = lax.broadcasted_iota(I32, (8, 128), 0)
    near = lax.broadcasted_iota(I32, (8, 128), 1) >> 4
    for half in range(2):
        start = 288 * half
        table = []
        for j in range(4):
            part = [rows_ref[start + 36 * r + 8 * j : start + 36 * r + 8 * j + 8, :] for r in range(8)]
            part.append(rows_ref[pl.ds(start + 32 + j, 8, stride=36), :])
            table.append(jnp.concatenate(part, axis=0))
        table = [x.astype(F32) for x in split3(jnp.concatenate(table, axis=1))]
        table = jnp.concatenate(table + [jnp.zeros((8, G_DEV), F32)], axis=0).astype(BF16)
        for r in range(0, RANKS, 2):
            ids = [asked_ref[pl.ds(16 * (r + i) + mine + half, 1), :] for i in range(2)]
            hot = one_hot(lid, jnp.concatenate(ids, axis=1).astype(I32))
            got = dot(table, hot, 1, 0)
            got = got[0:72] + got[72:144] + got[144:216]
            for i in range(2):
                part = got[:, 128 * i : 128 * (i + 1)]
                main = part[0:8]
                for n in range(1, 8):
                    main = jnp.where(near == n, part[8 * n : 8 * (n + 1)], main)
                at = 9 * (2 * (r + i) + half)
                out_ref[at : at + 8, :] = main
                last = jnp.sum(jnp.where(near == sub, part[64:72], 0.0), axis=0, keepdims=True)
                out_ref[at + 8 : at + 9, :] = last


def one_hot(lid, ids):
    ids = jnp.broadcast_to(ids, (16, 256)).astype(jnp.int16)
    same = lid == jnp.concatenate([ids] * (G_DEV // 16), axis=0)
    return jnp.where(same, jnp.ones(lid.shape, BF16), jnp.zeros(lid.shape, BF16))


def pair_ids(back_ref, n):
    left = lax.broadcasted_iota(I32, (8, 128), 1) < 64
    rows = [jnp.broadcast_to(back_ref[5 * (n + i) + 4 : 5 * (n + i) + 5, :], (8, 128)) for i in range(4)]
    pairs = [jnp.where(left, pltpu.roll(rows[i], 64, 1), rows[i + 1]) for i in (0, 2)]
    return jnp.concatenate(pairs, axis=1)[0:1].astype(I32)


def composite_kernel(
    got_ref, place_ref, inv_ref, kept_ref, names_ref, image_ref, out_ref,
    par_ref, alpha_ref, pull_ref, weight_ref, grad_ref,
):
    groups = 2 * RANKS
    last = got_ref[pl.ds(8, groups, stride=9), :]
    sub = lax.broadcasted_iota(I32, (8, 128), 0)
    for b in range(8):
        group = jnp.broadcast_to(place_ref[0:1, 128 * b : 128 * (b + 1)], (8, 128))
        lanes = jnp.broadcast_to(place_ref[1:2, 128 * b : 128 * (b + 1)], (8, 128))
        got = lane_gather(got_ref[0:8, :], lanes)
        for n in range(1, groups):
            got = jnp.where(group == n, lane_gather(got_ref[9 * n : 9 * n + 8, :], lanes), got)
        par_ref[0:8, 128 * b : 128 * (b + 1)] = got
        low = jnp.where(group == sub, lane_gather(last[0:8], lanes), 0.0)
        high = jnp.where(group == sub + 8, lane_gather(last[8:16], lanes), 0.0)
        par_ref[8:9, 128 * b : 128 * (b + 1)] = jnp.sum(low + high, axis=0, keepdims=True)

    q = lax.broadcasted_iota(I32, (16, 128), 1)
    row16 = lax.broadcasted_iota(I32, (16, 128), 0)
    X = (q & 15).astype(F32) - 7.5
    Y = (q >> 4).astype(F32) - 3.5
    mono = jnp.where(row16 == 0, 1.0, 0.0)
    for n, m in enumerate([X, Y, X * X, X * Y, Y * Y]):
        mono = jnp.where(row16 == n + 1, m, mono)
    mono8 = mono[0:8]
    mono16 = mono.astype(BF16)
    mono_twice = jnp.concatenate([mono16, mono16], axis=1)
    ex, ey = 1.0 / (16.0 * TILE_COLS), 1.0 / (16.0 * (TILES * OWNERS // TILE_COLS))

    zero = jnp.zeros((1, SLOTS), F32)
    zero5 = jnp.zeros((5, SLOTS), F32)
    blank = jnp.zeros((8, 128), F32)
    cots = []
    geometry = []
    for t in range(TILES):
        par = [par_ref[c : c + 1, SLOTS * t : SLOTS * (t + 1)] for c in range(9)]
        u, w, ca, cb, cc, log_op = par[:6]
        tile = place_ref[2:3, 0:SLOTS] + t
        cx = ((tile & (TILE_COLS - 1)) * 16 + 8).astype(F32) * ex - 0.5
        dx0 = cx - u
        A, B, C = -0.5 * LOG2E * ca, -LOG2E * cb, -0.5 * LOG2E * cc
        colors = jnp.concatenate([par[6], par[7], par[8], zero5], axis=0)
        chi, cmid, clo = [c.astype(F32) for c in split3(colors)]
        dy0s = []
        coefs, pulls = [], []
        for h in range(2):
            cy = ((tile >> 4) * 16 + 8 * h + 4).astype(F32) * ey - 0.5
            dy0 = cy - w
            dy0s.append(dy0)
            coef = [
                (A * dx0 + B * dy0) * dx0 + C * dy0 * dy0 + log_op,
                (2.0 * A * dx0 + B * dy0) * ex,
                (B * dx0 + 2.0 * C * dy0) * ey,
                A * (ex * ex),
                B * (ex * ey),
                C * (ey * ey),
                zero,
                zero,
            ]
            coefs += [k.astype(F32) for k in split3(jnp.concatenate(coef, axis=0))]
            g = [kept_ref[4 * c + t : 4 * c + t + 1, 128 * h : 128 * (h + 1)] for c in range(3)]
            ghi, gmid, glo = [x.astype(F32) for x in split3(jnp.concatenate(g + [blank[0:5]], axis=0))]
            cots.append((4 * h + t, ghi, gmid))
            pulls.append([ghi, gmid, glo, ghi, gmid, ghi])
        left = coefs + [chi, chi, chi, cmid, cmid, clo] + [jnp.zeros((32, SLOTS), F32)]
        left = jnp.transpose(jnp.concatenate(left, axis=0)).astype(BF16)
        right = []
        for h in range(2):
            right.append([blank] * (3 * h) + [mono8] * 3 + [blank] * (13 - 3 * h))
            right.append([blank] * 6 + pulls[h] + [blank] * 4)
        right = jnp.concatenate([jnp.concatenate(r, axis=0) for r in right], axis=1).astype(BF16)
        both = dot(left, right, 1, 0)
        for h in range(2):
            at = pl.ds(4 * h + t, SLOTS, stride=8)
            alpha_ref[at, :] = both[:, 256 * h : 256 * h + 128]
            pull_ref[at, :] = both[:, 256 * h + 128 : 256 * h + 256]
        geometry.append((ca, cb, cc, dx0, dy0s, chi, cmid))

    depth = jnp.concatenate(
        [place_ref[3:4, SLOTS * t + 128 * h : SLOTS * t + 128 * (h + 1)] for h in range(2) for t in range(TILES)], axis=0
    )
    segments = SEGMENTS
    length = SLOTS // segments

    ones, zeros = jnp.ones((8, 128), F32), jnp.zeros((8, 128), F32)
    trans, behind = [ones] * segments, [zeros] * segments
    for i in range(length):
        for n in range(segments):
            s = n * length + i
            at = slice(8 * s, 8 * s + 8)
            alpha = jnp.where(s < depth, jnp.exp2(alpha_ref[at, :]), 0.0)
            weight = trans[n] * alpha
            alpha_ref[at, :] = alpha
            weight_ref[at, :] = weight
            trans[n] = trans[n] - weight
            behind[n] = behind[n] + weight * pull_ref[at, :]
    starts, rest = [ones], [zeros]
    for n in range(1, segments):
        starts.append(starts[-1] * trans[n - 1])
        rest.insert(0, behind[segments - n] + trans[segments - n] * rest[0])

    for i in range(length):
        for n in range(segments):
            s = (n + 1) * length - 1 - i
            at = slice(8 * s, 8 * s + 8)
            more = pull_ref[at, :] - rest[n]
            rest[n] = rest[n] + alpha_ref[at, :] * more
            weight = starts[n] * weight_ref[at, :]
            weight_ref[at, :] = weight
            pull_ref[at, :] = weight * more

    cots = {th: (ghi, gmid) for th, ghi, gmid in cots}
    for t in range(TILES):
        ca, cb, cc, dx0, dy0s, chi, cmid = geometry[t]
        color_rows = jnp.concatenate([chi, cmid], axis=0).astype(BF16)
        total = [jnp.zeros((1, SLOTS), F32) for _ in range(6)]
        dcolor = jnp.zeros((3, SLOTS), F32)
        for h in range(2):
            th = 4 * h + t
            dy0 = dy0s[h]
            whi, wlo = split2(weight_ref[pl.ds(th, SLOTS, stride=8), :])
            weights = jnp.concatenate([whi, wlo], axis=1)
            ghi, glo = split2(pull_ref[pl.ds(th, SLOTS, stride=8), :])
            grads = jnp.concatenate([ghi, glo], axis=1)
            seen = dot(color_rows, weights, 1, 0)
            seen = seen[:, :128] + seen[:, 128:]
            seen = seen[0:8] + seen[8:16]
            for c in range(3):
                image_ref[c, t : t + 1, 128 * h : 128 * (h + 1)] = seen[c : c + 1]
            cot = jnp.concatenate(cots[th], axis=0).astype(BF16)
            dcol = dot(jnp.concatenate([cot, cot], axis=1), weights, 1, 1)
            dcolor = dcolor + dcol[0:3] + dcol[8:11]
            mom = dot(mono_twice, grads, 1, 1)
            m0 = mom[0:1]
            mx, my = ex * mom[1:2], ey * mom[2:3]
            total[0] = total[0] + m0
            total[1] = total[1] + dx0 * m0 + mx
            total[2] = total[2] + dy0 * m0 + my
            total[3] = total[3] + dx0 * (dx0 * m0 + 2.0 * mx) + (ex * ex) * mom[3:4]
            total[4] = total[4] + dx0 * (dy0 * m0 + my) + dy0 * mx + (ex * ey) * mom[4:5]
            total[5] = total[5] + dy0 * (dy0 * m0 + 2.0 * my) + (ey * ey) * mom[5:6]
        s0, sx, sy, sxx, sxy, syy = total
        made = [ca * sx + cb * sy, cb * sx + cc * sy, -0.5 * sxx, -sxy, -0.5 * syy, s0, dcolor]
        grad_ref[0:9, SLOTS * t : SLOTS * (t + 1)] = jnp.concatenate(made, axis=0)

    inv = inv_ref[...]

    def pick(tables, idx):
        at = jnp.maximum(idx - 1, 0)
        low, high = at & 127, at >> 7
        got = lane_gather(tables[0], low)
        for j in range(1, 8):
            got = jnp.where(high == j, lane_gather(tables[j], low), got)
        return jnp.where(idx > 0, got, 0.0)

    tables = [grad_ref[0:8, 128 * j : 128 * (j + 1)] for j in range(8)]
    last = [jnp.broadcast_to(grad_ref[8:9, 128 * j : 128 * (j + 1)], (8, 128)) for j in range(8)]
    left = lax.broadcasted_iota(I32, (4, 128), 1) < 64
    for n in range(PEERS):
        got = pick(tables, jnp.broadcast_to(inv[n : n + 1], (8, 128)))
        out_ref[5 * n : 5 * n + 4, :] = jnp.where(left, got[0:4], got[4:8])
    more = [pick(last, inv[n : n + 8]) for n in range(0, PEERS, 8)]
    left = lax.broadcasted_iota(I32, (PEERS, 128), 1) < 64
    out_ref[pl.ds(4, PEERS, stride=5), :] = jnp.where(left, jnp.concatenate(more, axis=0), names_ref[...])


def collect_kernel(back_ref, kept_ref, out_ref):
    lid = lax.broadcasted_iota(I32, (G_DEV, 256), 0).astype(jnp.int16)
    sub = lax.broadcasted_iota(I32, (8, 128), 0)
    lane = lax.broadcasted_iota(I32, (8, 128), 1)
    near, left = (lane & 63) >> 4, lane < 64
    acc = jnp.zeros((80, G_DEV), F32)
    for n in range(0, PEERS, 4):
        hot = one_hot(lid, pair_ids(back_ref, n))
        pairs = []
        for i in range(2):
            at = 5 * (n + 2 * i)
            one = jnp.concatenate([back_ref[at : at + 4, :]] * 2, axis=0)
            two = jnp.concatenate([back_ref[at + 5 : at + 9, :]] * 2, axis=0)
            other = jnp.where(left, pltpu.roll(one, 64, 1), two)
            straight = jnp.where(left, one, pltpu.roll(two, 64, 1))
            main = jnp.where(sub < 4, straight, other)
            last_one = jnp.broadcast_to(back_ref[at + 4 : at + 5, :], (8, 128))
            last_two = jnp.broadcast_to(back_ref[at + 9 : at + 10, :], (8, 128))
            last = jnp.where(left, last_one, pltpu.roll(last_two, 64, 1))
            rows = []
            for m, l in zip(split2(main), split2(last)):
                m, l = m.astype(F32), l.astype(F32)
                rows += [jnp.where(near == r, m, 0.0) for r in range(NEAR)] + [jnp.where(near == sub, l, 0.0)]
            pairs.append(jnp.concatenate(rows, axis=0).astype(BF16))
        acc = acc + dot(jnp.concatenate(pairs, axis=1), hot, 1, 1)
    rows = acc[0:40] + acc[40:80]
    tail = kept_ref[12:16, 0:128]
    for r in range(NEAR):
        part = [rows[8 * r : 8 * r + 8, 128 * j : 128 * (j + 1)] for j in range(4)]
        part += [rows[32 + r : 33 + r, 128 * j : 128 * (j + 1)] for j in range(4)] + [tail]
        part = jnp.concatenate(part, axis=0)
        for v in range(VIEWS):
            out_ref[40 * (NEAR * v + r) : 40 * (NEAR * v + r + 1), :] = part


def pull_kernel(parts_ref, wide_ref, image_in_ref, out_ref, image_ref, res_ref, all_ref):
    image_ref[...] = image_in_ref[...]
    for v in range(VIEWS):
        start = 40 * NEAR * v
        total = parts_ref[start : start + 36, :]
        for r in range(1, NEAR):
            total = total + parts_ref[start + 40 * r : start + 40 * r + 36, :]
        all_ref[40 * v : 40 * v + 36, :] = total
        all_ref[40 * v + 36 : 40 * v + 40, :] = parts_ref[start + 36 : start + 40, :]
    pos, logscale, quat, logit, sh = split_attributes(wide_ref)
    total = None
    opacity_grad = None
    for pair in range(VIEWS // 2):
        starts = (80 * pair, 80 * pair + 40)
        cot = [
            jnp.concatenate([all_ref[pl.ds(s + c, 4, stride=8), :] for s in starts], axis=0) for c in range(8)
        ]
        cot.append(jnp.concatenate([all_ref[s + 32 : s + 36, :] for s in starts], axis=0))
        cam = [
            jnp.concatenate(
                [jnp.broadcast_to(all_ref[s + 36 : s + 37, j : j + 1], (4, 128)) for s in starts], axis=0
            )
            for j in range(6)
        ]
        terms = camera_terms(cam[:3], cam[3:])
        _, pull = jax.vjp(lambda a, b, c, d: project(a, b, c, d, terms), pos, logscale, quat, sh)
        grads = jax.tree.leaves(pull(cot[:5] + cot[6:]))
        total = grads if total is None else [a + b for a, b in zip(total, grads)]
        opacity_grad = cot[5] if opacity_grad is None else opacity_grad + cot[5]
    grads = total[:10] + [opacity_grad / (1.0 + jnp.exp(logit))] + total[10:]
    for a in range(ATTR):
        res_ref[4 * a : 4 * a + 4, :] = grads[a][0:4] + grads[a][4:8]
    for j in range(4):
        out_ref[:, 128 * j : 128 * (j + 1)] = res_ref[pl.ds(j, ATTR, stride=4), :]


VMEM = pl.BlockSpec(memory_space=pltpu.VMEM)
SMEM = pl.BlockSpec(memory_space=pltpu.SMEM)
HBM = pl.BlockSpec(memory_space=pl.ANY)
MIB = 1024 * 1024


def call(kernel, outs, args, scratch=(), in_specs=None, out_specs=None, limit=24):
    return pl.pallas_call(
        kernel,
        out_shape=[jax.ShapeDtypeStruct(s, d) for s, d in outs],
        in_specs=in_specs or [VMEM] * len(args),
        out_specs=out_specs or [VMEM] * len(outs),
        scratch_shapes=list(scratch),
        compiler_params=pltpu.CompilerParams(vmem_limit_bytes=limit * MIB),
    )(*args)


def in_hbm(x):
    return pltpu.with_memory_space_constraint(x, pltpu.HBM)


def vmem(*shape, dtype=F32):
    return pltpu.VMEM(shape, dtype)


def route(first_tile, owner, local, attributes, camera, depth, cot):
    return call(
        route_kernel,
        [
            ((2 * RANKS, 128), F32), ((PEERS, 128), I32), ((8, TILES * SLOTS), I32), ((36 * PLANES, 128), F32),
            ((16, SLOTS), F32), ((PEERS, 128), F32), ((ATTR * 8, 128), F32),
        ],
        (first_tile, *[in_hbm(x) for x in (owner, local, attributes, camera, depth, cot)]),
        [
            vmem(1, TILES * SLOTS, dtype=I32), vmem(TILES, SLOTS, dtype=I32), vmem(ATTR, G_DEV), vmem(1, 6),
            vmem(TILES, SLOTS, dtype=I32), vmem(3, TILES, SLOTS), vmem(36, 128),
            vmem(36 * PLANES, 128), pltpu.SemaphoreType.DMA((7,)),
        ],
        [SMEM] + [HBM] * 6,
        [VMEM] * 3 + [HBM] + [VMEM] * 3,
    )


def serve(first_tile, asked, rows):
    return call(
        serve_kernel, [((18 * RANKS, 128), F32)], (first_tile, asked, rows), (), [SMEM] + [VMEM] * 2
    )[0]


def composite(got, place, inv, kept, names):
    big = vmem(SLOTS * 8, 128)
    return call(
        composite_kernel,
        [((3, TILES, 256), F32), ((5 * PEERS, 128), F32)],
        (got, place, inv, kept, names),
        [vmem(16, TILES * SLOTS), big, big, big, vmem(16, TILES * SLOTS)],
    )


def collect(back, kept):
    return call(collect_kernel, [((VIEWS * NEAR * 40, 128), F32)], (back, kept))[0]


def pull_back(parts, wide, image):
    return call(
        pull_kernel,
        [((ATTR, G_DEV), F32), (image.shape, F32)],
        (parts, wide, image),
        [vmem(ATTR * 4, 128), vmem(40 * VIEWS, 128)],
    )


def exchange(x, axis, groups):
    return lax.all_to_all(x, axis, split_axis=0, concat_axis=0, tiled=True, axis_index_groups=groups)


ALONG = [[8 * z + r for z in range(PLANES)] for r in range(RANKS)]
PLANE = [[8 * z + r for r in range(RANKS)] for z in range(PLANES)]
ACROSS = [[8 * z + 2 * y + c for z in range(PLANES) for c in range(2)] for y in range(NEAR)]
WITHIN = [[8 * z + 2 * y + c for y in range(NEAR)] for z in range(PLANES) for c in range(2)]
VIEWS_WITHIN = [[OWNERS * v + d for v in range(VIEWS) for d in group] for group in WITHIN]


def per_device(attributes, camera, list_owner, list_local, term_depth, image_cot):
    owner = list_owner.reshape(1, -1)
    first_tile = (lax.axis_index("dev") * TILES).astype(I32).reshape(1)
    asked, inv, place, rows, kept, names, wide = route(
        first_tile, owner, list_local[0], attributes, camera, term_depth[0], image_cot[0]
    )
    rows = exchange(rows.reshape(PLANES, 1, 4608), "dev", ALONG).reshape(PLANES * 36, 128)
    asked = lax.all_gather(asked, "dev", axis_index_groups=PLANE, tiled=True)
    sent = serve(first_tile, asked, rows)
    got = exchange(sent.reshape(RANKS, 1, 2304), "dev", PLANE).reshape(18 * RANKS, 128)
    image, grads = composite(got, place, inv, kept, names)
    back = exchange(grads.reshape(PEERS, 1, 640), "dev", ACROSS).reshape(5 * PEERS, 128)
    mine = collect(back, kept)
    parts = exchange(mine.reshape(VIEWS * NEAR, 40, 128), ("view", "dev"), VIEWS_WITHIN)
    grad, image = pull_back(parts.reshape(VIEWS * NEAR * 40, 128), wide, image)
    return image[None], grad


def solution(mesh):
    in_specs = (
        P(None, "dev"),
        P("view", None),
        P("view", "dev", None, None),
        P("view", "dev", None),
        P("view", "dev", None),
        P("view", None, "dev", None),
    )
    out_specs = (P("view", None, "dev", None), P(None, "dev"))
    return jax.shard_map(
        per_device, mesh=mesh, in_specs=in_specs, out_specs=out_specs, check_vma=False
    )
```
